32 devices in a mesh: dp: 8 (over z, x), seq: 4 (over y, core).
Axes of the slice: x: 2, y: 2, z: 4, core: 2. Of those that a mesh axis runs over, the one named last changes fastest.
Arguments:
- tokens_in: bfloat16 [10240, 1600], P(('dp', 'seq')), may hold values from -6 to 6
- doc_lengths: int32 [8, 2], P('dp'), may hold values from 40 to 1240, as said below
- norm_gains: bfloat16 [4, 1600], P(None, 'dp'), may hold values from 0.5 to 1.5
- w_qkv: bfloat16 [1600, 2240], P('dp', 'seq'), may hold values from -0.15625 to 0.15625
- w_o: bfloat16 [1600, 1600], P('dp', 'seq'), may hold values from -0.15625 to 0.15625
- w_xz: bfloat16 [1600, 6400], P('dp', 'seq'), may hold values from -0.15625 to 0.15625
- w_bcdt: bfloat16 [1600, 82], P('dp'), may hold values from -0.15625 to 0.15625
- conv_w: bfloat16 [4, 3200], P(None, 'dp'), may hold values from -3 to 3
- ssm_rate: float32 [50], replicated, may hold values from 0.0001 to 0.05
- ssm_skip: float32 [50], replicated, may hold values from 0.5 to 1.5
- w_out: bfloat16 [3200, 1600], P('dp', 'seq'), may hold values from -0.109375 to 0.109375
- w_gate_up: bfloat16 [1600, 2, 5504], P('dp', None, 'seq'), may hold values from -0.15625 to 0.15625
- w_down: bfloat16 [1600, 5504], P('dp', 'seq'), may hold values from -0.078125 to 0.078125
- cotangent: bfloat16 [10240, 1600], P(('dp', 'seq')), may hold values from -6 to 6
Outputs:
- mixed_out: bfloat16 [10240, 1600], P(('dp', 'seq'))
- input_grad: bfloat16 [10240, 1600], P(('dp', 'seq'))
- grad_gains: float32 [4, 1600], P(None, 'dp')
- grad_qkv: float32 [1600, 2240], P('dp', 'seq')
- grad_o: float32 [1600, 1600], P('dp', 'seq')
- grad_xz: float32 [1600, 6400], P('dp', 'seq')
- grad_bcdt: float32 [1600, 82], P('dp')
- grad_conv: float32 [4, 3200], P(None, 'dp')
- grad_rate: float32 [50], replicated
- grad_skip: float32 [50], replicated
- grad_out: float32 [3200, 1600], P('dp', 'seq')
- grad_gate_up: float32 [1600, 2, 5504], P('dp', None, 'seq')
- grad_down: float32 [1600, 5504], P('dp', 'seq')
The draws below stay inside these ranges and needn't reach their ends.
Inputs may be any that keep to these rules, and one draw needn't show every extreme that they name: `doc_lengths`: each row holds a group's two document lengths in the order in which they are packed from the group's first slot. One has 40 to 80 tokens; the other fills the group but for fewer than 40 padding slots at its end, so that it starts in the block of the group's first device and ends in the block of its last. Some group reaches both ends of the range.
All inputs are finite; a program needn't handle non-finite values.
Results may differ from the reference program's by a relative error of at most 0.02.
Values may be sent and summed in bfloat16 or wider, within the bound.
A program may use at most 576 MiB of HBM per device.

```python
import math
import jax
import jax.numpy as jnp
from jax import lax

D = 1600
HEADS = 25
KV_HEADS = 5
HEAD = 64
INNER = 3200
SSM_HEAD = 64
STATE = 16
CONV = 4
FF = 5504
WINDOW = 1024
TOK_DEV = 320
SSM_HEADS = 50
GROUP_TOK = 1280
GROUPS = 8
TOKENS = 10240


def draw_doc_lengths(key, part):
    key = jax.random.fold_in(key, 11)
    short_key, pad_key, order_key = jax.random.split(key, 3)
    least_short = TOK_DEV // 8
    short_len = jax.random.randint(short_key, (GROUPS,), least_short, TOK_DEV // 4 + 1)
    pad_len = jax.random.randint(pad_key, (GROUPS,), 0, max(1, TOK_DEV // 8))
    short_len = short_len.at[0].set(least_short)
    pad_len = pad_len.at[0].set(0)
    long_len = GROUP_TOK - short_len - pad_len
    order_bit = jax.random.randint(order_key, (GROUPS,), 0, 2)
    first_len = jnp.where(order_bit == 1, long_len, short_len)
    second_len = jnp.where(order_bit == 1, short_len, long_len)
    return jnp.stack([first_len, second_len], axis=1).astype(jnp.int32)


def steps_of(own_key, shape, cuts, least, high):
    def one(position, shards_of):
        steps = jax.random.uniform(jax.random.fold_in(jax.random.fold_in(own_key, 6), position), (shards_of,), jnp.float32, least / len(cuts), high / len(cuts))
        return jnp.repeat(jnp.exp(steps), shape[position] // shards_of).reshape((-1,) + (1,) * (len(shape) - position - 1))

    factor_of = one(*cuts[0])
    for cut in cuts[1:]:
        factor_of = factor_of * one(*cut)
    return factor_of


def bell_draw(key, extent, spread, bound, shards=(), kind=jnp.bfloat16):
    result = spread * jax.random.normal(key, extent, jnp.float32)
    if shards:
        result = result * steps_of(key, extent, shards, -0.22, 0.18)
    return jnp.clip(result, -bound, bound).astype(kind)


def setup_inputs(seed: int = 0) -> dict:
    arg_keys = jax.random.split(jax.random.key(seed), 15)
    tokens_in = bell_draw(arg_keys[0], (TOKENS, D), 1.0, 6.0, ((0, 32),))
    doc_lengths = draw_doc_lengths(jax.random.fold_in(arg_keys[14], 71), 0)
    norm_gains = jnp.clip(1.0 + 0.1 * jax.random.normal(arg_keys[2], (4, D), jnp.float32), 0.5, 1.5).astype(jnp.bfloat16)
    w_qkv = bell_draw(arg_keys[3], (D, D + 2 * KV_HEADS * HEAD), D ** -0.5, 0.15625, ((0, 8), (1, 4)))
    w_o = bell_draw(arg_keys[4], (D, D), D ** -0.5, 0.15625, ((0, 8), (1, 4)))
    w_xz = bell_draw(arg_keys[5], (D, 2 * INNER), D ** -0.5, 0.15625, ((0, 8), (1, 4)))
    w_bcdt = bell_draw(arg_keys[6], (D, 2 * STATE + SSM_HEADS), D ** -0.5, 0.15625, ((0, 8),))
    conv_w = bell_draw(arg_keys[7], (CONV, INNER), CONV ** -0.5, 3.0, ((1, 8),))
    ssm_rate = jnp.clip(jnp.exp(jax.random.uniform(arg_keys[8], (SSM_HEADS,), jnp.float32, math.log(0.0001), math.log(0.05))), 0.0001, 0.05)
    ssm_skip = jnp.clip(jax.random.uniform(arg_keys[9], (SSM_HEADS,), jnp.float32, 0.5, 1.5), 0.5, 1.5)
    w_out = bell_draw(arg_keys[10], (INNER, D), INNER ** -0.5, 0.109375, ((0, 8), (1, 4)))
    w_gate_up = bell_draw(arg_keys[11], (D, 2, FF), D ** -0.5, 0.15625, ((0, 8), (2, 4)))
    w_down = bell_draw(arg_keys[12], (D, FF), FF ** -0.5, 0.078125, ((0, 8), (1, 4)))
    cotangent = bell_draw(arg_keys[13], (TOKENS, D), 1.0, 6.0, ((0, 32),))
    return {"tokens_in": tokens_in, "doc_lengths": doc_lengths, "norm_gains": norm_gains, "w_qkv": w_qkv, "w_o": w_o, "w_xz": w_xz, "w_bcdt": w_bcdt, "conv_w": conv_w, "ssm_rate": ssm_rate, "ssm_skip": ssm_skip, "w_out": w_out, "w_gate_up": w_gate_up, "w_down": w_down, "cotangent": cotangent}


@jax.custom_vjp
def low(v):
    return lax.optimization_barrier(v.astype(jnp.bfloat16)).astype(jnp.float32)

@jax.custom_vjp
def low_back(v):
    return v

def low_keep(v):
    return (low(v), None)

def low_pass(kept, grad):
    return (grad,)

def back_keep(v):
    return (v, None)

def back_low(kept, grad):
    return (low(grad),)
low.defvjp(low_keep, low_pass)
low_back.defvjp(back_keep, back_low)
NORM_EPS = 1e-05
MASKED = -1e+30

def matmul(left, right):
    return jnp.dot(left, right, precision=lax.Precision.HIGHEST)

def rms_norm(values, gain):
    return values * lax.rsqrt(lax.optimization_barrier(jnp.mean(values * values, axis=-1, keepdims=True)) + NORM_EPS) * gain

def document_ids(lengths, positions):
    first_end = lengths[0]
    second_end = lengths[0] + lengths[1]
    doc_ids = (positions >= first_end).astype(jnp.int32) + (positions >= second_end).astype(jnp.int32)
    return (jnp.where(positions < 0, -1, doc_ids).astype(jnp.int32), positions < second_end)

def attention(queries, key_rows, value_rows, doc_ids):
    row_total = queries.shape[0]
    group_heads = HEADS // KV_HEADS
    scale = HEAD ** (-0.5)
    positions = jnp.arange(row_total, dtype=jnp.int32)
    key_heads = key_rows.reshape(row_total, KV_HEADS, HEAD)
    value_heads = value_rows.reshape(row_total, KV_HEADS, HEAD)

    def attend_block(row_start):
        query_block = lax.dynamic_slice_in_dim(queries, row_start, TOK_DEV, 0).reshape(TOK_DEV, KV_HEADS, group_heads, HEAD)
        query_pos = row_start + jnp.arange(TOK_DEV, dtype=jnp.int32)
        query_ids = lax.dynamic_slice_in_dim(doc_ids, row_start, TOK_DEV, 0)
        distance = query_pos[:, None] - positions[None, :]
        allowed = (distance >= 0) & (distance < WINDOW) & (query_ids[:, None] == doc_ids[None, :])
        scores = low_back(scale * jnp.einsum('tkgd,skd->kgts', query_block, key_heads, precision=lax.Precision.HIGHEST))
        scores = jnp.where(allowed[None, None], scores, MASKED)
        weights = low(jax.nn.softmax(scores, axis=-1))
        mixed = jnp.einsum('kgts,skd->tkgd', weights, value_heads, precision=lax.Precision.HIGHEST)
        return mixed.reshape(TOK_DEV, HEADS * HEAD)
    starts = jnp.arange(row_total // TOK_DEV, dtype=jnp.int32) * TOK_DEV
    blocks = lax.map(jax.checkpoint(attend_block), starts)
    return blocks.reshape(row_total, HEADS * HEAD)

def convolve(raw_x, conv_weight, doc_ids):
    row_total = raw_x.shape[0]
    padded = jnp.concatenate([jnp.zeros((CONV - 1, raw_x.shape[1]), jnp.float32), raw_x], axis=0)
    padded_ids = jnp.concatenate([jnp.full((CONV - 1,), -1, jnp.int32), doc_ids])
    conv_sum = jnp.zeros_like(raw_x)
    for tap_index in range(CONV):
        same_doc = (padded_ids[tap_index:tap_index + row_total] == doc_ids).astype(jnp.float32)
        conv_sum = conv_sum + conv_weight[tap_index] * padded[tap_index:tap_index + row_total] * same_doc[:, None]
    return jax.nn.silu(conv_sum)

def mixer_state(conv_act, b_in, c_in, step_size, ssm_rate, ssm_skip, doc_ids):
    row_total = conv_act.shape[0]
    heads_x = conv_act.reshape(row_total, SSM_HEADS, SSM_HEAD)
    same_prev = jnp.concatenate([jnp.zeros((1,), jnp.int32), (doc_ids[1:] == doc_ids[:-1]).astype(jnp.int32)])
    token_decay = jnp.exp(-step_size * ssm_rate[None, :]) * same_prev.astype(jnp.float32)[:, None]

    def token_step(ssm_state, inputs):
        decay_now, step_now, b_now, c_now, x_now = inputs
        ssm_state = decay_now[:, None, None] * ssm_state + step_now[:, None, None] * b_now[None, :, None] * x_now[:, None, :]
        readout = jnp.einsum('n,hnd->hd', c_now, ssm_state, precision=lax.Precision.HIGHEST)
        return (ssm_state, readout)

    def block_step(ssm_state, inputs):
        return lax.scan(token_step, ssm_state, inputs)
    blocks = row_total // TOK_DEV
    stacked = tuple((member.reshape((blocks, TOK_DEV) + member.shape[1:]) for member in (token_decay, step_size, b_in, c_in, heads_x)))
    start_state = jnp.zeros((SSM_HEADS, STATE, SSM_HEAD), jnp.float32)
    final_state, readouts = lax.scan(jax.checkpoint(block_step), start_state, stacked)
    readouts = readouts.reshape(row_total, SSM_HEADS, SSM_HEAD) + ssm_skip[None, :, None] * heads_x
    return readouts.reshape(row_total, INNER)

def layer(inputs_x, lengths, norm_gains, w_qkv, w_o, w_xz, w_bcdt, conv_w, ssm_rate, ssm_skip, w_out, w_gate_up, w_down):
    row_total = inputs_x.shape[0]
    kv_width = KV_HEADS * HEAD
    doc_ids, live_mask = document_ids(lengths, jnp.arange(row_total, dtype=jnp.int32))
    normed = low(rms_norm(inputs_x, norm_gains[0]))
    qkv_proj = low(low_back(matmul(normed, w_qkv)))
    attended = low(low_back(attention(qkv_proj[:, :D], qkv_proj[:, D:D + kv_width], qkv_proj[:, D + kv_width:], doc_ids)))
    attn_o = low_back(matmul(attended, w_o))
    xz_proj = low_back(matmul(normed, w_xz))
    raw_x = low(xz_proj[:, :INNER])
    gate_z = xz_proj[:, INNER:]
    bcdt_proj = low_back(matmul(normed, w_bcdt))
    step_size = jax.nn.softplus(bcdt_proj[:, 2 * STATE:])
    conv_act = convolve(raw_x, conv_w, doc_ids)
    ssm_read = mixer_state(conv_act, bcdt_proj[:, :STATE], bcdt_proj[:, STATE:2 * STATE], step_size, ssm_rate, ssm_skip, doc_ids)
    gated = low(ssm_read * jax.nn.silu(gate_z))
    ssm_o = low_back(matmul(gated, w_out))
    residual = inputs_x + 0.5 * (rms_norm(attn_o, norm_gains[1]) + rms_norm(ssm_o, norm_gains[2]))
    normed_two = low(rms_norm(residual, norm_gains[3]))
    ffn_gate = low_back(matmul(normed_two, w_gate_up[:, 0, :]))
    ffn_up = low_back(matmul(normed_two, w_gate_up[:, 1, :]))
    ffn_act = low(jax.nn.silu(ffn_gate) * ffn_up)
    ffn_out = low_back(matmul(ffn_act, jnp.transpose(w_down)))
    return (residual + ffn_out) * live_mask.astype(jnp.float32)[:, None]

def reference(tokens_in, doc_lengths, norm_gains, w_qkv, w_o, w_xz, w_bcdt, conv_w, ssm_rate, ssm_skip, w_out, w_gate_up, w_down, cotangent):
    weights = (norm_gains.astype(jnp.float32), w_qkv.astype(jnp.float32), w_o.astype(jnp.float32), w_xz.astype(jnp.float32), w_bcdt.astype(jnp.float32), conv_w.astype(jnp.float32), ssm_rate.astype(jnp.float32), ssm_skip.astype(jnp.float32), w_out.astype(jnp.float32), w_gate_up.astype(jnp.float32), w_down.astype(jnp.float32))
    token_groups = tokens_in.astype(jnp.float32).reshape(GROUPS, GROUP_TOK, D)
    cot_groups = cotangent.astype(jnp.float32).reshape(GROUPS, GROUP_TOK, D)

    def one_group(totals, inputs):
        group_x, group_lengths, group_cot = inputs

        def group_layer(layer_x, *layer_weights):
            return layer(layer_x, group_lengths, *layer_weights)
        group_out, pull_back = jax.vjp(group_layer, group_x, *weights)
        grads = pull_back(group_cot)
        totals = tuple((total_now + grad_now for total_now, grad_now in zip(totals, grads[1:])))
        return (totals, (group_out, grads[0]))
    start_totals = tuple((jnp.zeros_like(weight_now) for weight_now in weights))
    totals, (group_outs, group_grads) = lax.scan(one_group, start_totals, (token_groups, doc_lengths, cot_groups))
    mixed_out = group_outs.reshape(TOKENS, D).astype(jnp.bfloat16)
    input_grad = group_grads.reshape(TOKENS, D).astype(jnp.bfloat16)
    return (mixed_out, input_grad, totals[0], totals[1], totals[2], totals[3], totals[4], totals[5], totals[6], totals[7], totals[8], totals[9], totals[10])
```

```python
import jax
import jax.numpy as jnp
from jax import lax
from jax.sharding import PartitionSpec as P

D = 1600
HEADS = 25
KV_HEADS = 5
HEAD = 64
INNER = 3200
SSM_HEAD = 64
STATE = 16
CONV = 4
FF = 5504
WINDOW = 1024
SSM_HEADS = 50

NORM_EPS = 1e-05
MASKED = -1e30
LOW = jnp.bfloat16
FULL = jnp.float32

SEQ = 4
GROUP_HEADS = HEADS // KV_HEADS
QW = GROUP_HEADS * HEAD
LOCAL_HEADS = 13
LOCAL_CH = LOCAL_HEADS * SSM_HEAD
CHUNK = 128
UNITS = FF // SEQ
UNITS_PAD = 1408
BCDT_PAD = 128
OUT_AT, O_AT, O5_AT, OUT_WIDTH = 0, 896, 1280, 1600
FIRST_HEAD = tuple((SSM_HEADS * s // 2 + 1) // 2 for s in range(SEQ))
HEAD_COUNT = tuple(b - a for a, b in zip(FIRST_HEAD, FIRST_HEAD[1:] + (SSM_HEADS,)))


def swap(value, axis, bit):
    return lax.ppermute(value, axis, [(i, i ^ bit) for i in range(lax.axis_size(axis))])


def hop(value, step, senders):
    return lax.ppermute(
        value, "dp", [(2 * z + x, 2 * (z + step) + x) for z in senders for x in (0, 1)]
    )


def place(blocks):
    stacked = jnp.zeros((len(blocks),) + blocks[0][1].shape, blocks[0][1].dtype)
    for index, block in blocks:
        stacked = lax.dynamic_update_index_in_dim(stacked, block, index, 0)
    return stacked


def gather_seq(block):
    me = lax.axis_index("seq")
    far = swap(block, "seq", 2)
    near = swap(block, "seq", 1)
    near_far = swap(far, "seq", 1)
    return place([(me, block), (me ^ 1, near), (me ^ 2, far), (me ^ 3, near_far)])


def scatter_seq(rows, out_dtype):
    me = lax.axis_index("seq")
    core, far = me % 2, me // 2
    by_core = rows.reshape((2, 2) + rows.shape[1:])
    give = lax.dynamic_index_in_dim(by_core, 1 - core, 1, False)
    keep = lax.dynamic_index_in_dim(by_core, core, 1, False)
    got = swap(give, "seq", 1)
    give_far = (
        lax.dynamic_index_in_dim(keep, 1 - far, 0, False).astype(FULL)
        + lax.dynamic_index_in_dim(got, 1 - far, 0, False).astype(FULL)
    ).astype(LOW)
    got_far = swap(give_far, "seq", 2)
    return (
        lax.dynamic_index_in_dim(keep, far, 0, False).astype(FULL)
        + lax.dynamic_index_in_dim(got, far, 0, False).astype(FULL)
        + got_far.astype(FULL)
    ).astype(out_dtype)


def gather_dp(block):
    count = lax.axis_size("dp")
    if count != 8:
        return lax.all_gather(block, "dp", axis=0)
    line = count // 2
    me = lax.axis_index("dp")
    z, x = me // 2, me % 2
    up, down = [block], [block]
    for k in range(1, line):
        up.append(hop(up[-1], 1, range(k - 1, line - 1)))
        down.append(hop(down[-1], -1, range(1, line - k + 1)))
    placed = []
    for j in range(line):
        held = block if j == 0 else jnp.where(z + j < line, down[j], up[line - j])
        other = swap(held, "dp", 1)
        at = 2 * lax.rem(z + j, line)
        placed += [(at + x, held), (at + 1 - x, other)]
    return place(placed)


def scatter_dp(parts):
    count = lax.axis_size("dp")
    parts = parts.astype(LOW)
    if count != 8:
        summed = lax.psum_scatter(parts, "dp", scatter_dimension=0)
        return lax.optimization_barrier(summed).astype(FULL)
    line = count // 2
    me = lax.axis_index("dp")
    z, x = me // 2, me % 2
    grid = parts.reshape((line, 2) + parts.shape[1:])
    got = swap(lax.dynamic_index_in_dim(grid, 1 - x, 1, False), "dp", 1)
    part = lax.dynamic_index_in_dim(grid, x, 1, False).astype(FULL) + got.astype(FULL)
    part = part.astype(LOW)

    def own(t):
        return lax.dynamic_index_in_dim(part, jnp.clip(t, 0, line - 1), 0, False).astype(FULL)

    up = down = None
    for k in range(1, line):
        send_up, send_down = own(line - k + z), own(z - (line - k))
        if k > 1:
            send_up, send_down = send_up + up.astype(FULL), send_down + down.astype(FULL)
        up = hop(send_up.astype(LOW), 1, range(0, k))
        down = hop(send_down.astype(LOW), -1, range(line - k, line))
    return own(z) + up.astype(FULL) + down.astype(FULL)


def sum_all(value):
    for axis in ("seq", "dp"):
        bit = 1
        while bit < lax.axis_size(axis):
            value = value + swap(value, axis, bit)
            bit *= 2
    return value


def mm(left, right):
    return jnp.dot(left, right, preferred_element_type=FULL)


def mm_nt(left, right):
    return lax.dot_general(left, right, (((1,), (1,)), ((), ())), preferred_element_type=FULL)


def mm_tn(left, right):
    return lax.dot_general(left, right, (((0,), (0,)), ((), ())), preferred_element_type=FULL)


def rms_norm(values, gain):
    return values * lax.rsqrt(jnp.mean(values * values, axis=-1, keepdims=True) + NORM_EPS) * gain


def join_tail(inputs_x, attn_o, ssm_o, gains):
    residual = inputs_x + 0.5 * (rms_norm(attn_o, gains[1]) + rms_norm(ssm_o, gains[2]))
    return (residual, rms_norm(residual, gains[3]))


def document_ids(lengths, positions):
    first_end = lengths[0]
    second_end = lengths[0] + lengths[1]
    return (positions >= first_end).astype(jnp.int32) + (positions >= second_end).astype(jnp.int32)


def convolve(raw_x, conv_weight, doc_ids):
    row_count = raw_x.shape[0]
    padded = jnp.pad(raw_x, ((CONV - 1, 0), (0, 0)))
    padded_ids = jnp.pad(doc_ids, (CONV - 1, 0), constant_values=-1)
    conv_sum = jnp.zeros(raw_x.shape, FULL)
    for tap in range(CONV):
        same = (padded_ids[tap : tap + row_count] == doc_ids).astype(FULL)
        conv_sum = conv_sum + conv_weight[tap] * padded[tap : tap + row_count] * same[:, None]
    return jax.nn.silu(conv_sum)


def allowed_block(row_ids, row_pos, key_ids, key_pos):
    distance = row_pos[:, None] - key_pos[None, :]
    return (distance >= 0) & (distance < WINDOW) & (row_ids[:, None] == key_ids[None, :])


def head_forward(q, k, v, allowed):
    scale = HEAD ** (-0.5)
    scores = scale * jnp.einsum("gtd,sd->gts", q, k, preferred_element_type=FULL)
    scores = jnp.where(allowed[None], scores, MASKED)
    top = jnp.max(scores, axis=-1, keepdims=True)
    expos = jnp.exp(scores - top)
    denom = jnp.sum(expos, axis=-1, keepdims=True)
    weights = (expos / denom).astype(LOW)
    mixed = jnp.einsum("gts,sd->gtd", weights, v, preferred_element_type=FULL)
    return mixed, top + jnp.log(denom)


def head_backward(q, k, v, allowed, log_total, d_mixed):
    scale = HEAD ** (-0.5)
    scores = scale * jnp.einsum("gtd,sd->gts", q, k, preferred_element_type=FULL)
    probs = jnp.where(allowed[None], jnp.exp(scores - log_total), 0.0)
    d_v = jnp.einsum("gts,gtd->sd", probs.astype(LOW), d_mixed, preferred_element_type=FULL)
    d_probs = jnp.einsum("gtd,sd->gts", d_mixed, v, preferred_element_type=FULL)
    d_scores = probs * (d_probs - jnp.sum(probs * d_probs, axis=-1, keepdims=True))
    d_low = d_scores.astype(LOW)
    d_q = scale * jnp.einsum("gts,sd->gtd", d_low, k, preferred_element_type=FULL)
    d_k = scale * jnp.einsum("gts,gtd->sd", d_low, q, preferred_element_type=FULL)
    return d_q, d_k, d_v


def to_heads(block):
    return block.reshape(block.shape[0], GROUP_HEADS, HEAD).transpose(1, 0, 2)


def from_heads(block):
    return block.transpose(1, 0, 2).reshape(block.shape[1], QW)


def attention_steps(rows, seq_index, doc_ids):
    positions = jnp.arange(doc_ids.shape[0], dtype=jnp.int32)
    steps = []
    for t in range(SEQ + 1):
        last = t == SEQ
        extent = (SEQ if last else t + 1) * rows
        at = seq_index * rows if last else t * rows
        allowed = allowed_block(
            lax.dynamic_slice_in_dim(doc_ids, at, rows),
            lax.dynamic_slice_in_dim(positions, at, rows),
            doc_ids[:extent],
            positions[:extent],
        )
        steps.append((t, 1 if last else 0, extent, allowed))
    return steps


def attention_forward(queries, kv, steps, rows):
    out, logs = [], []
    for t, which, extent, allowed in steps:
        k = kv[:extent, which * 128 : which * 128 + 64]
        v = kv[:extent, which * 128 + 64 : which * 128 + 128]
        mixed, log_total = head_forward(to_heads(queries[t * rows : (t + 1) * rows]), k, v, allowed)
        out.append(from_heads(mixed).astype(LOW))
        logs.append(log_total)
    return jnp.concatenate(out), logs


def attention_backward(queries, kv, logs, d_out, steps, rows):
    d_q = []
    d_k = [jnp.zeros((kv.shape[0], HEAD), FULL) for _ in range(2)]
    d_v = [jnp.zeros((kv.shape[0], HEAD), FULL) for _ in range(2)]
    for (t, which, extent, allowed), log_total in zip(steps, logs):
        k = kv[:extent, which * 128 : which * 128 + 64]
        v = kv[:extent, which * 128 + 64 : which * 128 + 128]
        part = slice(t * rows, (t + 1) * rows)
        q_one, k_one, v_one = head_backward(
            to_heads(queries[part]), k, v, allowed, log_total, to_heads(d_out[part])
        )
        d_q.append(from_heads(q_one))
        d_k[which] = d_k[which].at[:extent].add(k_one)
        d_v[which] = d_v[which].at[:extent].add(v_one)
    d_kv = jnp.concatenate([d_k[0], d_v[0], d_k[1], d_v[1]], axis=1)
    return jnp.concatenate(d_q).astype(LOW), d_kv.astype(LOW)


def ssm_group(conv_act, bcdt, rate, skip, gate_z, doc_ids):
    total = conv_act.shape[0]
    chunks = total // CHUNK
    heads = rate.shape[0]
    low = lambda v: v.astype(LOW)
    ein = lambda spec, *v: jnp.einsum(spec, *v, preferred_element_type=FULL)
    ids = doc_ids.reshape(chunks, CHUNK)
    ids_prev = jnp.concatenate([jnp.full((1,), -1, jnp.int32), ids[:-1, -1]])
    step = jax.nn.softplus(bcdt[:, 2 * STATE : 2 * STATE + heads]).reshape(chunks, CHUNK, heads)
    b_in = bcdt[:, :STATE].reshape(chunks, CHUNK, STATE)
    c_in = bcdt[:, STATE : 2 * STATE].reshape(chunks, CHUNK, STATE)
    x = conv_act.reshape(chunks, CHUNK, heads, SSM_HEAD)
    log = jnp.cumsum(-step * rate, axis=1)
    places = jnp.arange(CHUNK, dtype=jnp.int32)
    causal = (places[:, None] >= places[None, :])[None] & (ids[:, :, None] == ids[:, None, :])
    log_h = log.transpose(0, 2, 1)
    gap = log_h[:, :, :, None] - log_h[:, :, None, :]
    decays = jnp.where(causal[:, None], jnp.exp(jnp.where(causal[:, None], gap, 0.0)), 0.0)
    gram = ein("ctn,csn->cts", low(c_in), low(b_in))
    mixing = decays * gram[:, None]
    step_x = low(x * step[..., None])
    within = ein("chts,cshd->cthd", low(mixing), step_x)
    last = log[:, -1]
    ends = jnp.exp(last[:, None] - log) * (ids == ids[:, -1:]).astype(FULL)[..., None]
    state_end = ein("cshd,csn->chnd", low(x * (step * ends)[..., None]), low(b_in))
    carry = jnp.exp(last) * (ids[:, -1] == ids_prev).astype(FULL)[:, None]
    state = jnp.zeros(state_end.shape[1:], FULL)
    states = []
    for c in range(chunks):
        states.append(state)
        state = carry[c][:, None, None] * state + state_end[c]
    states = jnp.stack(states)
    reach = jnp.exp(log) * (ids == ids_prev[:, None]).astype(FULL)[..., None]
    from_state = ein("ctn,chnd->cthd", low(c_in), low(states)) * reach[..., None]
    read = within + from_state + skip[:, None] * x
    return read.reshape(total, heads * SSM_HEAD) * jax.nn.silu(gate_z)


def pick(options, seq_index):
    return lax.select_n(seq_index, *options)


def own_cut(values, seq_index, axis, unit):
    cuts = []
    for first, count in zip(FIRST_HEAD, HEAD_COUNT):
        cut = lax.slice_in_dim(values, first * unit, (first + count) * unit, axis=axis)
        pads = [(0, 0)] * values.ndim
        pads[axis] = (0, (LOCAL_HEADS - count) * unit)
        cuts.append(jnp.pad(cut, pads))
    return pick(cuts, seq_index)


def own_spread(values, seq_index, unit):
    spreads = []
    for first, count in zip(FIRST_HEAD, HEAD_COUNT):
        pads = [(0, 0)] * (values.ndim - 1) + [(first * unit, (SSM_HEADS - first - count) * unit)]
        spreads.append(jnp.pad(values[..., : count * unit], pads))
    return pick(spreads, seq_index)


def channel_cut(wide, seq_index, axis):
    return own_cut(wide, seq_index, axis, SSM_HEAD)


def bcdt_cut(w_bcdt, seq_index):
    first = pick([jnp.int32(h) for h in FIRST_HEAD], seq_index)
    count = pick([jnp.int32(c) for c in HEAD_COUNT], seq_index)
    source = jnp.arange(w_bcdt.shape[1], dtype=jnp.int32)[:, None]
    target = jnp.arange(BCDT_PAD, dtype=jnp.int32)[None]
    shared = (target < 2 * STATE) & (source == target)
    steps = (target >= 2 * STATE) & (target < 2 * STATE + count) & (source == target + first)
    return mm(w_bcdt, (shared | steps).astype(LOW)).astype(LOW)


def wide_of(gathered):
    return gathered.transpose(1, 0, 2).reshape(gathered.shape[1], -1)


def on_device(
    tokens_in,
    doc_lengths,
    norm_gains,
    w_qkv,
    w_o,
    w_xz,
    w_bcdt,
    conv_w,
    ssm_rate,
    ssm_skip,
    w_out,
    w_gate_up,
    w_down,
    cotangent,
):
    rows = tokens_in.shape[0]
    group = rows * SEQ
    s = lax.axis_index("seq")
    dp_index = lax.axis_index("dp")
    dp_total = lax.axis_size("dp")
    block_rows = w_qkv.shape[0]
    kv_width = KV_HEADS * HEAD
    lengths = doc_lengths[0]
    doc_ids = document_ids(lengths, jnp.arange(group, dtype=jnp.int32))
    live = (jnp.arange(rows, dtype=jnp.int32) + s * rows < lengths[0] + lengths[1]).astype(FULL)[:, None]

    gains_block = norm_gains.shape[1]
    conv_block = conv_w.shape[1]
    width = -(-max(conv_block, gains_block) // 128) * 128
    small = jnp.concatenate(
        [
            jnp.pad(conv_w, ((0, 4), (0, width - conv_block))),
            jnp.pad(norm_gains, ((0, 4), (0, width - gains_block))),
        ]
    )
    small = gather_dp(small)
    full_conv = small[:, :4, :conv_block].transpose(1, 0, 2).reshape(4, INNER).astype(FULL)
    gains = small[:, 8:12, :gains_block].transpose(1, 0, 2).reshape(4, D).astype(FULL)

    tokens_group = gather_seq(tokens_in).reshape(group, D)
    qkv_wide = wide_of(gather_seq(w_qkv))
    q_at = lambda h: lax.dynamic_slice_in_dim(qkv_wide, h * QW, QW, 1)
    kv_at = lambda h: [
        lax.dynamic_slice_in_dim(qkv_wide, D + h * HEAD, HEAD, 1),
        lax.dynamic_slice_in_dim(qkv_wide, D + kv_width + h * HEAD, HEAD, 1),
    ]
    qkv_packet = jnp.concatenate(kv_at(s) + kv_at(KV_HEADS - 1) + [q_at(s), q_at(KV_HEADS - 1)], axis=1)
    full_qkv = gather_dp(qkv_packet).reshape(D, -1)

    xz_wide = wide_of(gather_seq(w_xz))
    bcdt_own = bcdt_cut(w_bcdt, s)
    xz_packet = jnp.concatenate(
        [
            channel_cut(xz_wide[:, :INNER], s, 1),
            channel_cut(xz_wide[:, INNER:], s, 1),
            bcdt_own,
        ],
        axis=1,
    )
    full_xz = gather_dp(xz_packet).reshape(D, -1)

    out_block = w_out.shape[0]
    out_cols = gather_dp(jnp.concatenate([w_o, w_out], axis=0))
    o_cols = out_cols[:, :block_rows].reshape(D, -1)
    mamba_cols = out_cols[:, block_rows:].reshape(INNER, -1)

    def rows_for(peer):
        return jnp.concatenate(
            [
                jnp.pad(channel_cut(mamba_cols, peer, 0).T, ((0, 0), (0, O_AT - LOCAL_CH))),
                jnp.pad(
                    lax.dynamic_slice_in_dim(o_cols, peer * QW, QW, 0).T, ((0, 0), (0, O5_AT - O_AT - QW))
                ),
                o_cols[(KV_HEADS - 1) * QW :].T,
            ],
            axis=1,
        )

    out_t = place(
        [(s, rows_for(s))] + [(s ^ bit, swap(rows_for(s ^ bit), "seq", bit)) for bit in (1, 2, 3)]
    ).reshape(D, OUT_WIDTH)
    w_out_t = out_t[:, :LOCAL_CH]
    w_o_t = out_t[:, O_AT : O_AT + QW]
    w_o5_t = out_t[:, O5_AT:]

    gate_up_packet = jnp.pad(w_gate_up, ((0, 0), (0, 0), (0, UNITS_PAD - UNITS))).reshape(block_rows, -1)
    full_gate_up = gather_dp(gate_up_packet).reshape(D, -1)
    full_down = gather_dp(jnp.pad(w_down, ((0, 0), (0, UNITS_PAD - UNITS)))).reshape(D, -1)

    d_total = cotangent.astype(FULL) * live
    d_ffn_group = gather_seq(d_total.astype(LOW)).reshape(group, D)

    own = lambda a: lax.dynamic_slice_in_dim(a, s * rows, rows, 0)
    normed = rms_norm(tokens_group.astype(FULL), gains[0]).astype(LOW)
    normed_own = own(normed)
    kvq = mm(normed, full_qkv[:, : 256 + QW]).astype(LOW)
    q_last = mm(normed_own, full_qkv[:, 256 + QW :]).astype(LOW)
    queries = jnp.concatenate([kvq[:, 256:], q_last])
    kv = kvq[:, :256]
    steps = attention_steps(rows, s, doc_ids)
    attended, logs = attention_forward(queries, kv, steps, rows)
    attn_part = mm_nt(attended[:group], w_o_t).astype(LOW)
    attn_o = scatter_seq(attn_part.reshape(SEQ, rows, D), FULL) + mm_nt(attended[group:], w_o5_t)

    xzb = mm(normed, full_xz)
    raw_x = xzb[:, :LOCAL_CH].astype(LOW)
    gate_z = xzb[:, LOCAL_CH : 2 * LOCAL_CH]
    bcdt = xzb[:, 2 * LOCAL_CH :]
    conv_own = channel_cut(full_conv, s, 1)
    rate = own_cut(ssm_rate, s, 0, 1)
    skip = own_cut(ssm_skip, s, 0, 1)
    conv_act, pull_conv = jax.vjp(
        lambda a, w: convolve(a, w, doc_ids), raw_x.astype(FULL), conv_own
    )
    gated, pull_ssm = jax.vjp(
        lambda *v: ssm_group(*v, doc_ids), conv_act, bcdt, rate, skip, gate_z
    )
    gated = gated.astype(LOW)
    ssm_part = mm_nt(gated, w_out_t).astype(LOW)
    ssm_o = scatter_seq(ssm_part.reshape(SEQ, rows, D), FULL)

    inputs_x = tokens_in.astype(FULL)
    (residual, normed_two), pull_join = jax.vjp(join_tail, inputs_x, attn_o, ssm_o, gains)
    normed_two = gather_seq(normed_two.astype(LOW)).reshape(group, D)
    gate_up = mm(normed_two, full_gate_up)
    ffn_gate, ffn_up = gate_up[:, :UNITS_PAD], gate_up[:, UNITS_PAD:]
    ffn_act = (jax.nn.silu(ffn_gate) * ffn_up).astype(LOW)
    ffn_part = mm_nt(ffn_act, full_down).astype(LOW)
    ffn_own = scatter_seq(ffn_part.reshape(SEQ, rows, D), FULL)
    mixed_out = ((residual + ffn_own) * live).astype(LOW)

    d_act = mm(d_ffn_group, full_down)
    sig = jax.nn.sigmoid(ffn_gate)
    d_gate = d_act * ffn_up * (sig * (1.0 + ffn_gate * (1.0 - sig)))
    d_up = d_act * ffn_gate * sig
    d_gate_up = jnp.concatenate([d_gate.astype(LOW), d_up.astype(LOW)], axis=1)
    d_two_part = mm_nt(d_gate_up, full_gate_up).astype(LOW)
    d_normed_two = scatter_seq(d_two_part.reshape(SEQ, rows, D), FULL)
    grad_gate_up_sum = scatter_dp(mm_tn(normed_two, d_gate_up).reshape(dp_total, block_rows, -1))
    grad_down_sum = scatter_dp(mm_tn(d_ffn_group, ffn_act).reshape(dp_total, block_rows, -1))
    grad_gate_up = grad_gate_up_sum.reshape(block_rows, 2, UNITS_PAD)[:, :, :UNITS]
    grad_down = grad_down_sum[:, :UNITS]

    d_x_tail, d_attn_o, d_ssm_o, d_gains = pull_join((d_total, d_normed_two))
    d_attn_own = d_attn_o.astype(LOW)
    d_attn = gather_seq(d_attn_own).reshape(group, D)
    d_ssm = gather_seq(d_ssm_o.astype(LOW)).reshape(group, D)
    d_gated = mm(d_ssm, w_out_t)
    d_attended = jnp.concatenate([mm(d_attn, w_o_t), mm(d_attn_own, w_o5_t)]).astype(LOW)

    def padded(a, width):
        return jnp.pad(a.astype(LOW), ((0, 0), (0, width - a.shape[1])))

    grad_out_t = jnp.concatenate(
        [
            padded(mm_tn(d_ssm, gated), O_AT),
            padded(mm_tn(d_attn, attended[:group]), O5_AT - O_AT),
            mm_tn(d_attn_own, attended[group:]).astype(LOW),
        ],
        axis=1,
    ).reshape(SEQ, D // SEQ, OUT_WIDTH)
    cut_for = lambda peer: lax.dynamic_index_in_dim(grad_out_t, peer, 0, False)
    arrived = place([(s, cut_for(s))] + [(s ^ bit, swap(cut_for(s ^ bit), "seq", bit)) for bit in (1, 2, 3)])
    arrived = arrived.transpose(0, 2, 1)
    grad_o_cols = jnp.concatenate(
        [arrived[j, O_AT : O_AT + QW] for j in range(SEQ)]
        + [jnp.sum(arrived[:, O5_AT:].astype(FULL), axis=0).astype(LOW)]
    )
    grad_mamba_cols = jnp.concatenate(
        [arrived[j, : HEAD_COUNT[j] * SSM_HEAD] for j in range(SEQ)]
    )
    grad_out_sum = scatter_dp(
        jnp.concatenate(
            [
                grad_o_cols.reshape(dp_total, block_rows, -1),
                grad_mamba_cols.reshape(dp_total, out_block, -1),
            ],
            axis=1,
        )
    )
    grad_o, grad_out = grad_out_sum[:block_rows], grad_out_sum[block_rows:]

    d_act_conv, d_bcdt, d_rate, d_skip, d_gate_z = pull_ssm(d_gated)
    d_raw, d_conv = pull_conv(d_act_conv)
    d_xzb = jnp.concatenate([d_raw, d_gate_z, d_bcdt], axis=1).astype(LOW)
    grad_xz_part = scatter_dp(mm_tn(normed, d_xzb).reshape(dp_total, block_rows, -1))
    xz_all = gather_seq(grad_xz_part.astype(LOW)).astype(FULL)
    x_cols = [xz_all[j, :, : HEAD_COUNT[j] * SSM_HEAD] for j in range(SEQ)]
    z_cols = [xz_all[j, :, LOCAL_CH : LOCAL_CH + HEAD_COUNT[j] * SSM_HEAD] for j in range(SEQ)]
    xz_width = w_xz.shape[1]
    grad_xz = lax.dynamic_slice_in_dim(jnp.concatenate(x_cols + z_cols, axis=1), s * xz_width, xz_width, 1)
    bc_at = 2 * LOCAL_CH
    grad_bcdt = jnp.concatenate(
        [jnp.sum(xz_all[:, :, bc_at : bc_at + 2 * STATE], axis=0)]
        + [xz_all[j, :, bc_at + 2 * STATE : bc_at + 2 * STATE + HEAD_COUNT[j]] for j in range(SEQ)],
        axis=1,
    )

    d_queries, d_kv = attention_backward(queries, kv, logs, d_attended, steps, rows)
    d_kvq = jnp.concatenate([d_kv, d_queries[:group]], axis=1)
    d_q_last = d_queries[group:]
    grad_qkv_part = scatter_dp(
        jnp.concatenate(
            [mm_tn(normed, d_kvq).astype(LOW), mm_tn(normed_own, d_q_last).astype(LOW)], axis=1
        ).reshape(dp_total, block_rows, -1)
    )
    qkv_all = gather_seq(grad_qkv_part.astype(LOW)).astype(FULL)
    col = lambda j, at, width: qkv_all[j, :, at : at + width]
    last = lambda at, width: jnp.sum(qkv_all[:, :, at : at + width], axis=0)
    grad_qkv_wide = jnp.concatenate(
        [col(j, 256, QW) for j in range(SEQ)]
        + [last(256 + QW, QW)]
        + [col(j, 0, HEAD) for j in range(SEQ)]
        + [last(128, HEAD)]
        + [col(j, HEAD, HEAD) for j in range(SEQ)]
        + [last(128 + HEAD, HEAD)],
        axis=1,
    )
    qkv_width = w_qkv.shape[1]
    grad_qkv = lax.dynamic_slice_in_dim(grad_qkv_wide, s * qkv_width, qkv_width, 1)

    d_normed_part = mm_nt(d_xzb, full_xz) + mm_nt(d_kvq, full_qkv[:, : 256 + QW])
    d_normed = scatter_seq(d_normed_part.astype(LOW).reshape(SEQ, rows, D), FULL)
    d_normed = d_normed + mm_nt(d_q_last, full_qkv[:, 256 + QW :])
    _, pull_norm = jax.vjp(rms_norm, inputs_x, gains[0])
    d_x_head, d_gain_first = pull_norm(d_normed)
    input_grad = (d_x_tail + d_x_head).astype(LOW)
    d_gains = d_gains.at[0].add(d_gain_first)

    d_rate = own_spread(d_rate, s, 1)
    d_skip = own_spread(d_skip, s, 1)
    d_conv = own_spread(d_conv, s, SSM_HEAD)
    flat = jnp.concatenate([d_conv.reshape(-1), d_gains.reshape(-1), d_rate, d_skip])
    size = flat.shape[0]
    flat = jnp.pad(flat, (0, -size % 1024)).reshape(-1, 128)
    flat = sum_all(flat).reshape(-1)[:size]
    conv_sum = flat[: CONV * INNER].reshape(CONV, INNER)
    gain_sum = flat[CONV * INNER : CONV * INNER + 4 * D].reshape(4, D)
    grad_conv = lax.dynamic_slice_in_dim(conv_sum, dp_index * conv_block, conv_block, 1)
    grad_gains = lax.dynamic_slice_in_dim(gain_sum, dp_index * gains_block, gains_block, 1)
    grad_rate = flat[size - 2 * SSM_HEADS : size - SSM_HEADS]
    grad_skip = flat[size - SSM_HEADS :]
    return (
        mixed_out,
        input_grad,
        grad_gains,
        grad_qkv,
        grad_o,
        grad_xz,
        grad_bcdt,
        grad_conv,
        grad_rate,
        grad_skip,
        grad_out,
        grad_gate_up,
        grad_down,
    )


def solution(mesh):
    placed = (
        P(("dp", "seq"), None),
        P("dp", None),
        P(None, "dp"),
        P("dp", "seq"),
        P("dp", "seq"),
        P("dp", "seq"),
        P("dp", None),
        P(None, "dp"),
        P(),
        P(),
        P("dp", "seq"),
        P("dp", None, "seq"),
        P("dp", "seq"),
        P(("dp", "seq"), None),
    )
    return jax.shard_map(
        on_device,
        mesh=mesh,
        in_specs=placed,
        out_specs=(
            P(("dp", "seq"), None),
            P(("dp", "seq"), None),
            P(None, "dp"),
            P("dp", "seq"),
            P("dp", "seq"),
            P("dp", "seq"),
            P("dp", None),
            P(None, "dp"),
            P(),
            P(),
            P("dp", "seq"),
            P("dp", None, "seq"),
            P("dp", "seq"),
        ),
        check_vma=False,
    )
```

```python
import jax
import jax.numpy as jnp
from jax import lax
from jax.experimental import pallas as pl
from jax.experimental.pallas import tpu as pltpu
from jax.sharding import PartitionSpec as P

D = 1600
HEADS = 25
KV_HEADS = 5
HEAD = 64
INNER = 3200
SSM_HEAD = 64
STATE = 16
CONV = 4
FF = 5504
WINDOW = 1024
SSM_HEADS = 50

NORM_EPS = 1e-05
MASKED = -1e30
LOW = jnp.bfloat16
FULL = jnp.float32

SEQ = 4
GROUP_HEADS = HEADS // KV_HEADS
QW = GROUP_HEADS * HEAD
LOCAL_HEADS = 13
LOCAL_CH = LOCAL_HEADS * SSM_HEAD
CHUNK = 128
UNITS = FF // SEQ
UNITS_PAD = 1408
BCDT_PAD = 128
OUT_AT, O_AT, O5_AT, OUT_WIDTH = 0, 896, 1280, 1600
FIRST_HEAD = tuple((SSM_HEADS * s // 2 + 1) // 2 for s in range(SEQ))
HEAD_COUNT = tuple(b - a for a, b in zip(FIRST_HEAD, FIRST_HEAD[1:] + (SSM_HEADS,)))


def swap(value, axis, bit):
    return lax.ppermute(value, axis, [(i, i ^ bit) for i in range(lax.axis_size(axis))])


def place_kernel(count, index_ref, *refs):
    blocks, stacked, held, in_sems, out_sems = refs[:count], *refs[count:]
    loads = [
        pltpu.make_async_copy(block, held.at[i], in_sems.at[i]) for i, block in enumerate(blocks)
    ]
    stores = [
        pltpu.make_async_copy(held.at[i], stacked.at[index_ref[i]], out_sems.at[i])
        for i in range(count)
    ]
    for load in loads:
        load.start()
    for load, store in zip(loads, stores):
        load.wait()
        store.start()
    for store in stores:
        store.wait()


def place(blocks):
    count = len(blocks)
    block = blocks[0][1]
    anywhere = pl.BlockSpec(memory_space=pl.ANY)
    return pl.pallas_call(
        lambda *refs: place_kernel(count, *refs),
        out_shape=jax.ShapeDtypeStruct((count,) + block.shape, block.dtype),
        grid_spec=pltpu.PrefetchScalarGridSpec(
            num_scalar_prefetch=1,
            grid=(1,),
            in_specs=[anywhere] * count,
            out_specs=anywhere,
            scratch_shapes=[
                pltpu.VMEM((count,) + block.shape, block.dtype),
                pltpu.SemaphoreType.DMA((count,)),
                pltpu.SemaphoreType.DMA((count,)),
            ],
        ),
        compiler_params=pltpu.CompilerParams(vmem_limit_bytes=32 << 20),
        cost_estimate=pl.CostEstimate(
            flops=0, bytes_accessed=2 * count * block.size * block.dtype.itemsize, transcendentals=0
        ),
    )(jnp.stack([jnp.asarray(i, jnp.int32) for i, _ in blocks]), *[b for _, b in blocks])


def gather_seq(block):
    me = lax.axis_index("seq")
    far = swap(block, "seq", 2)
    near = swap(block, "seq", 1)
    near_far = swap(far, "seq", 1)
    return place([(me, block), (me ^ 1, near), (me ^ 2, far), (me ^ 3, near_far)])


def scatter_seq(rows, out_dtype):
    me = lax.axis_index("seq")
    core, far = me % 2, me // 2
    by_core = rows.reshape((2, 2) + rows.shape[1:])
    give = lax.dynamic_index_in_dim(by_core, 1 - core, 1, False)
    keep = lax.dynamic_index_in_dim(by_core, core, 1, False)
    got = swap(give, "seq", 1)
    give_far = (
        lax.dynamic_index_in_dim(keep, 1 - far, 0, False).astype(FULL)
        + lax.dynamic_index_in_dim(got, 1 - far, 0, False).astype(FULL)
    ).astype(LOW)
    got_far = swap(give_far, "seq", 2)
    return (
        lax.dynamic_index_in_dim(keep, far, 0, False).astype(FULL)
        + lax.dynamic_index_in_dim(got, far, 0, False).astype(FULL)
        + got_far.astype(FULL)
    ).astype(out_dtype)


def line_place():
    me = lax.axis_index("dp")
    return lax.axis_size("dp") // 2, me // 2, lax.rem(me, 2)


def greet(line, z, x):
    barrier = pltpu.get_barrier_semaphore()

    def signal(target):
        pl.semaphore_signal(
            barrier, inc=1, device_id={"dp": target}, device_id_type=pl.DeviceIdType.MESH
        )

    signal(2 * z + 1 - x)
    pl.when(z > 0)(lambda: signal(2 * (z - 1) + x))
    pl.when(z < line - 1)(lambda: signal(2 * (z + 1) + x))
    pl.semaphore_wait(
        barrier, 1 + (z > 0).astype(jnp.int32) + (z < line - 1).astype(jnp.int32)
    )


def gather_kernel(count, line, *refs):
    packets, outs = refs[:count], refs[count : 2 * count]
    own_sem, up_sem, down_sem, line_sem, give_sem, got_sem = refs[2 * count :]
    _, z, x = line_place()
    greet(line, z, x)

    def copy(src, i, zb, send_sem, recv_sem, target):
        return pltpu.make_async_remote_copy(
            src_ref=src,
            dst_ref=outs[i].at[2 * zb + x],
            send_sem=send_sem.at[i, zb],
            recv_sem=recv_sem.at[i, zb],
            device_id={"dp": target},
            device_id_type=pl.DeviceIdType.MESH,
        )

    up_to = lambda src, i, zb: copy(src, i, zb, up_sem, line_sem, 2 * (z + 1) + x)
    down_to = lambda src, i, zb: copy(src, i, zb, down_sem, line_sem, 2 * (z - 1) + x)
    give = lambda src, i, zb: copy(src, i, zb, give_sem, got_sem, 2 * z + 1 - x)
    held = lambda i, zb: outs[i].at[2 * zb + x]
    own = lambda i: pltpu.make_async_copy(packets[i], held(i, z), own_sem.at[i])

    for turn in range(count + line - 1):
        for i in range(count):
            far = turn - i
            if far == 0:
                own(i).start()
                give(packets[i], i, z).start()
                pl.when(z < line - 1)(lambda: up_to(packets[i], i, z).start())
                pl.when(z > 0)(lambda: down_to(packets[i], i, z).start())
            elif 0 < far < line:

                @pl.when(z - far >= 0)
                def _():
                    zb = z - far
                    up_to(held(i, zb), i, zb).wait_recv()
                    pl.when(z < line - 1)(lambda: up_to(held(i, zb), i, zb).start())
                    give(held(i, zb), i, zb).start()

                @pl.when(z + far < line)
                def _():
                    zb = z + far
                    down_to(held(i, zb), i, zb).wait_recv()
                    pl.when(z > 0)(lambda: down_to(held(i, zb), i, zb).start())
                    give(held(i, zb), i, zb).start()

    for i in range(count):
        own(i).wait()
        for zb in range(line):
            give(held(i, zb), i, zb).wait()
            pl.when((zb <= z) & (z < line - 1))(lambda: up_to(held(i, zb), i, zb).wait_send())
            pl.when((zb >= z) & (z > 0))(lambda: down_to(held(i, zb), i, zb).wait_send())


def gather_dp(packets, collective_id):
    total = lax.axis_size("dp")
    if total != 8:
        return [lax.all_gather(packet, "dp", axis=0) for packet in packets]
    count, line = len(packets), total // 2
    sems = lambda *shape: pltpu.SemaphoreType.DMA(shape)
    return pl.pallas_call(
        lambda *refs: gather_kernel(count, line, *refs),
        out_shape=[jax.ShapeDtypeStruct((total,) + p.shape, p.dtype) for p in packets],
        in_specs=[pl.BlockSpec(memory_space=pltpu.VMEM)] * count,
        out_specs=[pl.BlockSpec(memory_space=pl.ANY)] * count,
        scratch_shapes=[sems(count)] + [sems(count, line) for _ in range(5)],
        compiler_params=pltpu.CompilerParams(
            collective_id=collective_id, has_side_effects=True, vmem_limit_bytes=32 << 20
        ),
        cost_estimate=pl.CostEstimate(
            flops=0,
            bytes_accessed=2 * total * sum(p.size * p.dtype.itemsize for p in packets),
            transcendentals=0,
        ),
    )(*packets)


def add_columns(total, parts):
    width = total.shape[-1]
    step = 128 if width % 256 else 256

    def columns(c):
        at = pl.ds(pl.multiple_of(c * step, step), step)
        total[:, at] = sum(part[:, at].astype(FULL) for part in parts).astype(total.dtype)

    pl.loop(0, width // step)(columns)
    if width % step:
        at = slice(width // step * step, width)
        total[:, at] = sum(part[:, at].astype(FULL) for part in parts).astype(total.dtype)


def scatter_kernel(count, line, *refs):
    parts, outs = refs[:count], refs[count : 2 * count]
    own_refs, near_refs, line_refs = (
        refs[2 * count : 3 * count],
        refs[3 * count : 4 * count],
        refs[4 * count : 5 * count],
    )
    load_sem, give_sem, got_sem, send_sem, line_sem = refs[5 * count :]
    _, z, x = line_place()
    greet(line, z, x)
    order = [t for pair in zip(range(line - 1, -1, -1), range(line)) for t in pair][:line]
    remote = lambda src, dst, send, recv, target: pltpu.make_async_remote_copy(
        src_ref=src,
        dst_ref=dst,
        send_sem=send,
        recv_sem=recv,
        device_id={"dp": target},
        device_id_type=pl.DeviceIdType.MESH,
    )
    give = lambda i, t: remote(
        parts[i].at[2 * t + 1 - x],
        near_refs[i].at[t],
        give_sem.at[i, t],
        got_sem.at[i, t],
        2 * z + 1 - x,
    )
    load = lambda i, t: pltpu.make_async_copy(
        parts[i].at[2 * t + x], own_refs[i].at[t], load_sem.at[i, t]
    )
    along = lambda i, t, slot, target: remote(
        own_refs[i].at[t], line_refs[i].at[slot], send_sem.at[i, t], line_sem.at[i, slot], target
    )
    for i in range(count):
        for t in order:
            load(i, t).start()
            give(i, t).start()
    for i in range(count):
        own, near, held = own_refs[i], near_refs[i], line_refs[i]
        for t in order:
            load(i, t).wait()
            give(i, t).wait_recv()

            @pl.when((t > z) & (z > 0) | (t < z) & (z < line - 1))
            def _():
                along(i, t, t, 0).wait_recv()
                add_columns(own.at[t], (own.at[t], near.at[t], held.at[t]))

            @pl.when((t > z) & (z == 0) | (t < z) & (z == line - 1))
            def _():
                add_columns(own.at[t], (own.at[t], near.at[t]))

            pl.when(t > z)(lambda: along(i, t, t, 2 * (z + 1) + x).start())
            pl.when(t == z - 1)(lambda: along(i, t, line, 2 * (z - 1) + x).start())
            pl.when(t < z - 1)(lambda: along(i, t, t, 2 * (z - 1) + x).start())
    for i in range(count):
        own, near, held = own_refs[i], near_refs[i], line_refs[i]
        pl.when(z > 0)(lambda: along(i, z, z, 0).wait_recv())
        pl.when(z < line - 1)(lambda: along(i, z, line, 0).wait_recv())
        for t in range(line):

            @pl.when(t == z)
            def _():
                terms = [own.at[t], near.at[t]]
                terms += [held.at[t]] if t > 0 else []
                terms += [held.at[line]] if t < line - 1 else []
                add_columns(outs[i], terms)

            pl.when(t != z)(lambda: along(i, t, t, 0).wait_send())
            give(i, t).wait_send()


def scatter_dp(parts, collective_id):
    parts = [p.astype(LOW) for p in parts]
    total = lax.axis_size("dp")
    if total != 8:
        sums = [lax.psum_scatter(p, "dp", scatter_dimension=0) for p in parts]
        return [lax.optimization_barrier(p).astype(FULL) for p in sums]
    count, line = len(parts), total // 2
    sems = lambda *shape: pltpu.SemaphoreType.DMA(shape)
    return pl.pallas_call(
        lambda *refs: scatter_kernel(count, line, *refs),
        out_shape=[jax.ShapeDtypeStruct(p.shape[1:], FULL) for p in parts],
        in_specs=[pl.BlockSpec(memory_space=pl.ANY)] * count,
        out_specs=[pl.BlockSpec(memory_space=pltpu.VMEM)] * count,
        scratch_shapes=[pltpu.VMEM((line,) + p.shape[1:], LOW) for p in parts]
        + [pltpu.VMEM((line,) + p.shape[1:], LOW) for p in parts]
        + [pltpu.VMEM((line + 1,) + p.shape[1:], LOW) for p in parts]
        + [sems(count, line) for _ in range(4)]
        + [sems(count, line + 1)],
        compiler_params=pltpu.CompilerParams(
            collective_id=collective_id, has_side_effects=True, vmem_limit_bytes=56 << 20
        ),
        cost_estimate=pl.CostEstimate(
            flops=0, bytes_accessed=sum(p.size * 2 for p in parts), transcendentals=0
        ),
    )(*parts)


def gather_dp_apart(packet):
    return lax.all_gather(packet, "dp", axis=0)


def scatter_dp_apart(parts):
    summed = lax.psum_scatter(parts.astype(LOW), "dp", scatter_dimension=0)
    return lax.optimization_barrier(summed).astype(FULL)


def trade_halves(first, last):
    me = lax.axis_index("seq")
    one = lax.ppermute(jnp.where(me == 0, last, first), "seq", [(0, 1), (1, 2), (2, 0)])
    two = lax.ppermute(jnp.where(me == 3, first, last), "seq", [(1, 3), (2, 1), (3, 2)])
    return pick([first, one, one, two], me), pick([one, two, two, last], me)


def trade_back(x_part, z_part):
    me = lax.axis_index("seq")
    one = lax.ppermute(jnp.where(me == 0, z_part, x_part), "seq", [(1, 0), (2, 1), (0, 2)])
    two = lax.ppermute(jnp.where(me == 3, x_part, z_part), "seq", [(3, 1), (1, 2), (2, 3)])
    return pick([x_part, one, one, two], me), pick([one, two, two, z_part], me)


def sum_all(value):
    for axis in ("seq", "dp"):
        bit = 1
        while bit < lax.axis_size(axis):
            value = value + swap(value, axis, bit)
            bit *= 2
    return value


def mm(left, right):
    return jnp.dot(left, right, preferred_element_type=FULL)


def mm_nt(left, right):
    return lax.dot_general(left, right, (((1,), (1,)), ((), ())), preferred_element_type=FULL)


def mm_tn(left, right):
    return lax.dot_general(left, right, (((0,), (0,)), ((), ())), preferred_element_type=FULL)


def rms_norm(values, gain):
    return values * lax.rsqrt(jnp.mean(values * values, axis=-1, keepdims=True) + NORM_EPS) * gain


def join_tail(inputs_x, attn_o, ssm_o, gains):
    residual = inputs_x + 0.5 * (rms_norm(attn_o, gains[1]) + rms_norm(ssm_o, gains[2]))
    return (residual, rms_norm(residual, gains[3]))


def document_ids(lengths, positions):
    first_end = lengths[0]
    second_end = lengths[0] + lengths[1]
    return (positions >= first_end).astype(jnp.int32) + (positions >= second_end).astype(jnp.int32)


def convolve(raw_x, conv_weight, doc_ids):
    row_count = raw_x.shape[0]
    padded = jnp.pad(raw_x, ((CONV - 1, 0), (0, 0)))
    padded_ids = jnp.pad(doc_ids, (CONV - 1, 0), constant_values=-1)
    conv_sum = jnp.zeros(raw_x.shape, FULL)
    for tap in range(CONV):
        same = (padded_ids[tap : tap + row_count] == doc_ids).astype(FULL)
        conv_sum = conv_sum + conv_weight[tap] * padded[tap : tap + row_count] * same[:, None]
    return jax.nn.silu(conv_sum)


def allowed_block(row_ids, row_pos, key_ids, key_pos):
    distance = row_pos[:, None] - key_pos[None, :]
    return (distance >= 0) & (distance < WINDOW) & (row_ids[:, None] == key_ids[None, :])


def head_forward(q, k, v, allowed):
    scale = HEAD ** (-0.5)
    scores = scale * jnp.einsum("gtd,sd->gts", q, k, preferred_element_type=FULL)
    scores = jnp.where(allowed[None], scores, MASKED)
    top = jnp.max(scores, axis=-1, keepdims=True)
    expos = jnp.exp(scores - top)
    denom = jnp.sum(expos, axis=-1, keepdims=True)
    weights = (expos / denom).astype(LOW)
    mixed = jnp.einsum("gts,sd->gtd", weights, v, preferred_element_type=FULL)
    return mixed, top + jnp.log(denom)


def head_backward(q, k, v, allowed, log_total, d_mixed):
    scale = HEAD ** (-0.5)
    scores = scale * jnp.einsum("gtd,sd->gts", q, k, preferred_element_type=FULL)
    probs = jnp.where(allowed[None], jnp.exp(scores - log_total), 0.0)
    d_v = jnp.einsum("gts,gtd->sd", probs.astype(LOW), d_mixed, preferred_element_type=FULL)
    d_probs = jnp.einsum("gtd,sd->gts", d_mixed, v, preferred_element_type=FULL)
    d_scores = probs * (d_probs - jnp.sum(probs * d_probs, axis=-1, keepdims=True))
    d_low = d_scores.astype(LOW)
    d_q = scale * jnp.einsum("gts,sd->gtd", d_low, k, preferred_element_type=FULL)
    d_k = scale * jnp.einsum("gts,gtd->sd", d_low, q, preferred_element_type=FULL)
    return d_q, d_k, d_v


def to_heads(block):
    return block.reshape(block.shape[0], GROUP_HEADS, HEAD).transpose(1, 0, 2)


def from_heads(block):
    return block.transpose(1, 0, 2).reshape(block.shape[1], QW)


def attention_steps(rows, seq_index, doc_ids):
    positions = jnp.arange(doc_ids.shape[0], dtype=jnp.int32)
    steps = []
    for t in range(SEQ + 1):
        last = t == SEQ
        extent = (SEQ if last else t + 1) * rows
        at = seq_index * rows if last else t * rows
        allowed = allowed_block(
            lax.dynamic_slice_in_dim(doc_ids, at, rows),
            lax.dynamic_slice_in_dim(positions, at, rows),
            doc_ids[:extent],
            positions[:extent],
        )
        steps.append((t, 1 if last else 0, extent, allowed))
    return steps


def attention_forward(queries, kv, steps, rows):
    out, logs = [], []
    for t, which, extent, allowed in steps:
        k = kv[:extent, which * 128 : which * 128 + 64]
        v = kv[:extent, which * 128 + 64 : which * 128 + 128]
        mixed, log_total = head_forward(to_heads(queries[t * rows : (t + 1) * rows]), k, v, allowed)
        out.append(from_heads(mixed).astype(LOW))
        logs.append(log_total)
    return jnp.concatenate(out), logs


def attention_backward(queries, kv, logs, d_out, steps, rows):
    d_q = []
    d_k = [jnp.zeros((kv.shape[0], HEAD), FULL) for _ in range(2)]
    d_v = [jnp.zeros((kv.shape[0], HEAD), FULL) for _ in range(2)]
    for (t, which, extent, allowed), log_total in zip(steps, logs):
        k = kv[:extent, which * 128 : which * 128 + 64]
        v = kv[:extent, which * 128 + 64 : which * 128 + 128]
        part = slice(t * rows, (t + 1) * rows)
        q_one, k_one, v_one = head_backward(
            to_heads(queries[part]), k, v, allowed, log_total, to_heads(d_out[part])
        )
        d_q.append(from_heads(q_one))
        d_k[which] = d_k[which].at[:extent].add(k_one)
        d_v[which] = d_v[which].at[:extent].add(v_one)
    d_kv = jnp.concatenate([d_k[0], d_v[0], d_k[1], d_v[1]], axis=1)
    return jnp.concatenate(d_q).astype(LOW), d_kv.astype(LOW)


def ssm_group(conv_act, bcdt, rate, skip, gate_z, doc_ids):
    total = conv_act.shape[0]
    chunks = total // CHUNK
    heads = rate.shape[0]
    low = lambda v: v.astype(LOW)
    ein = lambda spec, *v: jnp.einsum(spec, *v, preferred_element_type=FULL)
    ids = doc_ids.reshape(chunks, CHUNK)
    ids_prev = jnp.concatenate([jnp.full((1,), -1, jnp.int32), ids[:-1, -1]])
    step = jax.nn.softplus(bcdt[:, 2 * STATE : 2 * STATE + heads]).reshape(chunks, CHUNK, heads)
    b_in = bcdt[:, :STATE].reshape(chunks, CHUNK, STATE)
    c_in = bcdt[:, STATE : 2 * STATE].reshape(chunks, CHUNK, STATE)
    x = conv_act.reshape(chunks, CHUNK, heads, SSM_HEAD)
    places = jnp.arange(CHUNK, dtype=jnp.int32)
    before = (places[:, None] >= places[None, :]).astype(FULL)
    log = jnp.einsum("ts,csh->cth", before, -step * rate, precision=lax.Precision.HIGHEST)
    causal = (places[:, None] >= places[None, :])[None] & (ids[:, :, None] == ids[:, None, :])
    log_h = log.transpose(0, 2, 1)
    gap = log_h[:, :, :, None] - log_h[:, :, None, :]
    decays = jnp.where(causal[:, None], jnp.exp(jnp.where(causal[:, None], gap, 0.0)), 0.0)
    gram = ein("ctn,csn->cts", low(c_in), low(b_in))
    mixing = decays * gram[:, None]
    step_x = low(x * step[..., None])
    within = ein("chts,cshd->cthd", low(mixing), step_x)
    last = log[:, -1]
    ends = jnp.exp(last[:, None] - log) * (ids == ids[:, -1:]).astype(FULL)[..., None]
    state_end = ein("cshd,csn->chnd", low(x * (step * ends)[..., None]), low(b_in))
    carry = jnp.exp(last) * (ids[:, -1] == ids_prev).astype(FULL)[:, None]
    state = jnp.zeros(state_end.shape[1:], FULL)
    states = []
    for c in range(chunks):
        states.append(state)
        state = carry[c][:, None, None] * state + state_end[c]
    states = jnp.stack(states)
    reach = jnp.exp(log) * (ids == ids_prev[:, None]).astype(FULL)[..., None]
    from_state = ein("ctn,chnd->cthd", low(c_in), low(states)) * reach[..., None]
    read = within + from_state + skip[:, None] * x
    return read.reshape(total, heads * SSM_HEAD) * jax.nn.silu(gate_z)


def pick(options, seq_index):
    return lax.select_n(seq_index, *options)


def own_cut(values, seq_index, axis, unit):
    cuts = []
    for first, count in zip(FIRST_HEAD, HEAD_COUNT):
        cut = lax.slice_in_dim(values, first * unit, (first + count) * unit, axis=axis)
        pads = [(0, 0)] * values.ndim
        pads[axis] = (0, (LOCAL_HEADS - count) * unit)
        cuts.append(jnp.pad(cut, pads))
    return pick(cuts, seq_index)


def own_spread(values, seq_index, unit):
    spreads = []
    for first, count in zip(FIRST_HEAD, HEAD_COUNT):
        pads = [(0, 0)] * (values.ndim - 1) + [(first * unit, (SSM_HEADS - first - count) * unit)]
        spreads.append(jnp.pad(values[..., : count * unit], pads))
    return pick(spreads, seq_index)


def channel_cut(wide, seq_index, axis):
    return own_cut(wide, seq_index, axis, SSM_HEAD)


def bcdt_cut(w_bcdt, seq_index):
    first = pick([jnp.int32(h) for h in FIRST_HEAD], seq_index)
    count = pick([jnp.int32(c) for c in HEAD_COUNT], seq_index)
    source = jnp.arange(w_bcdt.shape[1], dtype=jnp.int32)[:, None]
    target = jnp.arange(BCDT_PAD, dtype=jnp.int32)[None]
    shared = (target < 2 * STATE) & (source == target)
    steps = (target >= 2 * STATE) & (target < 2 * STATE + count) & (source == target + first)
    return mm(w_bcdt, (shared | steps).astype(LOW)).astype(LOW)


def wide_of(gathered):
    return gathered.transpose(1, 0, 2).reshape(gathered.shape[1], -1)


def on_device(
    tokens_in,
    doc_lengths,
    norm_gains,
    w_qkv,
    w_o,
    w_xz,
    w_bcdt,
    conv_w,
    ssm_rate,
    ssm_skip,
    w_out,
    w_gate_up,
    w_down,
    cotangent,
):
    rows = tokens_in.shape[0]
    group = rows * SEQ
    s = lax.axis_index("seq")
    dp_index = lax.axis_index("dp")
    dp_total = lax.axis_size("dp")
    block_rows = w_qkv.shape[0]
    kv_width = KV_HEADS * HEAD
    lengths = doc_lengths[0]
    doc_ids = document_ids(lengths, jnp.arange(group, dtype=jnp.int32))
    live = (jnp.arange(rows, dtype=jnp.int32) + s * rows < lengths[0] + lengths[1]).astype(FULL)[:, None]

    gains_block = norm_gains.shape[1]
    conv_block = conv_w.shape[1]
    width = -(-max(conv_block, gains_block) // 128) * 128
    small = jnp.concatenate(
        [
            jnp.pad(conv_w, ((0, 4), (0, width - conv_block))),
            jnp.pad(norm_gains, ((0, 4), (0, width - gains_block))),
        ]
    )
    (small,) = gather_dp([small], 0)
    full_conv = small[:, :4, :conv_block].transpose(1, 0, 2).reshape(4, INNER).astype(FULL)
    gains = small[:, 8:12, :gains_block].transpose(1, 0, 2).reshape(4, D).astype(FULL)

    tokens_group = gather_seq(tokens_in).reshape(group, D)
    qkv_wide = wide_of(gather_seq(w_qkv))
    q_at = lambda h: lax.dynamic_slice_in_dim(qkv_wide, h * QW, QW, 1)
    kv_at = lambda h: [
        lax.dynamic_slice_in_dim(qkv_wide, D + h * HEAD, HEAD, 1),
        lax.dynamic_slice_in_dim(qkv_wide, D + kv_width + h * HEAD, HEAD, 1),
    ]
    qkv_packet = jnp.concatenate(kv_at(s) + kv_at(KV_HEADS - 1) + [q_at(s), q_at(KV_HEADS - 1)], axis=1)
    bcdt_own = bcdt_cut(w_bcdt, s)
    x_part, z_part = trade_halves(
        w_xz[:, :LOCAL_CH], jnp.pad(w_xz[:, LOCAL_CH:], ((0, 0), (0, 2 * LOCAL_CH - w_xz.shape[1])))
    )
    xz_packet = jnp.concatenate(
        [
            x_part,
            z_part,
            bcdt_own,
        ],
        axis=1,
    )
    out_block = w_out.shape[0]
    out_packet = jnp.concatenate([w_o, w_out], axis=0)
    full_qkv, full_xz, out_cols = gather_dp([qkv_packet, xz_packet, out_packet], 1)
    full_qkv = full_qkv.reshape(D, -1)
    full_xz = full_xz.reshape(D, -1)
    o_cols = out_cols[:, :block_rows].reshape(D, -1)
    mamba_cols = out_cols[:, block_rows:].reshape(INNER, -1)

    def rows_for(peer):
        return jnp.concatenate(
            [
                jnp.pad(channel_cut(mamba_cols, peer, 0).T, ((0, 0), (0, O_AT - LOCAL_CH))),
                jnp.pad(
                    lax.dynamic_slice_in_dim(o_cols, peer * QW, QW, 0).T, ((0, 0), (0, O5_AT - O_AT - QW))
                ),
                o_cols[(KV_HEADS - 1) * QW :].T,
            ],
            axis=1,
        )

    out_t = place(
        [(s, rows_for(s))] + [(s ^ bit, swap(rows_for(s ^ bit), "seq", bit)) for bit in (1, 2, 3)]
    ).reshape(D, OUT_WIDTH)
    w_out_t = out_t[:, :LOCAL_CH]
    w_o_t = out_t[:, O_AT : O_AT + QW]
    w_o5_t = out_t[:, O5_AT:]

    gate_up_packet = jnp.pad(w_gate_up, ((0, 0), (0, 0), (0, UNITS_PAD - UNITS))).reshape(block_rows, -1)
    full_gate_up = gather_dp_apart(gate_up_packet).reshape(D, -1)
    full_down = gather_dp_apart(jnp.pad(w_down, ((0, 0), (0, UNITS_PAD - UNITS)))).reshape(D, -1)

    d_total = cotangent.astype(FULL) * live
    d_ffn_group = gather_seq(d_total.astype(LOW)).reshape(group, D)

    own = lambda a: lax.dynamic_slice_in_dim(a, s * rows, rows, 0)
    normed = rms_norm(tokens_group.astype(FULL), gains[0]).astype(LOW)
    normed_own = own(normed)
    kvq = mm(normed, full_qkv[:, : 256 + QW]).astype(LOW)
    q_last = mm(normed_own, full_qkv[:, 256 + QW :]).astype(LOW)
    queries = jnp.concatenate([kvq[:, 256:], q_last])
    kv = kvq[:, :256]
    steps = attention_steps(rows, s, doc_ids)
    attended, logs = attention_forward(queries, kv, steps, rows)
    attn_part = mm_nt(attended[:group], w_o_t).astype(LOW)
    attn_o = scatter_seq(attn_part.reshape(SEQ, rows, D), FULL) + mm_nt(attended[group:], w_o5_t)

    xzb = mm(normed, full_xz)
    raw_x = xzb[:, :LOCAL_CH].astype(LOW)
    gate_z = xzb[:, LOCAL_CH : 2 * LOCAL_CH]
    bcdt = xzb[:, 2 * LOCAL_CH :]
    conv_own = channel_cut(full_conv, s, 1)
    rate = own_cut(ssm_rate, s, 0, 1)
    skip = own_cut(ssm_skip, s, 0, 1)
    conv_act, pull_conv = jax.vjp(
        lambda a, w: convolve(a, w, doc_ids), raw_x.astype(FULL), conv_own
    )
    gated, pull_ssm = jax.vjp(
        lambda *v: ssm_group(*v, doc_ids), conv_act, bcdt, rate, skip, gate_z
    )
    gated = gated.astype(LOW)
    ssm_part = mm_nt(gated, w_out_t).astype(LOW)
    ssm_o = scatter_seq(ssm_part.reshape(SEQ, rows, D), FULL)

    inputs_x = tokens_in.astype(FULL)
    (residual, normed_two), pull_join = jax.vjp(join_tail, inputs_x, attn_o, ssm_o, gains)
    normed_two = gather_seq(normed_two.astype(LOW)).reshape(group, D)
    gate_up = mm(normed_two, full_gate_up)
    ffn_gate, ffn_up = gate_up[:, :UNITS_PAD], gate_up[:, UNITS_PAD:]
    ffn_act = (jax.nn.silu(ffn_gate) * ffn_up).astype(LOW)
    ffn_part = mm_nt(ffn_act, full_down).astype(LOW)
    ffn_own = scatter_seq(ffn_part.reshape(SEQ, rows, D), FULL)
    mixed_out = ((residual + ffn_own) * live).astype(LOW)

    d_act = mm(d_ffn_group, full_down)
    sig = jax.nn.sigmoid(ffn_gate)
    d_gate = d_act * ffn_up * (sig * (1.0 + ffn_gate * (1.0 - sig)))
    d_up = d_act * ffn_gate * sig
    d_gate_up = jnp.concatenate([d_gate.astype(LOW), d_up.astype(LOW)], axis=1)
    d_two_part = mm_nt(d_gate_up, full_gate_up).astype(LOW)
    d_normed_two = scatter_seq(d_two_part.reshape(SEQ, rows, D), FULL)
    grad_gate_up_sum = scatter_dp_apart(mm_tn(normed_two, d_gate_up).reshape(dp_total, block_rows, -1))
    grad_down_sum = scatter_dp_apart(mm_tn(d_ffn_group, ffn_act).reshape(dp_total, block_rows, -1))
    grad_gate_up = grad_gate_up_sum.reshape(block_rows, 2, UNITS_PAD)[:, :, :UNITS]
    grad_down = grad_down_sum[:, :UNITS]

    d_x_tail, d_attn_o, d_ssm_o, d_gains = pull_join((d_total, d_normed_two))
    d_attn_own = d_attn_o.astype(LOW)
    d_attn = gather_seq(d_attn_own).reshape(group, D)
    d_ssm = gather_seq(d_ssm_o.astype(LOW)).reshape(group, D)
    d_gated = mm(d_ssm, w_out_t)
    d_attended = jnp.concatenate([mm(d_attn, w_o_t), mm(d_attn_own, w_o5_t)]).astype(LOW)

    def padded(a, width):
        return jnp.pad(a.astype(LOW), ((0, 0), (0, width - a.shape[1])))

    grad_out_t = jnp.concatenate(
        [
            padded(mm_tn(d_ssm, gated), O_AT),
            padded(mm_tn(d_attn, attended[:group]), O5_AT - O_AT),
            mm_tn(d_attn_own, attended[group:]).astype(LOW),
        ],
        axis=1,
    ).reshape(SEQ, D // SEQ, OUT_WIDTH)
    cut_for = lambda peer: lax.dynamic_index_in_dim(grad_out_t, peer, 0, False)
    arrived = place([(s, cut_for(s))] + [(s ^ bit, swap(cut_for(s ^ bit), "seq", bit)) for bit in (1, 2, 3)])
    arrived = arrived.transpose(0, 2, 1)
    grad_o_cols = jnp.concatenate(
        [arrived[j, O_AT : O_AT + QW] for j in range(SEQ)]
        + [jnp.sum(arrived[:, O5_AT:].astype(FULL), axis=0).astype(LOW)]
    )
    grad_mamba_cols = jnp.concatenate(
        [arrived[j, : HEAD_COUNT[j] * SSM_HEAD] for j in range(SEQ)]
    )
    grad_out_part = jnp.concatenate(
        [
            grad_o_cols.reshape(dp_total, block_rows, -1),
            grad_mamba_cols.reshape(dp_total, out_block, -1),
        ],
        axis=1,
    )

    d_act_conv, d_bcdt, d_rate, d_skip, d_gate_z = pull_ssm(d_gated)
    d_raw, d_conv = pull_conv(d_act_conv)
    d_xzb = jnp.concatenate([d_raw, d_gate_z, d_bcdt], axis=1).astype(LOW)
    grad_xz_part = mm_tn(normed, d_xzb).astype(LOW).reshape(dp_total, block_rows, -1)

    d_queries, d_kv = attention_backward(queries, kv, logs, d_attended, steps, rows)
    d_kvq = jnp.concatenate([d_kv, d_queries[:group]], axis=1)
    d_q_last = d_queries[group:]
    grad_qkv_part = jnp.concatenate(
        [mm_tn(normed, d_kvq).astype(LOW), mm_tn(normed_own, d_q_last).astype(LOW)], axis=1
    ).reshape(dp_total, block_rows, -1)
    grad_out_sum, grad_xz_sum, grad_qkv_sum = scatter_dp(
        [grad_out_part, grad_xz_part, grad_qkv_part], 2
    )
    grad_o, grad_out = grad_out_sum[:block_rows], grad_out_sum[block_rows:]
    grad_xz_sum = grad_xz_sum.astype(LOW)
    first, last = trade_back(grad_xz_sum[:, :LOCAL_CH], grad_xz_sum[:, LOCAL_CH : 2 * LOCAL_CH])
    grad_xz = jnp.concatenate([first, last], axis=1)[:, : w_xz.shape[1]].astype(FULL)
    bcdt_all = gather_seq(grad_xz_sum[:, 2 * LOCAL_CH :]).astype(FULL)
    grad_bcdt = jnp.concatenate(
        [jnp.sum(bcdt_all[:, :, : 2 * STATE], axis=0)]
        + [bcdt_all[j, :, 2 * STATE : 2 * STATE + HEAD_COUNT[j]] for j in range(SEQ)],
        axis=1,
    )
    qkv_all = gather_seq(grad_qkv_sum.astype(LOW)).astype(FULL)
    col = lambda j, at, width: qkv_all[j, :, at : at + width]
    shared = lambda at, width: jnp.sum(qkv_all[:, :, at : at + width], axis=0)
    grad_qkv_wide = jnp.concatenate(
        [col(j, 256, QW) for j in range(SEQ)]
        + [shared(256 + QW, QW)]
        + [col(j, 0, HEAD) for j in range(SEQ)]
        + [shared(128, HEAD)]
        + [col(j, HEAD, HEAD) for j in range(SEQ)]
        + [shared(128 + HEAD, HEAD)],
        axis=1,
    )
    qkv_width = w_qkv.shape[1]
    grad_qkv = lax.dynamic_slice_in_dim(grad_qkv_wide, s * qkv_width, qkv_width, 1)

    d_normed_part = mm_nt(d_xzb, full_xz) + mm_nt(d_kvq, full_qkv[:, : 256 + QW])
    d_normed = scatter_seq(d_normed_part.astype(LOW).reshape(SEQ, rows, D), FULL)
    d_normed = d_normed + mm_nt(d_q_last, full_qkv[:, 256 + QW :])
    _, pull_norm = jax.vjp(rms_norm, inputs_x, gains[0])
    d_x_head, d_gain_first = pull_norm(d_normed)
    input_grad = (d_x_tail + d_x_head).astype(LOW)
    d_gains = d_gains.at[0].add(d_gain_first)

    d_rate = own_spread(d_rate, s, 1)
    d_skip = own_spread(d_skip, s, 1)
    d_conv = own_spread(d_conv, s, SSM_HEAD)
    flat = jnp.concatenate([d_conv.reshape(-1), d_gains.reshape(-1), d_rate, d_skip])
    size = flat.shape[0]
    flat = jnp.pad(flat, (0, -size % 1024)).reshape(-1, 128)
    flat = sum_all(flat).reshape(-1)[:size]
    conv_sum = flat[: CONV * INNER].reshape(CONV, INNER)
    gain_sum = flat[CONV * INNER : CONV * INNER + 4 * D].reshape(4, D)
    grad_conv = lax.dynamic_slice_in_dim(conv_sum, dp_index * conv_block, conv_block, 1)
    grad_gains = lax.dynamic_slice_in_dim(gain_sum, dp_index * gains_block, gains_block, 1)
    grad_rate = flat[size - 2 * SSM_HEADS : size - SSM_HEADS]
    grad_skip = flat[size - SSM_HEADS :]
    return (
        mixed_out,
        input_grad,
        grad_gains,
        grad_qkv,
        grad_o,
        grad_xz,
        grad_bcdt,
        grad_conv,
        grad_rate,
        grad_skip,
        grad_out,
        grad_gate_up,
        grad_down,
    )


def solution(mesh):
    placed = (
        P(("dp", "seq"), None),
        P("dp", None),
        P(None, "dp"),
        P("dp", "seq"),
        P("dp", "seq"),
        P("dp", "seq"),
        P("dp", None),
        P(None, "dp"),
        P(),
        P(),
        P("dp", "seq"),
        P("dp", None, "seq"),
        P("dp", "seq"),
        P(("dp", "seq"), None),
    )
    return jax.shard_map(
        on_device,
        mesh=mesh,
        in_specs=placed,
        out_specs=(
            P(("dp", "seq"), None),
            P(("dp", "seq"), None),
            P(None, "dp"),
            P("dp", "seq"),
            P("dp", "seq"),
            P("dp", "seq"),
            P("dp", None),
            P(None, "dp"),
            P(),
            P(),
            P("dp", "seq"),
            P("dp", None, "seq"),
            P("dp", "seq"),
        ),
        check_vma=False,
    )
```

```python
import jax
import jax.numpy as jnp
from jax import lax
from jax.experimental import pallas as pl
from jax.experimental.pallas import tpu as pltpu
from jax.sharding import PartitionSpec as P

D = 1600
HEADS = 25
KV_HEADS = 5
HEAD = 64
INNER = 3200
SSM_HEAD = 64
STATE = 16
CONV = 4
FF = 5504
WINDOW = 1024
SSM_HEADS = 50

NORM_EPS = 1e-05
MASKED = -1e30
LOW = jnp.bfloat16
FULL = jnp.float32

SEQ = 4
GROUP_HEADS = HEADS // KV_HEADS
QW = GROUP_HEADS * HEAD
LOCAL_HEADS = 13
LOCAL_CH = LOCAL_HEADS * SSM_HEAD
CHUNK = 128
UNITS = FF // SEQ
UNITS_PAD = 1408
BCDT_PAD = 128
OUT_AT, O_AT, O5_AT, OUT_WIDTH = 0, 896, 1280, 1600
FIRST_HEAD = tuple((SSM_HEADS * s // 2 + 1) // 2 for s in range(SEQ))
HEAD_COUNT = tuple(b - a for a, b in zip(FIRST_HEAD, FIRST_HEAD[1:] + (SSM_HEADS,)))


def swap(value, axis, bit):
    return lax.ppermute(value, axis, [(i, i ^ bit) for i in range(lax.axis_size(axis))])


def place_kernel(count, index_ref, *refs):
    blocks, stacked, held, in_sems, out_sems = refs[:count], *refs[count:]
    loads = [
        pltpu.make_async_copy(block, held.at[i], in_sems.at[i]) for i, block in enumerate(blocks)
    ]
    stores = [
        pltpu.make_async_copy(held.at[i], stacked.at[index_ref[i]], out_sems.at[i])
        for i in range(count)
    ]
    for load in loads:
        load.start()
    for load, store in zip(loads, stores):
        load.wait()
        store.start()
    for store in stores:
        store.wait()


def place(blocks):
    count = len(blocks)
    block = blocks[0][1]
    anywhere = pl.BlockSpec(memory_space=pl.ANY)
    return pl.pallas_call(
        lambda *refs: place_kernel(count, *refs),
        out_shape=jax.ShapeDtypeStruct((count,) + block.shape, block.dtype),
        grid_spec=pltpu.PrefetchScalarGridSpec(
            num_scalar_prefetch=1,
            grid=(1,),
            in_specs=[anywhere] * count,
            out_specs=anywhere,
            scratch_shapes=[
                pltpu.VMEM((count,) + block.shape, block.dtype),
                pltpu.SemaphoreType.DMA((count,)),
                pltpu.SemaphoreType.DMA((count,)),
            ],
        ),
        compiler_params=pltpu.CompilerParams(vmem_limit_bytes=32 << 20),
        cost_estimate=pl.CostEstimate(
            flops=0, bytes_accessed=2 * count * block.size * block.dtype.itemsize, transcendentals=0
        ),
    )(jnp.stack([jnp.asarray(i, jnp.int32) for i, _ in blocks]), *[b for _, b in blocks])


def seq_order():
    me = lax.axis_index("seq")
    return [me, me ^ 1, me ^ 2, me ^ 3]


def seq_arrivals(block):
    far = swap(block, "seq", 2)
    return [block, swap(block, "seq", 1), far, swap(far, "seq", 1)]


def gather_seq(block):
    return place(list(zip(seq_order(), seq_arrivals(block))))


def scatter_begin(part):
    core = lax.axis_index("seq") % 2
    by_core = part.astype(LOW).reshape((2, 2, part.shape[0] // SEQ) + part.shape[1:])
    give = lax.dynamic_index_in_dim(by_core, 1 - core, 1, False)
    keep = lax.dynamic_index_in_dim(by_core, core, 1, False)
    return keep, swap(give, "seq", 1)


def scatter_far(keep, got):
    far = lax.axis_index("seq") // 2
    at = lambda a, i: lax.dynamic_index_in_dim(a, i, 0, False).astype(FULL)
    give_far = (at(keep, 1 - far) + at(got, 1 - far)).astype(LOW)
    return at(keep, far) + at(got, far), swap(give_far, "seq", 2)


def scatter_end(held, got_far):
    return held + got_far.astype(FULL)


def after(values, done):
    return lax.optimization_barrier((values, done))[0]


def line_place():
    me = lax.axis_index("dp")
    return lax.axis_size("dp") // 2, me // 2, lax.rem(me, 2)


def greet(line, z, x):
    barrier = pltpu.get_barrier_semaphore()

    def signal(target):
        pl.semaphore_signal(
            barrier, inc=1, device_id={"dp": target}, device_id_type=pl.DeviceIdType.MESH
        )

    signal(2 * z + 1 - x)
    pl.when(z > 0)(lambda: signal(2 * (z - 1) + x))
    pl.when(z < line - 1)(lambda: signal(2 * (z + 1) + x))
    pl.semaphore_wait(
        barrier, 1 + (z > 0).astype(jnp.int32) + (z < line - 1).astype(jnp.int32)
    )


def gather_kernel(count, line, *refs):
    packets, outs = refs[:count], refs[count : 2 * count]
    own_sem, up_sem, down_sem, line_sem, give_sem, got_sem = refs[2 * count :]
    _, z, x = line_place()
    greet(line, z, x)

    def copy(src, i, zb, send_sem, recv_sem, target):
        return pltpu.make_async_remote_copy(
            src_ref=src,
            dst_ref=outs[i].at[2 * zb + x],
            send_sem=send_sem.at[i, zb],
            recv_sem=recv_sem.at[i, zb],
            device_id={"dp": target},
            device_id_type=pl.DeviceIdType.MESH,
        )

    up_to = lambda src, i, zb: copy(src, i, zb, up_sem, line_sem, 2 * (z + 1) + x)
    down_to = lambda src, i, zb: copy(src, i, zb, down_sem, line_sem, 2 * (z - 1) + x)
    give = lambda src, i, zb: copy(src, i, zb, give_sem, got_sem, 2 * z + 1 - x)
    held = lambda i, zb: outs[i].at[2 * zb + x]
    own = lambda i: pltpu.make_async_copy(packets[i], held(i, z), own_sem.at[i])

    for turn in range(count + line - 1):
        for i in range(count):
            far = turn - i
            if far == 0:
                own(i).start()
                give(packets[i], i, z).start()
                pl.when(z < line - 1)(lambda: up_to(packets[i], i, z).start())
                pl.when(z > 0)(lambda: down_to(packets[i], i, z).start())
            elif 0 < far < line:

                @pl.when(z - far >= 0)
                def _():
                    zb = z - far
                    up_to(held(i, zb), i, zb).wait_recv()
                    pl.when(z < line - 1)(lambda: up_to(held(i, zb), i, zb).start())
                    give(held(i, zb), i, zb).start()

                @pl.when(z + far < line)
                def _():
                    zb = z + far
                    down_to(held(i, zb), i, zb).wait_recv()
                    pl.when(z > 0)(lambda: down_to(held(i, zb), i, zb).start())
                    give(held(i, zb), i, zb).start()

    for i in range(count):
        own(i).wait()
        for zb in range(line):
            give(held(i, zb), i, zb).wait()
            pl.when((zb <= z) & (z < line - 1))(lambda: up_to(held(i, zb), i, zb).wait_send())
            pl.when((zb >= z) & (z > 0))(lambda: down_to(held(i, zb), i, zb).wait_send())


def gather_dp(packets, collective_id):
    total = lax.axis_size("dp")
    if total != 8:
        return [lax.all_gather(packet, "dp", axis=0) for packet in packets]
    count, line = len(packets), total // 2
    sems = lambda *shape: pltpu.SemaphoreType.DMA(shape)
    return pl.pallas_call(
        lambda *refs: gather_kernel(count, line, *refs),
        out_shape=[jax.ShapeDtypeStruct((total,) + p.shape, p.dtype) for p in packets],
        in_specs=[pl.BlockSpec(memory_space=pltpu.VMEM)] * count,
        out_specs=[pl.BlockSpec(memory_space=pl.ANY)] * count,
        scratch_shapes=[sems(count)] + [sems(count, line) for _ in range(5)],
        compiler_params=pltpu.CompilerParams(
            collective_id=collective_id, has_side_effects=True, vmem_limit_bytes=32 << 20
        ),
        cost_estimate=pl.CostEstimate(
            flops=0,
            bytes_accessed=2 * total * sum(p.size * p.dtype.itemsize for p in packets),
            transcendentals=0,
        ),
    )(*packets)


def add_columns(total, parts):
    width = total.shape[-1]
    step = 128 if width % 256 else 256

    def columns(c):
        at = pl.ds(pl.multiple_of(c * step, step), step)
        total[:, at] = sum(part[:, at].astype(FULL) for part in parts).astype(total.dtype)

    pl.loop(0, width // step)(columns)
    if width % step:
        at = slice(width // step * step, width)
        total[:, at] = sum(part[:, at].astype(FULL) for part in parts).astype(total.dtype)


def scatter_kernel(count, line, *refs):
    parts, outs = refs[:count], refs[count : 2 * count]
    own_refs, near_refs, line_refs = (
        refs[2 * count : 3 * count],
        refs[3 * count : 4 * count],
        refs[4 * count : 5 * count],
    )
    load_sem, give_sem, got_sem, send_sem, line_sem = refs[5 * count :]
    _, z, x = line_place()
    greet(line, z, x)
    order = [t for pair in zip(range(line - 1, -1, -1), range(line)) for t in pair][:line]
    remote = lambda src, dst, send, recv, target: pltpu.make_async_remote_copy(
        src_ref=src,
        dst_ref=dst,
        send_sem=send,
        recv_sem=recv,
        device_id={"dp": target},
        device_id_type=pl.DeviceIdType.MESH,
    )
    give = lambda i, t: remote(
        parts[i].at[2 * t + 1 - x],
        near_refs[i].at[t],
        give_sem.at[i, t],
        got_sem.at[i, t],
        2 * z + 1 - x,
    )
    load = lambda i, t: pltpu.make_async_copy(
        parts[i].at[2 * t + x], own_refs[i].at[t], load_sem.at[i, t]
    )
    along = lambda i, t, slot, target: remote(
        own_refs[i].at[t], line_refs[i].at[slot], send_sem.at[i, t], line_sem.at[i, slot], target
    )
    for i in range(count):
        for t in order:
            load(i, t).start()
            give(i, t).start()
    for i in range(count):
        own, near, held = own_refs[i], near_refs[i], line_refs[i]
        for t in order:
            load(i, t).wait()
            give(i, t).wait_recv()

            @pl.when((t > z) & (z > 0) | (t < z) & (z < line - 1))
            def _():
                along(i, t, t, 0).wait_recv()
                add_columns(own.at[t], (own.at[t], near.at[t], held.at[t]))

            @pl.when((t > z) & (z == 0) | (t < z) & (z == line - 1))
            def _():
                add_columns(own.at[t], (own.at[t], near.at[t]))

            pl.when(t > z)(lambda: along(i, t, t, 2 * (z + 1) + x).start())
            pl.when(t == z - 1)(lambda: along(i, t, line, 2 * (z - 1) + x).start())
            pl.when(t < z - 1)(lambda: along(i, t, t, 2 * (z - 1) + x).start())
    for i in range(count):
        own, near, held = own_refs[i], near_refs[i], line_refs[i]
        pl.when(z > 0)(lambda: along(i, z, z, 0).wait_recv())
        pl.when(z < line - 1)(lambda: along(i, z, line, 0).wait_recv())
        for t in range(line):

            @pl.when(t == z)
            def _():
                terms = [own.at[t], near.at[t]]
                terms += [held.at[t]] if t > 0 else []
                terms += [held.at[line]] if t < line - 1 else []
                add_columns(outs[i], terms)

            pl.when(t != z)(lambda: along(i, t, t, 0).wait_send())
            give(i, t).wait_send()


def scatter_dp(parts, collective_id):
    total = lax.axis_size("dp")
    if total != 8:
        sums = [lax.psum_scatter(p, "dp", scatter_dimension=0) for p in parts]
        return [lax.optimization_barrier(p).astype(FULL) for p in sums]
    count, line = len(parts), total // 2
    sems = lambda *shape: pltpu.SemaphoreType.DMA(shape)
    return pl.pallas_call(
        lambda *refs: scatter_kernel(count, line, *refs),
        out_shape=[jax.ShapeDtypeStruct(p.shape[1:], FULL) for p in parts],
        in_specs=[pl.BlockSpec(memory_space=pl.ANY)] * count,
        out_specs=[pl.BlockSpec(memory_space=pltpu.VMEM)] * count,
        scratch_shapes=[pltpu.VMEM((line,) + p.shape[1:], p.dtype) for p in parts]
        + [pltpu.VMEM((line,) + p.shape[1:], p.dtype) for p in parts]
        + [pltpu.VMEM((line + 1,) + p.shape[1:], p.dtype) for p in parts]
        + [sems(count, line) for _ in range(4)]
        + [sems(count, line + 1)],
        compiler_params=pltpu.CompilerParams(
            collective_id=collective_id, has_side_effects=True, vmem_limit_bytes=56 << 20
        ),
        cost_estimate=pl.CostEstimate(
            flops=0, bytes_accessed=sum(p.size * 2 for p in parts), transcendentals=0
        ),
    )(*parts)


def gather_dp_apart(packet):
    return lax.all_gather(packet, "dp", axis=0, tiled=True)


def scatter_dp_apart(parts):
    summed = lax.psum_scatter(parts.astype(LOW), "dp", scatter_dimension=0, tiled=True)
    return lax.optimization_barrier(summed).astype(FULL)


def trade_halves(first, last):
    me = lax.axis_index("seq")
    one = lax.ppermute(jnp.where(me == 0, last, first), "seq", [(0, 1), (1, 2), (2, 0)])
    two = lax.ppermute(jnp.where(me == 3, first, last), "seq", [(1, 3), (2, 1), (3, 2)])
    return pick([first, one, one, two], me), pick([one, two, two, last], me)


def trade_back(x_part, z_part):
    me = lax.axis_index("seq")
    one = lax.ppermute(jnp.where(me == 0, z_part, x_part), "seq", [(1, 0), (2, 1), (0, 2)])
    two = lax.ppermute(jnp.where(me == 3, x_part, z_part), "seq", [(3, 1), (1, 2), (2, 3)])
    return pick([x_part, one, one, two], me), pick([one, two, two, z_part], me)


def mm(left, right):
    return jnp.dot(left, right, preferred_element_type=FULL)


def mm_nt(left, right):
    return lax.dot_general(left, right, (((1,), (1,)), ((), ())), preferred_element_type=FULL)


def mm_tn(left, right):
    return lax.dot_general(left, right, (((0,), (0,)), ((), ())), preferred_element_type=FULL)


def rms_norm(values, gain):
    return values * lax.rsqrt(jnp.mean(values * values, axis=-1, keepdims=True) + NORM_EPS) * gain


def join_tail(inputs_x, attn_o, ssm_o, gains):
    residual = inputs_x + 0.5 * (rms_norm(attn_o, gains[1]) + rms_norm(ssm_o, gains[2]))
    return (residual, rms_norm(residual, gains[3]))


STEP_AT = 2 * STATE
WIDE = 896
PAIRS = WIDE // 128
XZB = 1792


def dot_any(left, right, contract):
    return lax.dot_general(
        left, right, ((contract[:1], contract[1:]), ((), ())), preferred_element_type=FULL
    )


def low_dot(left, right, contract):
    return dot_any(left.astype(LOW), right.astype(LOW), contract)


def iota(shape, axis):
    return lax.broadcasted_iota(jnp.int32, shape, axis)


def pair_spread(values):
    rows = values.shape[0]
    low_half = iota((rows, 128), 1) < SSM_HEAD
    tiles = []
    for p in range(PAIRS):
        one = values[:, STEP_AT + 2 * p : STEP_AT + 2 * p + 1]
        two = values[:, STEP_AT + 2 * p + 1 : STEP_AT + 2 * p + 2]
        tiles.append(
            jnp.where(
                low_half,
                jnp.broadcast_to(one, (rows, 128)),
                jnp.broadcast_to(two, (rows, 128)),
            )
        )
    return jnp.concatenate(tiles, axis=1)


def halves(tile):
    low_half = iota(tile.shape, 1) < SSM_HEAD
    zero = jnp.zeros_like(tile)
    return jnp.concatenate([jnp.where(low_half, tile, zero), jnp.where(low_half, zero, tile)], axis=0)


def mamba_chunk(c, lengths_ref, xzb_ref, tail_ref, conv_ref, rate_ref, pad_ref):
    first_end = lengths_ref[0, 0]
    second_end = first_end + lengths_ref[0, 1]
    doc_of = lambda pos: (pos >= first_end).astype(jnp.int32) + (pos >= second_end).astype(jnp.int32)
    base = c * CHUNK
    square = (CHUNK, CHUNK)
    row, lane = iota(square, 0), iota(square, 1)
    doc_row = doc_of(base + row)
    doc_lane = doc_of(base + lane)
    before = jnp.where(c > 0, doc_of(base - 1), -1)
    end = doc_of(base + CHUNK - 1)
    causal = (row >= lane) & (doc_row == doc_lane)
    channel = iota((CHUNK, WIDE), 1) < LOCAL_CH

    raw = jnp.where(channel, xzb_ref[:, :WIDE], 0.0).astype(LOW).astype(FULL)
    gate = pltpu.roll(xzb_ref[:, LOCAL_CH - 64 :], XZB - LOCAL_CH, 1)[:, :WIDE]
    gate = jnp.where(channel, gate, 0.0)
    pad_ref[0:8] = tail_ref[:, :WIDE].astype(LOW).astype(FULL)
    pad_ref[8 : 8 + CHUNK] = raw
    taps = []
    pos = base + iota((CHUNK, 1), 0)
    conv = jnp.zeros((CHUNK, WIDE), FULL)
    for k in range(CONV):
        back = CONV - 1 - k
        same = (doc_of(pos) == doc_of(pos - back)) & (pos >= back)
        shifted = jnp.where(same, pad_ref[8 - back : 8 - back + CHUNK], 0.0)
        taps.append(shifted)
        conv = conv + conv_ref[k : k + 1] * shifted
    conv_sig = jax.nn.sigmoid(conv)
    act = conv * conv_sig

    bc = xzb_ref[:, 2 * LOCAL_CH :]
    b_in = jnp.where(lane < STATE, bc, 0.0)
    c_at = jnp.where((lane >= STATE) & (lane < 2 * STATE), bc, 0.0)
    c_in = pltpu.roll(c_at, CHUNK - STATE, 1)
    step = jnp.maximum(bc, 0.0) + jnp.log(1.0 + jnp.exp(-jnp.abs(bc)))
    lower = (row >= lane).astype(FULL)
    log = lax.dot_general(
        lower,
        -step * rate_ref[0:1],
        (((1,), (0,)), ((), ())),
        precision=lax.Precision.HIGHEST,
        preferred_element_type=FULL,
    )
    last = log[CHUNK - 1 : CHUNK]
    ends = jnp.where(doc_row == end, jnp.exp(last - log), 0.0)
    reach = jnp.where(doc_row == before, jnp.exp(log), 0.0)
    carry = jnp.where(end == before, jnp.exp(last), 0.0)
    gram = low_dot(c_in, b_in, (1, 1))
    log_t = log.T

    def decays(h):
        gap = log[:, STEP_AT + h : STEP_AT + h + 1] - log_t[STEP_AT + h : STEP_AT + h + 1]
        return jnp.exp(jnp.where(causal, gap, MASKED))

    step_wide = pair_spread(step)
    return dict(
        row=row, lane=lane, pos=pos, doc_of=doc_of, gate=gate, taps=taps, conv=conv, conv_sig=conv_sig,
        act=act, bc=bc, b_in=b_in, c_in=c_in, c_at=c_at, step=step, ends=ends, reach=reach,
        carry=carry, gram=gram, decays=decays, step_wide=step_wide, moved=act * step_wide,
    )


def mamba_forward_kernel(
    lengths_ref, xzb_ref, tail_ref, conv_ref, rate_ref, skip_ref, gated_ref, read_ref, states_ref, pad_ref, state_ref
):
    c = pl.program_id(0)

    @pl.when(c == 0)
    def _():
        state_ref[...] = jnp.zeros_like(state_ref)

    v = mamba_chunk(c, lengths_ref, xzb_ref, tail_ref, conv_ref, rate_ref, pad_ref)
    states_ref[0] = state_ref[STATE : 2 * STATE]
    moved = v["moved"]
    from_state = low_dot(v["c_at"], state_ref[...], (1, 0)) * pair_spread(v["reach"])
    tiles = []
    for p in range(PAIRS):
        mixing = jnp.concatenate(
            [(v["decays"](2 * p + j) * v["gram"]).astype(LOW) for j in range(2)], axis=1
        )
        tiles.append(dot_any(mixing, halves(moved[:, 128 * p : 128 * p + 128].astype(LOW)), (1, 0)))
    read = jnp.concatenate(tiles, axis=1) + from_state + skip_ref[0:1] * v["act"]
    read_ref[...] = read.astype(LOW)
    gated_ref[...] = (read * v["gate"] * jax.nn.sigmoid(v["gate"])).astype(LOW)
    added = low_dot(v["b_in"], moved * pair_spread(v["ends"]), (0, 0))[:STATE]
    state_ref[STATE : 2 * STATE] = pair_spread(v["carry"]) * state_ref[STATE : 2 * STATE] + added


def mamba_backward_kernel(
    lengths_ref, xzb_ref, tail_ref, conv_ref, rate_ref, skip_ref, states_ref, read_ref, d_gated_ref,
    d_xzb_ref, d_chan_ref, d_rate_ref, pad_ref, state_ref, d_state_ref, d_pad_ref,
):
    g = pl.program_id(0)
    c = pl.num_programs(0) - 1 - g

    @pl.when(g == 0)
    def _():
        state_ref[...] = jnp.zeros_like(state_ref)
        d_state_ref[...] = jnp.zeros_like(d_state_ref)
        d_pad_ref[...] = jnp.zeros_like(d_pad_ref)
        d_chan_ref[...] = jnp.zeros_like(d_chan_ref)
        d_rate_ref[...] = jnp.zeros_like(d_rate_ref)

    v = mamba_chunk(c, lengths_ref, xzb_ref, tail_ref, conv_ref, rate_ref, pad_ref)
    row, lane, act, moved, gate = v["row"], v["lane"], v["act"], v["moved"], v["gate"]
    state_ref[STATE : 2 * STATE] = states_ref[0]
    by_head = (iota((WIDE, 128), 0) // SSM_HEAD + STEP_AT == iota((WIDE, 128), 1)).astype(LOW)
    head_sum = lambda wide: dot_any(wide.astype(LOW), by_head, (1, 0))

    d_gated = d_gated_ref[...].astype(FULL)
    gate_sig = jax.nn.sigmoid(gate)
    d_read = d_gated * gate * gate_sig
    d_gate = d_gated * read_ref[...].astype(FULL) * gate_sig * (1.0 + gate * (1.0 - gate_sig))
    d_chan_ref[CONV : CONV + 1] += jnp.sum(d_read * act, axis=0, keepdims=True)
    d_act = skip_ref[0:1] * d_read

    d_log = jnp.zeros_like(v["gram"])
    d_log_t = jnp.zeros_like(v["gram"])
    d_gram = jnp.zeros_like(v["gram"])
    tiles = []
    for p in range(PAIRS):
        at = slice(128 * p, 128 * p + 128)
        d_pair = halves(d_read[:, at].astype(LOW))
        d_mixing = dot_any(d_pair, moved[:, at].astype(LOW), (1, 1))
        mixings = []
        for j in range(2):
            h = 2 * p + j
            decay = v["decays"](h)
            mixing = decay * v["gram"]
            d_one = d_mixing[CHUNK * j : CHUNK * (j + 1)]
            d_gram = d_gram + d_one * decay
            d_gap = d_one * mixing
            mixings.append(mixing.astype(LOW))
            d_log = d_log + jnp.where(lane == STEP_AT + h, jnp.sum(d_gap, axis=1, keepdims=True), 0.0)
            d_log_t = d_log_t + jnp.where(row == STEP_AT + h, jnp.sum(d_gap, axis=0, keepdims=True), 0.0)
        tiles.append(dot_any(jnp.concatenate(mixings, axis=0), d_pair, (0, 0)))
    d_moved = jnp.concatenate(tiles, axis=1)
    d_log = d_log - d_log_t.T

    d_product = d_read * pair_spread(v["reach"])
    state_low = state_ref[...].astype(LOW)
    product = dot_any(v["c_at"].astype(LOW), state_low, (1, 0))
    d_log = d_log + head_sum(d_product * product)
    d_c = low_dot(d_product, state_low, (1, 1)) + low_dot(d_gram, pltpu.roll(v["b_in"], STATE, 1), (1, 0))
    d_state_in = low_dot(v["c_at"], d_product, (0, 0))[STATE : 2 * STATE]

    d_state = d_state_ref[...]
    d_state_low = d_state.astype(LOW)
    ends_wide = pair_spread(v["ends"])
    d_put = dot_any(v["b_in"].astype(LOW), d_state_low, (1, 0)) * ends_wide
    d_b = low_dot(moved * ends_wide, d_state_low, (1, 1)) + low_dot(d_gram, v["c_in"], (0, 0))
    d_moved = d_moved + d_put
    d_ends = head_sum(d_put * moved)
    carry_wide = pair_spread(v["carry"])
    d_carry = head_sum(
        jnp.broadcast_to(
            jnp.sum(d_state[:STATE] * states_ref[0], axis=0, keepdims=True) * carry_wide, (16, WIDE)
        )
    )[0:1]
    d_last = jnp.sum(d_ends, axis=0, keepdims=True) + d_carry
    d_log = d_log - d_ends + jnp.where(row == CHUNK - 1, d_last, 0.0)
    d_state_ref[:STATE] = d_state_in + carry_wide * d_state[:STATE]

    d_act = d_act + d_moved * v["step_wide"]
    d_rate_step = lax.dot_general(
        (row >= lane).astype(FULL),
        d_log,
        (((0,), (0,)), ((), ())),
        precision=lax.Precision.HIGHEST,
        preferred_element_type=FULL,
    )
    d_step = head_sum(d_moved * act) - rate_ref[0:1] * d_rate_step
    d_rate_ref[0:1] += jnp.sum(-v["step"] * d_rate_step, axis=0, keepdims=True)
    is_step = (lane >= STEP_AT) & (lane < STEP_AT + LOCAL_HEADS)
    d_bc = d_b + d_c + jnp.where(is_step, d_step * jax.nn.sigmoid(v["bc"]), 0.0)

    d_conv = d_act * v["conv_sig"] * (1.0 + v["conv"] * (1.0 - v["conv_sig"]))
    d_pad_ref[0:CHUNK] = d_conv
    d_raw = jnp.zeros_like(d_conv)
    for k in range(CONV):
        ahead = CONV - 1 - k
        d_chan_ref[k : k + 1] += jnp.sum(d_conv * v["taps"][k], axis=0, keepdims=True)
        same = v["doc_of"](v["pos"]) == v["doc_of"](v["pos"] + ahead)
        d_raw = d_raw + conv_ref[k : k + 1] * jnp.where(same, d_pad_ref[ahead : ahead + CHUNK], 0.0)
    d_pad_ref[CHUNK : CHUNK + 8] = d_conv[0:8]

    moved_gate = pltpu.roll(jnp.concatenate([d_gate, jnp.zeros_like(row).astype(FULL)], axis=1), 64, 1)
    d_xzb_ref[:, : LOCAL_CH - 64] = d_raw[:, : LOCAL_CH - 64].astype(LOW)
    d_xzb_ref[:, LOCAL_CH - 64 : LOCAL_CH + 64] = (
        d_raw[:, LOCAL_CH - 64 :] + moved_gate[:, :128]
    ).astype(LOW)
    d_xzb_ref[:, LOCAL_CH + 64 : 2 * LOCAL_CH] = moved_gate[:, 128:WIDE].astype(LOW)
    d_xzb_ref[:, 2 * LOCAL_CH :] = d_bc.astype(LOW)


def mamba_specs(chunk_of):
    tail = lambda g: (jnp.maximum(chunk_of(g) * (CHUNK // 8) - 1, 0), 0)
    fixed = lambda shape: pl.BlockSpec(shape, lambda g: (0,) * len(shape))
    return [
        pl.BlockSpec(memory_space=pltpu.SMEM),
        pl.BlockSpec((CHUNK, XZB), lambda g: (chunk_of(g), 0)),
        pl.BlockSpec((8, XZB), tail),
        fixed((8, WIDE)),
        fixed((8, 128)),
        fixed((8, WIDE)),
    ]


def mamba_forward(lengths, xzb, conv_rows, rate_row, skip_row):
    total = xzb.shape[0]
    chunks = total // CHUNK
    by_chunk = lambda width: pl.BlockSpec((CHUNK, width), lambda g: (g, 0))
    return pl.pallas_call(
        mamba_forward_kernel,
        grid=(chunks,),
        in_specs=mamba_specs(lambda g: g),
        out_specs=[by_chunk(WIDE), by_chunk(WIDE), pl.BlockSpec((1, STATE, WIDE), lambda g: (g, 0, 0))],
        out_shape=[
            jax.ShapeDtypeStruct((total, WIDE), LOW),
            jax.ShapeDtypeStruct((total, WIDE), LOW),
            jax.ShapeDtypeStruct((chunks, STATE, WIDE), FULL),
        ],
        scratch_shapes=[pltpu.VMEM((8 + CHUNK, WIDE), FULL), pltpu.VMEM((CHUNK, WIDE), FULL)],
        compiler_params=pltpu.CompilerParams(vmem_limit_bytes=32 << 20),
        cost_estimate=pl.CostEstimate(flops=2 * 10**9, bytes_accessed=16 << 20, transcendentals=10**7),
    )(lengths, xzb, xzb, conv_rows, rate_row, skip_row)


def mamba_backward(lengths, xzb, conv_rows, rate_row, skip_row, states, read, d_gated):
    total = xzb.shape[0]
    chunks = total // CHUNK
    chunk_of = lambda g: chunks - 1 - g
    by_chunk = lambda width: pl.BlockSpec((CHUNK, width), lambda g: (chunk_of(g), 0))
    return pl.pallas_call(
        mamba_backward_kernel,
        grid=(chunks,),
        in_specs=mamba_specs(chunk_of)
        + [pl.BlockSpec((1, STATE, WIDE), lambda g: (chunk_of(g), 0, 0)), by_chunk(WIDE), by_chunk(WIDE)],
        out_specs=[
            by_chunk(XZB),
            pl.BlockSpec((8, WIDE), lambda g: (0, 0)),
            pl.BlockSpec((8, 128), lambda g: (0, 0)),
        ],
        out_shape=[
            jax.ShapeDtypeStruct((total, XZB), LOW),
            jax.ShapeDtypeStruct((8, WIDE), FULL),
            jax.ShapeDtypeStruct((8, 128), FULL),
        ],
        scratch_shapes=[
            pltpu.VMEM((8 + CHUNK, WIDE), FULL),
            pltpu.VMEM((CHUNK, WIDE), FULL),
            pltpu.VMEM((CHUNK, WIDE), FULL),
            pltpu.VMEM((8 + CHUNK, WIDE), FULL),
        ],
        compiler_params=pltpu.CompilerParams(vmem_limit_bytes=32 << 20),
        cost_estimate=pl.CostEstimate(flops=5 * 10**9, bytes_accessed=24 << 20, transcendentals=10**7),
    )(lengths, xzb, xzb, conv_rows, rate_row, skip_row, states, read, d_gated)


def head_under(h, at, value):
    row, lane = iota((QW, 128), 0), iota((QW, 128), 1)
    inside = (lane >= at) & (lane < at + HEAD) & (row == h * HEAD + lane - at)
    return jnp.where(inside, value, 0.0).astype(LOW)


def row_block(t):
    return jnp.where(t < SEQ, t, lax.axis_index("seq"))


def allowed_keys(lengths_ref, block, rows, extent):
    first_end = lengths_ref[0, 0]
    second_end = first_end + lengths_ref[0, 1]
    row = block * rows + iota((rows, 1), 0)
    start = jnp.where(row >= second_end, second_end, jnp.where(row >= first_end, first_end, 0))
    least = jnp.maximum(start, row - (WINDOW - 1))
    key = iota((rows, extent), 1)
    return (key >= least) & (key <= row)


def for_extent(block, rows, run):
    for e in range(SEQ):
        pl.when(block == e)(lambda e=e: run((e + 1) * rows))


def attention_forward_kernel(lengths_ref, q_ref, kv_ref, out_ref, log_ref):
    t, h = pl.program_id(0), pl.program_id(1)
    rows = q_ref.shape[0]
    block = row_block(t)

    def run(extent):
        q = dot_any(q_ref[...], head_under(h, 0, HEAD ** (-0.5)), (1, 0)).astype(LOW)
        kv = kv_ref[:extent]
        scores = dot_any(q, kv, (1, 1))
        scores = jnp.where(allowed_keys(lengths_ref, block, rows, extent), scores, MASKED)
        top = jnp.max(scores, axis=1, keepdims=True)
        expos = jnp.exp(scores - top)
        denom = jnp.sum(expos, axis=1, keepdims=True)
        mixed = dot_any((expos * (1.0 / denom)).astype(LOW), kv, (1, 0)).astype(LOW)
        out = dot_any(mixed, head_under(h, HEAD, 1.0), (1, 1)).astype(LOW)
        log = jnp.where(iota((rows, 128), 1) == h, top + jnp.log(denom), 0.0)

        @pl.when(h == 0)
        def _():
            out_ref[...] = out
            log_ref[...] = log

        @pl.when(h > 0)
        def _():
            out_ref[...] += out
            log_ref[...] += log

    for_extent(block, rows, run)


def attention_backward_kernel(
    lengths_ref, q_ref, kv_ref, out_ref, log_ref, d_out_ref, d_q_ref, d_kv_ref, sum_ref
):
    t, h = pl.program_id(0), pl.program_id(1)
    rows = q_ref.shape[0]
    block = row_block(t)

    @pl.when((h == 0) & ((t == 0) | (t == SEQ)))
    def _():
        sum_ref[...] = jnp.zeros_like(sum_ref)

    def run(extent):
        under_q = head_under(h, 0, HEAD ** (-0.5))
        q = dot_any(q_ref[...], under_q, (1, 0)).astype(LOW)
        d_out = dot_any(d_out_ref[...], head_under(h, HEAD, 1.0), (1, 0)).astype(LOW)
        log = jnp.sum(jnp.where(iota((rows, 128), 1) == h, log_ref[...], 0.0), axis=1, keepdims=True)
        own = iota((rows, QW), 1) // HEAD == h
        product = d_out_ref[...].astype(FULL) * out_ref[...].astype(FULL)
        d_total = jnp.sum(jnp.where(own, product, 0.0), axis=1, keepdims=True)
        kv = kv_ref[:extent]
        scores = dot_any(q, kv, (1, 1))
        allowed = allowed_keys(lengths_ref, block, rows, extent)
        probs = jnp.exp(jnp.where(allowed, scores - log, MASKED))
        d_probs = dot_any(d_out, kv, (1, 1))
        d_scores = (probs * (d_probs - d_total)).astype(LOW)
        sum_ref[:extent] += dot_any(probs.astype(LOW), d_out, (0, 0)) + dot_any(d_scores, q, (0, 0))
        d_q = dot_any(dot_any(d_scores, kv, (1, 0)).astype(LOW), under_q, (1, 1)).astype(LOW)

        @pl.when(h == 0)
        def _():
            d_q_ref[...] = d_q

        @pl.when(h > 0)
        def _():
            d_q_ref[...] += d_q

    for_extent(block, rows, run)

    @pl.when((h == GROUP_HEADS - 1) & (t >= SEQ - 1))
    def _():
        d_kv_ref[...] = sum_ref[...].astype(LOW)


def attention_specs(rows, group):
    by_step = lambda width: pl.BlockSpec((rows, width), lambda t, h: (t, 0))
    kv_block = pl.BlockSpec((group, 128), lambda t, h: (0, t // SEQ))
    return by_step, kv_block


def attention_forward(lengths, queries, kv, rows):
    by_step, kv_block = attention_specs(rows, kv.shape[0])
    return pl.pallas_call(
        attention_forward_kernel,
        grid=(SEQ + 1, GROUP_HEADS),
        in_specs=[pl.BlockSpec(memory_space=pltpu.SMEM), by_step(QW), kv_block],
        out_specs=[by_step(QW), by_step(128)],
        out_shape=[
            jax.ShapeDtypeStruct(queries.shape, LOW),
            jax.ShapeDtypeStruct((queries.shape[0], 128), FULL),
        ],
        compiler_params=pltpu.CompilerParams(vmem_limit_bytes=32 << 20),
        cost_estimate=pl.CostEstimate(flops=3 * 10**9, bytes_accessed=4 << 20, transcendentals=8 * 10**6),
    )(lengths, queries, kv)


def attention_backward(lengths, queries, kv, out, logs, d_out, rows):
    group = kv.shape[0]
    by_step, kv_block = attention_specs(rows, group)
    return pl.pallas_call(
        attention_backward_kernel,
        grid=(SEQ + 1, GROUP_HEADS),
        in_specs=[pl.BlockSpec(memory_space=pltpu.SMEM), by_step(QW), kv_block]
        + [by_step(QW), by_step(128), by_step(QW)],
        out_specs=[by_step(QW), kv_block],
        out_shape=[jax.ShapeDtypeStruct(queries.shape, LOW), jax.ShapeDtypeStruct(kv.shape, LOW)],
        scratch_shapes=[pltpu.VMEM((group, 128), FULL)],
        compiler_params=pltpu.CompilerParams(vmem_limit_bytes=32 << 20),
        cost_estimate=pl.CostEstimate(flops=8 * 10**9, bytes_accessed=8 << 20, transcendentals=8 * 10**6),
    )(lengths, queries, kv, out, logs, d_out)


def pick(options, seq_index):
    return lax.select_n(seq_index, *options)


def own_cut(values, seq_index, axis, unit):
    cuts = []
    for first, count in zip(FIRST_HEAD, HEAD_COUNT):
        cut = lax.slice_in_dim(values, first * unit, (first + count) * unit, axis=axis)
        pads = [(0, 0)] * values.ndim
        pads[axis] = (0, (LOCAL_HEADS - count) * unit)
        cuts.append(jnp.pad(cut, pads))
    return pick(cuts, seq_index)


def own_spread(values, seq_index, unit):
    spreads = []
    for first, count in zip(FIRST_HEAD, HEAD_COUNT):
        pads = [(0, 0)] * (values.ndim - 1) + [(first * unit, (SSM_HEADS - first - count) * unit)]
        spreads.append(jnp.pad(values[..., : count * unit], pads))
    return pick(spreads, seq_index)


def channel_cut(wide, seq_index, axis):
    return own_cut(wide, seq_index, axis, SSM_HEAD)


def bcdt_cut(w_bcdt, seq_index):
    first = pick([jnp.int32(h) for h in FIRST_HEAD], seq_index)
    count = pick([jnp.int32(c) for c in HEAD_COUNT], seq_index)
    source = jnp.arange(w_bcdt.shape[1], dtype=jnp.int32)[:, None]
    target = jnp.arange(BCDT_PAD, dtype=jnp.int32)[None]
    shared = (target < 2 * STATE) & (source == target)
    steps = (target >= 2 * STATE) & (target < 2 * STATE + count) & (source == target + first)
    return mm(w_bcdt, (shared | steps).astype(LOW)).astype(LOW)


def wide_of(arrivals):
    me = lax.axis_index("seq")
    return jnp.concatenate([pick(arrivals, me ^ j) for j in range(SEQ)], axis=1)


def on_device(
    tokens_in,
    doc_lengths,
    norm_gains,
    w_qkv,
    w_o,
    w_xz,
    w_bcdt,
    conv_w,
    ssm_rate,
    ssm_skip,
    w_out,
    w_gate_up,
    w_down,
    cotangent,
):
    rows = tokens_in.shape[0]
    group = rows * SEQ
    s = lax.axis_index("seq")
    dp_index = lax.axis_index("dp")
    dp_total = lax.axis_size("dp")
    block_rows = w_qkv.shape[0]
    kv_width = KV_HEADS * HEAD
    lengths = doc_lengths[0]
    live = (jnp.arange(rows, dtype=jnp.int32) + s * rows < lengths[0] + lengths[1]).astype(FULL)[:, None]

    gains_block = norm_gains.shape[1]
    conv_block = conv_w.shape[1]
    width = -(-max(conv_block, gains_block) // 128) * 128
    small = jnp.concatenate(
        [
            jnp.pad(conv_w, ((0, 4), (0, width - conv_block))),
            jnp.pad(norm_gains, ((0, 4), (0, width - gains_block))),
        ]
    )
    out_block = w_out.shape[0]
    out_packet = jnp.concatenate([w_o, w_out], axis=0)
    qkv_shards = seq_arrivals(w_qkv)
    x_part, z_part = trade_halves(
        w_xz[:, :LOCAL_CH], jnp.pad(w_xz[:, LOCAL_CH:], ((0, 0), (0, 2 * LOCAL_CH - w_xz.shape[1])))
    )
    token_blocks = seq_arrivals(tokens_in)
    small, out_cols = gather_dp([small, out_packet], 0)
    small, out_cols, qkv_shards, x_part, z_part, token_blocks = lax.optimization_barrier(
        (small, out_cols, qkv_shards, x_part, z_part, token_blocks)
    )
    full_conv = small[:, :4, :conv_block].transpose(1, 0, 2).reshape(4, INNER).astype(FULL)
    gains = small[:, 8:12, :gains_block].transpose(1, 0, 2).reshape(4, D).astype(FULL)
    tokens_group = place(list(zip(seq_order(), token_blocks))).reshape(group, D)
    normed = rms_norm(tokens_group.astype(FULL), gains[0]).astype(LOW)
    qkv_wide = wide_of(qkv_shards)
    q_at = lambda h: lax.dynamic_slice_in_dim(qkv_wide, h * QW, QW, 1)
    kv_at = lambda h: [
        lax.dynamic_slice_in_dim(qkv_wide, D + h * HEAD, HEAD, 1),
        lax.dynamic_slice_in_dim(qkv_wide, D + kv_width + h * HEAD, HEAD, 1),
    ]
    qkv_packet = jnp.concatenate(kv_at(s) + kv_at(KV_HEADS - 1) + [q_at(s), q_at(KV_HEADS - 1)], axis=1)
    xz_packet = jnp.concatenate([x_part, z_part, bcdt_cut(w_bcdt, s)], axis=1)
    full_qkv, full_xz = gather_dp([qkv_packet, xz_packet], 1)
    gate_up_packet = jnp.pad(w_gate_up, ((0, 0), (0, 0), (0, UNITS_PAD - UNITS))).reshape(block_rows, -1)
    down_packet = jnp.pad(w_down, ((0, 0), (0, UNITS_PAD - UNITS)))
    full_qkv, full_xz, out_cols, gate_up_packet, down_packet = lax.optimization_barrier(
        (full_qkv, full_xz, out_cols, gate_up_packet, down_packet)
    )
    full_qkv = full_qkv.reshape(D, -1)
    full_xz = full_xz.reshape(D, -1)
    full_gate_up = gather_dp_apart(gate_up_packet)
    full_down = gather_dp_apart(down_packet)

    d_total = cotangent.astype(FULL) * live
    d_ffn_group = gather_seq(d_total.astype(LOW)).reshape(group, D)

    own = lambda a: lax.dynamic_slice_in_dim(a, s * rows, rows, 0)
    normed_own = own(normed)
    kvq = mm(normed, full_qkv[:, : 256 + QW]).astype(LOW)
    q_last = mm(normed_own, full_qkv[:, 256 + QW :]).astype(LOW)
    queries = jnp.concatenate([kvq[:, 256:], q_last])
    kv = kvq[:, :256]
    attended, logs = attention_forward(doc_lengths, queries, kv, rows)
    o_cols = out_cols[:, :block_rows].reshape(D, -1)
    mamba_cols = out_cols[:, block_rows:].reshape(INNER, -1)

    def rows_for(peer):
        cut = channel_cut(mamba_cols, peer, 0)
        heads = lax.dynamic_slice_in_dim(o_cols, peer * QW, QW, 0)
        spare = lambda n: jnp.zeros((n, cut.shape[1]), LOW)
        return jnp.concatenate(
            [cut, spare(O_AT - LOCAL_CH), heads, spare(O5_AT - O_AT - QW), o_cols[(KV_HEADS - 1) * QW :]]
        )

    out_pieces = [rows_for(s)] + [swap(rows_for(s ^ bit), "seq", bit) for bit in (1, 2, 3)]
    out_rows = lax.optimization_barrier(wide_of(after(out_pieces, attended)))
    w_out_rows = out_rows[:WIDE]
    w_o_rows = out_rows[O_AT : O_AT + QW]
    w_o5_rows = out_rows[O5_AT:]
    attn_part = mm(attended[:group], w_o_rows).astype(LOW)
    normed_now, attn_part = lax.optimization_barrier((normed, attn_part))
    attn_keep, attn_got = scatter_begin(attn_part)

    xzb = mm(normed_now, full_xz)
    attn_held, attn_far = scatter_far(attn_keep, after(attn_got, xzb))
    conv_rows = jnp.pad(channel_cut(full_conv, s, 1), ((0, 4), (0, WIDE - LOCAL_CH)))
    rate_row = jnp.pad(own_cut(ssm_rate, s, 0, 1), (STEP_AT, 128 - STEP_AT - LOCAL_HEADS))
    rate_row = jnp.broadcast_to(rate_row, (8, 128))
    skip_row = jnp.pad(jnp.repeat(own_cut(ssm_skip, s, 0, 1), SSM_HEAD), (0, WIDE - LOCAL_CH))
    skip_row = jnp.broadcast_to(skip_row, (8, WIDE))
    mamba_in = (doc_lengths, xzb, conv_rows, rate_row, skip_row)
    gated, read, states = mamba_forward(*mamba_in)
    ssm_held, ssm_far = scatter_far(*scatter_begin(mm(gated, w_out_rows)))
    attn_o = scatter_end(attn_held, after(attn_far, gated)) + mm(attended[group:], w_o5_rows)
    ssm_o = scatter_end(ssm_held, ssm_far)

    inputs_x = tokens_in.astype(FULL)
    (residual, normed_two), pull_join = jax.vjp(join_tail, inputs_x, attn_o, ssm_o, gains)
    normed_two = gather_seq(normed_two.astype(LOW)).reshape(group, D)
    gate_up = mm(normed_two, full_gate_up)
    ffn_gate, ffn_up = gate_up[:, :UNITS_PAD], gate_up[:, UNITS_PAD:]
    ffn_act = (jax.nn.silu(ffn_gate) * ffn_up).astype(LOW)

    d_act = mm(d_ffn_group, full_down)
    sig = jax.nn.sigmoid(ffn_gate)
    d_gate = d_act * ffn_up * (sig * (1.0 + ffn_gate * (1.0 - sig)))
    d_up = d_act * ffn_gate * sig
    d_gate_up = jnp.concatenate([d_gate.astype(LOW), d_up.astype(LOW)], axis=1)
    two_keep, two_got = scatter_begin(mm_nt(d_gate_up, full_gate_up))
    grad_down_part = mm_tn(d_ffn_group, ffn_act).astype(LOW)
    two_held, two_far = scatter_far(two_keep, after(two_got, grad_down_part))
    grad_gate_up_part = mm_tn(normed_two, d_gate_up).astype(LOW)
    d_normed_two = scatter_end(two_held, after(two_far, grad_gate_up_part))
    grad_gate_up_sum = scatter_dp_apart(grad_gate_up_part)
    grad_down_sum = scatter_dp_apart(grad_down_part)
    grad_gate_up = grad_gate_up_sum.reshape(block_rows, 2, UNITS_PAD)[:, :, :UNITS]
    grad_down = grad_down_sum[:, :UNITS]

    d_x_tail, d_attn_o, d_ssm_o, d_gains = pull_join((d_total, d_normed_two))
    ssm_arrivals = seq_arrivals(d_ssm_o.astype(LOW))
    ffn_part = mm_nt(ffn_act, full_down).astype(LOW)
    ssm_arrivals = after(ssm_arrivals, ffn_part)
    d_attn_own = after(d_attn_o.astype(LOW), ssm_arrivals[2])
    attn_arrivals = seq_arrivals(d_attn_own)
    d_ssm = place(list(zip(seq_order(), ssm_arrivals))).reshape(group, D)
    d_gated = mm_nt(d_ssm, w_out_rows).astype(LOW)

    def send_columns(grad):
        width = D // SEQ
        blocks = [grad[:, width * j : width * (j + 1)] for j in range(SEQ)]
        return [pick(blocks, s)] + [swap(pick(blocks, s ^ bit), "seq", bit) for bit in (1, 2, 3)]

    mamba_pieces = send_columns(mm_tn(gated, d_ssm).astype(LOW))
    d_xzb, d_chan, d_rate = mamba_backward(*mamba_in, states, read, d_gated)
    mamba_pieces, attn_arrivals = after((mamba_pieces, attn_arrivals), d_xzb)
    arrived = place(list(zip(seq_order(), mamba_pieces)))
    grad_out = scatter_dp_apart(
        jnp.concatenate([arrived[j, : HEAD_COUNT[j] * SSM_HEAD] for j in range(SEQ)])
    )

    d_attn = place(list(zip(seq_order(), attn_arrivals))).reshape(group, D)
    d_attended = jnp.concatenate([mm_nt(d_attn, w_o_rows), mm_nt(d_attn_own, w_o5_rows)]).astype(LOW)
    head_pieces = send_columns(
        jnp.concatenate([mm_tn(attended[:group], d_attn), mm_tn(attended[group:], d_attn_own)]).astype(LOW)
    )
    ffn_held, ffn_far = scatter_far(*scatter_begin(ffn_part))
    ffn_own = scatter_end(ffn_held, after(ffn_far, d_xzb))
    mixed_out = ((residual + ffn_own) * live).astype(LOW)
    d_conv = d_chan[:CONV, :LOCAL_CH]
    d_skip = jnp.sum(d_chan[CONV, :LOCAL_CH].reshape(LOCAL_HEADS, SSM_HEAD), axis=1)
    d_rate = d_rate[0, STEP_AT : STEP_AT + LOCAL_HEADS]
    grad_xz_part = mm_tn(normed, d_xzb).astype(LOW).reshape(dp_total, block_rows, -1)

    d_queries, d_kv = attention_backward(doc_lengths, queries, kv, attended, logs, d_attended, rows)
    arrived = place(list(zip(seq_order(), after(head_pieces, d_queries))))
    grad_o_part = jnp.concatenate(
        [arrived[j, :QW] for j in range(SEQ)] + [jnp.sum(arrived[:, QW:].astype(FULL), axis=0).astype(LOW)]
    ).reshape(dp_total, block_rows, -1)
    d_kvq = jnp.concatenate([d_kv, d_queries[:group]], axis=1)
    d_q_last = d_queries[group:]
    grad_qkv_part = jnp.concatenate(
        [mm_tn(normed, d_kvq).astype(LOW), mm_tn(normed_own, d_q_last).astype(LOW)], axis=1
    ).reshape(dp_total, block_rows, -1)
    d_normed_part = mm_nt(d_xzb, full_xz) + mm_nt(d_kvq, full_qkv[:, : 256 + QW])
    d_normed_own = mm_nt(d_q_last, full_qkv[:, 256 + QW :])

    tokens_wide = tokens_group.astype(FULL)
    unit = tokens_wide * lax.rsqrt(jnp.mean(tokens_wide * tokens_wide, axis=-1, keepdims=True) + NORM_EPS)
    d_gain_first = jnp.sum(d_normed_part * unit, axis=0) + jnp.sum(d_normed_own * own(unit), axis=0)
    d_gains = d_gains.at[0].add(d_gain_first)
    by_dp = lambda a: a.reshape(a.shape[0], dp_total, -1).transpose(1, 0, 2)
    d_heads = jnp.concatenate([own_spread(d_rate, s, 1), own_spread(d_skip, s, 1)])[None]
    small_part = jnp.concatenate(
        [
            jnp.pad(by_dp(own_spread(d_conv, s, SSM_HEAD)), ((0, 0), (0, 0), (0, width - conv_block))),
            jnp.pad(by_dp(d_gains), ((0, 0), (0, 0), (0, width - gains_block))),
            jnp.broadcast_to(
                jnp.pad(d_heads, ((0, 7), (0, width - d_heads.shape[1])))[None], (dp_total, 8, width)
            ),
        ],
        axis=1,
    )
    normed_keep, normed_got = scatter_begin(d_normed_part)
    normed_held, normed_far = scatter_far(normed_keep, after(normed_got, grad_qkv_part))
    grad_xz_part, normed_held = lax.optimization_barrier((grad_xz_part, normed_held))
    grad_o, grad_xz_sum, grad_qkv_sum, small_sum = scatter_dp(
        [grad_o_part, grad_xz_part, grad_qkv_part, small_part], 2
    )
    normed_far = after(normed_far, small_sum)
    small_sum = small_sum + swap(small_sum, "seq", 1)
    small_sum = small_sum + swap(small_sum, "seq", 2)
    grad_xz_sum = grad_xz_sum.astype(LOW)
    first, last = trade_back(grad_xz_sum[:, :LOCAL_CH], grad_xz_sum[:, LOCAL_CH : 2 * LOCAL_CH])
    grad_xz = jnp.concatenate([first, last], axis=1)[:, : w_xz.shape[1]].astype(FULL)
    both_all = gather_seq(jnp.concatenate([grad_qkv_sum.astype(LOW), grad_xz_sum[:, 2 * LOCAL_CH :]], axis=1))
    bcdt_all = both_all[:, :, grad_qkv_sum.shape[1] :].astype(FULL)
    grad_bcdt = jnp.concatenate(
        [jnp.sum(bcdt_all[:, :, : 2 * STATE], axis=0)]
        + [bcdt_all[j, :, 2 * STATE : 2 * STATE + HEAD_COUNT[j]] for j in range(SEQ)],
        axis=1,
    )
    qkv_all = both_all[:, :, : grad_qkv_sum.shape[1]].astype(FULL)
    col = lambda j, at, width: qkv_all[j, :, at : at + width]
    shared = lambda at, width: jnp.sum(qkv_all[:, :, at : at + width], axis=0)
    grad_qkv_wide = jnp.concatenate(
        [col(j, 256, QW) for j in range(SEQ)]
        + [shared(256 + QW, QW)]
        + [col(j, 0, HEAD) for j in range(SEQ)]
        + [shared(128, HEAD)]
        + [col(j, HEAD, HEAD) for j in range(SEQ)]
        + [shared(128 + HEAD, HEAD)],
        axis=1,
    )
    qkv_width = w_qkv.shape[1]
    grad_qkv = lax.dynamic_slice_in_dim(grad_qkv_wide, s * qkv_width, qkv_width, 1)

    d_normed = scatter_end(normed_held, normed_far) + d_normed_own
    d_unit = d_normed * gains[0]
    scale = lax.rsqrt(jnp.mean(inputs_x * inputs_x, axis=-1, keepdims=True) + NORM_EPS)
    d_x_head = scale * (
        d_unit - inputs_x * scale * scale * jnp.mean(d_unit * inputs_x, axis=-1, keepdims=True)
    )
    input_grad = (d_x_tail + d_x_head).astype(LOW)
    grad_conv = small_sum[:CONV, :conv_block]
    grad_gains = small_sum[CONV : CONV + 4, :gains_block]
    grad_rate = small_sum[8, :SSM_HEADS]
    grad_skip = small_sum[8, SSM_HEADS : 2 * SSM_HEADS]
    return (
        mixed_out,
        input_grad,
        grad_gains,
        grad_qkv,
        grad_o,
        grad_xz,
        grad_bcdt,
        grad_conv,
        grad_rate,
        grad_skip,
        grad_out,
        grad_gate_up,
        grad_down,
    )


def solution(mesh):
    placed = (
        P(("dp", "seq"), None),
        P("dp", None),
        P(None, "dp"),
        P("dp", "seq"),
        P("dp", "seq"),
        P("dp", "seq"),
        P("dp", None),
        P(None, "dp"),
        P(),
        P(),
        P("dp", "seq"),
        P("dp", None, "seq"),
        P("dp", "seq"),
        P(("dp", "seq"), None),
    )
    return jax.shard_map(
        on_device,
        mesh=mesh,
        in_specs=placed,
        out_specs=(
            P(("dp", "seq"), None),
            P(("dp", "seq"), None),
            P(None, "dp"),
            P("dp", "seq"),
            P("dp", "seq"),
            P("dp", "seq"),
            P("dp", None),
            P(None, "dp"),
            P(),
            P(),
            P("dp", "seq"),
            P("dp", None, "seq"),
            P("dp", "seq"),
        ),
        check_vma=False,
    )
```

```python
import jax
import jax.numpy as jnp
from jax import lax
from jax.experimental import pallas as pl
from jax.experimental.layout import Layout, with_layout_constraint
from jax.experimental.pallas import tpu as pltpu
from jax.sharding import PartitionSpec as P

D = 1600
HEADS = 25
KV_HEADS = 5
HEAD = 64
INNER = 3200
SSM_HEAD = 64
STATE = 16
CONV = 4
FF = 5504
WINDOW = 1024
SSM_HEADS = 50

NORM_EPS = 1e-05
MASKED = -1e30
LOW = jnp.bfloat16
FULL = jnp.float32

SEQ = 4
GROUP_HEADS = HEADS // KV_HEADS
QW = GROUP_HEADS * HEAD
LOCAL_HEADS = 13
LOCAL_CH = LOCAL_HEADS * SSM_HEAD
CHUNK = 128
UNITS = FF // SEQ
UNITS_PAD = 1408
BCDT_PAD = 128
OUT_AT, O_AT, O5_AT, OUT_WIDTH = 0, 896, 1280, 1600
FIRST_HEAD = tuple((SSM_HEADS * s // 2 + 1) // 2 for s in range(SEQ))
HEAD_COUNT = tuple(b - a for a, b in zip(FIRST_HEAD, FIRST_HEAD[1:] + (SSM_HEADS,)))


def swap(value, axis, bit):
    return lax.ppermute(value, axis, [(i, i ^ bit) for i in range(lax.axis_size(axis))])


def place_kernel(count, index_ref, *refs):
    blocks, stacked, held, in_sems, out_sems = refs[:count], *refs[count:]
    loads = [
        pltpu.make_async_copy(block, held.at[i], in_sems.at[i]) for i, block in enumerate(blocks)
    ]
    stores = [
        pltpu.make_async_copy(held.at[i], stacked.at[index_ref[i]], out_sems.at[i])
        for i in range(count)
    ]
    for load in loads:
        load.start()
    for load, store in zip(loads, stores):
        load.wait()
        store.start()
    for store in stores:
        store.wait()


def place(blocks):
    count = len(blocks)
    block = blocks[0][1]
    anywhere = pl.BlockSpec(memory_space=pl.ANY)
    return pl.pallas_call(
        lambda *refs: place_kernel(count, *refs),
        out_shape=jax.ShapeDtypeStruct((count,) + block.shape, block.dtype),
        grid_spec=pltpu.PrefetchScalarGridSpec(
            num_scalar_prefetch=1,
            grid=(1,),
            in_specs=[anywhere] * count,
            out_specs=anywhere,
            scratch_shapes=[
                pltpu.VMEM((count,) + block.shape, block.dtype),
                pltpu.SemaphoreType.DMA((count,)),
                pltpu.SemaphoreType.DMA((count,)),
            ],
        ),
        compiler_params=pltpu.CompilerParams(vmem_limit_bytes=32 << 20),
        cost_estimate=pl.CostEstimate(
            flops=0, bytes_accessed=2 * count * block.size * block.dtype.itemsize, transcendentals=0
        ),
    )(jnp.stack([jnp.asarray(i, jnp.int32) for i, _ in blocks]), *[b for _, b in blocks])


def seq_order():
    me = lax.axis_index("seq")
    return [me, me ^ 1, me ^ 2, me ^ 3]


def seq_arrivals(block, beside=None):
    far, near = swap(block, "seq", 2), swap(block, "seq", 1)
    if beside is not None:
        far, beside = meet(far, beside)
    blocks = [block, near, far, swap(far, "seq", 1)]
    return blocks if beside is None else (blocks, beside)


def gather_seq(block):
    return place(list(zip(seq_order(), seq_arrivals(block))))


def scatter_begin(part):
    core = lax.axis_index("seq") % 2
    part = with_layout_constraint(part.astype(LOW), Layout((0, 1)))
    by_core = part.reshape((2, 2, part.shape[0] // SEQ) + part.shape[1:])
    give = lax.dynamic_index_in_dim(by_core, 1 - core, 1, False)
    keep = lax.dynamic_index_in_dim(by_core, core, 1, False)
    return keep, swap(give, "seq", 1)


def scatter_far(keep, got):
    far = lax.axis_index("seq") // 2
    at = lambda a, i: lax.dynamic_index_in_dim(a, i, 0, False).astype(FULL)
    give_far = (at(keep, 1 - far) + at(got, 1 - far)).astype(LOW)
    return at(keep, far) + at(got, far), swap(give_far, "seq", 2)


def scatter_end(held, got_far):
    return held + got_far.astype(FULL)


def relative_begin(part):
    part = with_layout_constraint(part.astype(LOW), Layout((0, 1)))
    rows = part.shape[0] // SEQ
    block = lambda k: part[rows * k : rows * (k + 1)]
    got = swap(jnp.concatenate([block(1), block(3)]), "seq", 1)
    return (block(0), block(2)), got


def relative_far(keep, got):
    rows = got.shape[0] // 2
    add = lambda k: keep[k].astype(FULL) + got[rows * k : rows * (k + 1)].astype(FULL)
    return add(0), swap(add(1).astype(LOW), "seq", 2)


def meet(one, two):
    return lax.optimization_barrier((one, two))


def after(values, done):
    return lax.optimization_barrier((values, done))[0]


def line_place():
    me = lax.axis_index("dp")
    return lax.axis_size("dp") // 2, me // 2, lax.rem(me, 2)


def greet(line, z, x):
    barrier = pltpu.get_barrier_semaphore()

    def signal(target):
        pl.semaphore_signal(
            barrier, inc=1, device_id={"dp": target}, device_id_type=pl.DeviceIdType.MESH
        )

    signal(2 * z + 1 - x)
    pl.when(z > 0)(lambda: signal(2 * (z - 1) + x))
    pl.when(z < line - 1)(lambda: signal(2 * (z + 1) + x))
    pl.semaphore_wait(
        barrier, 1 + (z > 0).astype(jnp.int32) + (z < line - 1).astype(jnp.int32)
    )


def pieces_of(arrays, axis):
    pieces = []
    for i, array in enumerate(arrays):
        rows = array.shape[axis]
        count = 1 if rows < 64 else 3 if rows < 256 else 4
        size = rows // count // 16 * 16 if count > 1 else rows
        for k in range(count):
            pieces.append((i, pl.ds(k * size, size if k < count - 1 else rows - k * size)))
    return pieces


def gather_phases(pieces, line, refs):
    packets = pieces[-1][0] + 1
    sources, outs = refs[:packets], refs[packets : 2 * packets]
    own_sem, up_sem, down_sem, line_sem, give_sem, got_sem = refs[2 * packets :]
    _, z, x = line_place()
    held = lambda i, zb: outs[pieces[i][0]].at[2 * zb + x, pieces[i][1]]
    mine = lambda i: sources[pieces[i][0]].at[pieces[i][1]]

    def copy(src, i, zb, send_sem, recv_sem, target):
        return pltpu.make_async_remote_copy(
            src_ref=src,
            dst_ref=held(i, zb),
            send_sem=send_sem.at[i, zb],
            recv_sem=recv_sem.at[i, zb],
            device_id={"dp": target},
            device_id_type=pl.DeviceIdType.MESH,
        )

    up_to = lambda src, i, zb: copy(src, i, zb, up_sem, line_sem, 2 * (z + 1) + x)
    down_to = lambda src, i, zb: copy(src, i, zb, down_sem, line_sem, 2 * (z - 1) + x)
    give = lambda src, i, zb: copy(src, i, zb, give_sem, got_sem, 2 * z + 1 - x)
    own = lambda i: pltpu.make_async_copy(mine(i), held(i, z), own_sem.at[i])

    def take_turn(turn):
        if turn == 0:
            greet(line, z, x)
        for i in range(len(pieces)):
            far = turn - i
            if far == 0:
                pl.when(z < line - 1)(lambda: up_to(mine(i), i, z).start())
                pl.when(z > 0)(lambda: down_to(mine(i), i, z).start())
                give(mine(i), i, z).start()
                own(i).start()
            elif 0 < far < line:

                @pl.when(z - far >= 0)
                def _():
                    zb = z - far
                    up_to(held(i, zb), i, zb).wait_recv()
                    pl.when(z < line - 1)(lambda: up_to(held(i, zb), i, zb).start())
                    give(held(i, zb), i, zb).start()

                @pl.when(z + far < line)
                def _():
                    zb = z + far
                    down_to(held(i, zb), i, zb).wait_recv()
                    pl.when(z > 0)(lambda: down_to(held(i, zb), i, zb).start())
                    give(held(i, zb), i, zb).start()

    def finish():
        for i in range(len(pieces)):
            own(i).wait()
            for zb in range(line):
                give(held(i, zb), i, zb).wait()
                pl.when((zb <= z) & (z < line - 1))(lambda: up_to(held(i, zb), i, zb).wait_send())
                pl.when((zb >= z) & (z > 0))(lambda: down_to(held(i, zb), i, zb).wait_send())

    turns = len(pieces) + line - 1
    return [lambda turn=turn: take_turn(turn) for turn in range(turns)] + [finish]


def gather_kernel(pieces, line, *refs):
    for phase in gather_phases(pieces, line, refs):
        phase()


def gather_scratch(pieces, line):
    count = len(pieces)
    sems = lambda *shape: pltpu.SemaphoreType.DMA(shape)
    return [sems(count)] + [sems(count, line) for _ in range(5)]


def gather_shapes(packets):
    return [jax.ShapeDtypeStruct((lax.axis_size("dp"),) + p.shape, p.dtype) for p in packets]


def gather_dp(packets, collective_id):
    total = lax.axis_size("dp")
    if total != 8:
        return [lax.all_gather(packet, "dp", axis=0) for packet in packets]
    pieces, line = pieces_of(packets, 0), total // 2
    return pl.pallas_call(
        lambda *refs: gather_kernel(pieces, line, *refs),
        out_shape=gather_shapes(packets),
        in_specs=[pl.BlockSpec(memory_space=pltpu.VMEM)] * len(packets),
        out_specs=[pl.BlockSpec(memory_space=pl.ANY)] * len(packets),
        scratch_shapes=gather_scratch(pieces, line),
        compiler_params=pltpu.CompilerParams(
            collective_id=collective_id, has_side_effects=True, vmem_limit_bytes=32 << 20
        ),
        cost_estimate=pl.CostEstimate(
            flops=0,
            bytes_accessed=2 * total * sum(p.size * p.dtype.itemsize for p in packets),
            transcendentals=0,
        ),
    )(*packets)


def add_columns(total, parts):
    width = total.shape[-1]
    step = 128 if width % 256 else 256

    def columns(c):
        at = pl.ds(pl.multiple_of(c * step, step), step)
        total[:, at] = sum(part[:, at].astype(FULL) for part in parts).astype(total.dtype)

    pl.loop(0, width // step)(columns)
    if width % step:
        at = slice(width // step * step, width)
        total[:, at] = sum(part[:, at].astype(FULL) for part in parts).astype(total.dtype)


def scatter_phases(pieces, line, refs):
    count = pieces[-1][0] + 1
    parts, outs = refs[:count], refs[count : 2 * count]
    own_refs, near_refs, line_refs = (
        refs[2 * count : 3 * count],
        refs[3 * count : 4 * count],
        refs[4 * count : 5 * count],
    )
    load_sem, give_sem, got_sem, send_sem, line_sem = refs[5 * count :]
    _, z, x = line_place()
    order = [t for pair in zip(range(line - 1, -1, -1), range(line)) for t in pair][:line]
    at = lambda arrays, i, t: arrays[pieces[i][0]].at[t, pieces[i][1]]
    remote = lambda src, dst, send, recv, target: pltpu.make_async_remote_copy(
        src_ref=src,
        dst_ref=dst,
        send_sem=send,
        recv_sem=recv,
        device_id={"dp": target},
        device_id_type=pl.DeviceIdType.MESH,
    )
    give = lambda i, t: remote(
        at(parts, i, 2 * t + 1 - x),
        at(near_refs, i, t),
        give_sem.at[i, t],
        got_sem.at[i, t],
        2 * z + 1 - x,
    )
    load = lambda i, t: pltpu.make_async_copy(
        at(parts, i, 2 * t + x), at(own_refs, i, t), load_sem.at[i, t]
    )
    along = lambda i, t, slot, target: remote(
        at(own_refs, i, t), at(line_refs, i, slot), send_sem.at[i, t], line_sem.at[i, slot], target
    )
    def views(i):
        return [lambda t, arrays=arrays: at(arrays, i, t) for arrays in (own_refs, near_refs, line_refs)]

    def start():
        greet(line, z, x)
        for i in range(len(pieces)):
            for t in order:
                load(i, t).start()
                give(i, t).start()

    def pass_on(i, t, zz):
        own, near, held = views(i)
        load(i, t).wait()
        give(i, t).wait_recv()
        terms = [own(t), near(t)]
        if 0 < zz < t or t < zz < line - 1:
            along(i, t, t, 0).wait_recv()
            terms.append(held(t))
        add_columns(own(t), terms)
        step = 1 if t > zz else -1
        along(i, t, line if t == zz - 1 else t, 2 * (zz + step) + x).start()

    def take_round(r):
        for zz in range(line):

            @pl.when(z == zz)
            def _():
                up, down = r - zz, r - (line - 1 - zz)
                for t in range(line - 1, zz, -1):
                    if 0 <= up < len(pieces):
                        pass_on(up, t, zz)
                for t in range(zz):
                    if 0 <= down < len(pieces):
                        pass_on(down, t, zz)

    def finish():
        for i in range(len(pieces)):
            own, near, held = views(i)
            for t in range(line):

                @pl.when(t == z)
                def _():
                    load(i, t).wait()
                    give(i, t).wait_recv()
                    terms = [own(t), near(t)]
                    if t > 0:
                        along(i, t, t, 0).wait_recv()
                        terms.append(held(t))
                    if t < line - 1:
                        along(i, t, line, 0).wait_recv()
                        terms.append(held(line))
                    add_columns(outs[pieces[i][0]].at[pieces[i][1]], terms)

                pl.when(t != z)(lambda: along(i, t, t, 0).wait_send())
                give(i, t).wait_send()

    rounds = len(pieces) + line - 2
    return [start] + [lambda r=r: take_round(r) for r in range(rounds)] + [finish]


def scatter_kernel(pieces, line, *refs):
    for phase in scatter_phases(pieces, line, refs):
        phase()


def scatter_scratch(parts, pieces, line):
    count = len(pieces)
    sems = lambda *shape: pltpu.SemaphoreType.DMA(shape)
    buffers = [pltpu.VMEM((n,) + p.shape[1:], p.dtype) for n in (line, line, line + 1) for p in parts]
    return buffers + [sems(count, line) for _ in range(4)] + [sems(count, line + 1)]


def scatter_dp(parts, collective_id):
    total = lax.axis_size("dp")
    if total != 8:
        sums = [lax.psum_scatter(p, "dp", scatter_dimension=0) for p in parts]
        return [lax.optimization_barrier(p).astype(FULL) for p in sums]
    pieces, line = pieces_of(parts, 1), total // 2
    return pl.pallas_call(
        lambda *refs: scatter_kernel(pieces, line, *refs),
        out_shape=[jax.ShapeDtypeStruct(p.shape[1:], FULL) for p in parts],
        in_specs=[pl.BlockSpec(memory_space=pl.ANY)] * len(parts),
        out_specs=[pl.BlockSpec(memory_space=pltpu.VMEM)] * len(parts),
        scratch_shapes=scatter_scratch(parts, pieces, line),
        compiler_params=pltpu.CompilerParams(
            collective_id=collective_id, has_side_effects=True, vmem_limit_bytes=56 << 20
        ),
        cost_estimate=pl.CostEstimate(
            flops=0, bytes_accessed=sum(p.size * 2 for p in parts), transcendentals=0
        ),
    )(*parts)


def gather_dp_apart(packet):
    return lax.all_gather(packet, "dp", axis=0, tiled=True)


def scatter_dp_apart(parts):
    summed = lax.psum_scatter(parts.astype(LOW), "dp", scatter_dimension=0, tiled=True)
    return lax.optimization_barrier(summed).astype(FULL)


def trade_halves(first, last):
    me = lax.axis_index("seq")
    one = lax.ppermute(jnp.where(me == 0, last, first), "seq", [(0, 1), (1, 2), (2, 0)])
    two = lax.ppermute(jnp.where(me == 3, first, last), "seq", [(1, 3), (2, 1), (3, 2)])
    return pick([first, one, one, two], me), pick([one, two, two, last], me)


def trade_back(x_part, z_part):
    me = lax.axis_index("seq")
    one = lax.ppermute(jnp.where(me == 0, z_part, x_part), "seq", [(1, 0), (2, 1), (0, 2)])
    two = lax.ppermute(jnp.where(me == 3, x_part, z_part), "seq", [(3, 1), (1, 2), (2, 3)])
    return pick([x_part, one, one, two], me), pick([one, two, two, z_part], me)


def mm(left, right):
    return jnp.dot(left, right, preferred_element_type=FULL)


def mm_nt(left, right):
    return lax.dot_general(left, right, (((1,), (1,)), ((), ())), preferred_element_type=FULL)


def mm_tn(left, right):
    return lax.dot_general(left, right, (((0,), (0,)), ((), ())), preferred_element_type=FULL)


def rms_norm(values, gain):
    return values * lax.rsqrt(jnp.mean(values * values, axis=-1, keepdims=True) + NORM_EPS) * gain


def norm_rows_kernel(values_ref, gain_ref, out_ref):
    out_ref[...] = rms_norm(values_ref[...].astype(FULL), gain_ref[0:1]).astype(LOW)


def norm_rows(values, gain):
    rows, width = values.shape
    block = rows // SEQ
    by_block = pl.BlockSpec((block, width), lambda i: (i, 0))
    return pl.pallas_call(
        norm_rows_kernel,
        grid=(SEQ,),
        in_specs=[by_block, pl.BlockSpec((8, width), lambda i: (0, 0))],
        out_specs=by_block,
        out_shape=jax.ShapeDtypeStruct(values.shape, LOW),
        cost_estimate=pl.CostEstimate(flops=4 * values.size, bytes_accessed=4 * values.size, transcendentals=rows),
    )(values, jnp.broadcast_to(gain, (8, width)))


def join_tail(inputs_x, attn_o, ssm_o, gains):
    residual = inputs_x + 0.5 * (rms_norm(attn_o, gains[1]) + rms_norm(ssm_o, gains[2]))
    return (residual, rms_norm(residual, gains[3]))


STEP_AT = 2 * STATE
WIDE = 896
PAIRS = WIDE // 128
XZB = 1792


def dot_any(left, right, contract):
    return lax.dot_general(
        left, right, ((contract[:1], contract[1:]), ((), ())), preferred_element_type=FULL
    )


def low_dot(left, right, contract):
    return dot_any(left.astype(LOW), right.astype(LOW), contract)


def iota(shape, axis):
    return lax.broadcasted_iota(jnp.int32, shape, axis)


def pair_spread(values):
    rows = values.shape[0]
    low_half = iota((rows, 128), 1) < SSM_HEAD
    tiles = []
    for p in range(PAIRS):
        one = values[:, STEP_AT + 2 * p : STEP_AT + 2 * p + 1]
        two = values[:, STEP_AT + 2 * p + 1 : STEP_AT + 2 * p + 2]
        tiles.append(
            jnp.where(
                low_half,
                jnp.broadcast_to(one, (rows, 128)),
                jnp.broadcast_to(two, (rows, 128)),
            )
        )
    return jnp.concatenate(tiles, axis=1)


def halves(tile):
    low_half = iota(tile.shape, 1) < SSM_HEAD
    zero = jnp.zeros_like(tile)
    return jnp.concatenate([jnp.where(low_half, tile, zero), jnp.where(low_half, zero, tile)], axis=0)


def mamba_chunk(c, lengths_ref, xzb_ref, tail_ref, conv_ref, rate_ref, pad_ref):
    first_end = lengths_ref[0, 0]
    second_end = first_end + lengths_ref[0, 1]
    doc_of = lambda pos: (pos >= first_end).astype(jnp.int32) + (pos >= second_end).astype(jnp.int32)
    base = c * CHUNK
    square = (CHUNK, CHUNK)
    row, lane = iota(square, 0), iota(square, 1)
    doc_row = doc_of(base + row)
    doc_lane = doc_of(base + lane)
    before = jnp.where(c > 0, doc_of(base - 1), -1)
    end = doc_of(base + CHUNK - 1)
    causal = (row >= lane) & (doc_row == doc_lane)
    channel = iota((CHUNK, WIDE), 1) < LOCAL_CH

    raw = jnp.where(channel, xzb_ref[:, :WIDE], 0.0).astype(LOW).astype(FULL)
    gate = pltpu.roll(xzb_ref[:, LOCAL_CH - 64 :], XZB - LOCAL_CH, 1)[:, :WIDE]
    gate = jnp.where(channel, gate, 0.0)
    pad_ref[0:8] = tail_ref[:, :WIDE].astype(LOW).astype(FULL)
    pad_ref[8 : 8 + CHUNK] = raw
    taps = []
    pos = base + iota((CHUNK, 1), 0)
    conv = jnp.zeros((CHUNK, WIDE), FULL)
    for k in range(CONV):
        back = CONV - 1 - k
        same = (doc_of(pos) == doc_of(pos - back)) & (pos >= back)
        shifted = jnp.where(same, pad_ref[8 - back : 8 - back + CHUNK], 0.0)
        taps.append(shifted)
        conv = conv + conv_ref[k : k + 1] * shifted
    conv_sig = jax.nn.sigmoid(conv)
    act = conv * conv_sig

    bc = xzb_ref[:, 2 * LOCAL_CH :]
    b_in = jnp.where(lane < STATE, bc, 0.0)
    c_at = jnp.where((lane >= STATE) & (lane < 2 * STATE), bc, 0.0)
    c_in = pltpu.roll(c_at, CHUNK - STATE, 1)
    step = jnp.maximum(bc, 0.0) + jnp.log(1.0 + jnp.exp(-jnp.abs(bc)))
    lower = (row >= lane).astype(FULL)
    log = lax.dot_general(
        lower,
        -step * rate_ref[0:1],
        (((1,), (0,)), ((), ())),
        precision=lax.Precision.HIGHEST,
        preferred_element_type=FULL,
    )
    last = log[CHUNK - 1 : CHUNK]
    ends = jnp.where(doc_row == end, jnp.exp(last - log), 0.0)
    reach = jnp.where(doc_row == before, jnp.exp(log), 0.0)
    carry = jnp.where(end == before, jnp.exp(last), 0.0)
    gram = low_dot(c_in, b_in, (1, 1))
    log_t = log.T

    def decays(h):
        gap = log[:, STEP_AT + h : STEP_AT + h + 1] - log_t[STEP_AT + h : STEP_AT + h + 1]
        return jnp.exp(jnp.where(causal, gap, MASKED))

    step_wide = pair_spread(step)
    return dict(
        row=row, lane=lane, pos=pos, doc_of=doc_of, gate=gate, taps=taps, conv=conv, conv_sig=conv_sig,
        act=act, bc=bc, b_in=b_in, c_in=c_in, c_at=c_at, step=step, ends=ends, reach=reach,
        carry=carry, gram=gram, decays=decays, step_wide=step_wide, moved=act * step_wide,
    )


def mamba_forward_kernel(
    lengths_ref, xzb_ref, tail_ref, conv_ref, rate_ref, skip_ref, gated_ref, read_ref, states_ref, pad_ref, state_ref
):
    c = pl.program_id(0)

    @pl.when(c == 0)
    def _():
        state_ref[...] = jnp.zeros_like(state_ref)

    v = mamba_chunk(c, lengths_ref, xzb_ref, tail_ref, conv_ref, rate_ref, pad_ref)
    states_ref[0] = state_ref[STATE : 2 * STATE]
    moved = v["moved"]
    from_state = low_dot(v["c_at"], state_ref[...], (1, 0)) * pair_spread(v["reach"])
    tiles = []
    for p in range(PAIRS):
        mixing = jnp.concatenate(
            [(v["decays"](2 * p + j) * v["gram"]).astype(LOW) for j in range(2)], axis=1
        )
        tiles.append(dot_any(mixing, halves(moved[:, 128 * p : 128 * p + 128].astype(LOW)), (1, 0)))
    read = jnp.concatenate(tiles, axis=1) + from_state + skip_ref[0:1] * v["act"]
    read_ref[...] = read.astype(LOW)
    gated_ref[...] = (read * v["gate"] * jax.nn.sigmoid(v["gate"])).astype(LOW)
    added = low_dot(v["b_in"], moved * pair_spread(v["ends"]), (0, 0))[:STATE]
    state_ref[STATE : 2 * STATE] = pair_spread(v["carry"]) * state_ref[STATE : 2 * STATE] + added


def mamba_backward_kernel(
    lengths_ref, xzb_ref, tail_ref, conv_ref, rate_ref, skip_ref, states_ref, read_ref, d_gated_ref,
    d_xzb_ref, d_chan_ref, d_rate_ref, pad_ref, state_ref, d_state_ref, d_pad_ref,
):
    g = pl.program_id(0)
    c = pl.num_programs(0) - 1 - g

    @pl.when(g == 0)
    def _():
        state_ref[...] = jnp.zeros_like(state_ref)
        d_state_ref[...] = jnp.zeros_like(d_state_ref)
        d_pad_ref[...] = jnp.zeros_like(d_pad_ref)
        d_chan_ref[...] = jnp.zeros_like(d_chan_ref)
        d_rate_ref[...] = jnp.zeros_like(d_rate_ref)

    v = mamba_chunk(c, lengths_ref, xzb_ref, tail_ref, conv_ref, rate_ref, pad_ref)
    row, lane, act, moved, gate = v["row"], v["lane"], v["act"], v["moved"], v["gate"]
    state_ref[STATE : 2 * STATE] = states_ref[0]
    by_head = (iota((WIDE, 128), 0) // SSM_HEAD + STEP_AT == iota((WIDE, 128), 1)).astype(LOW)
    head_sum = lambda wide: dot_any(wide.astype(LOW), by_head, (1, 0))

    d_gated = d_gated_ref[...].astype(FULL)
    gate_sig = jax.nn.sigmoid(gate)
    d_read = d_gated * gate * gate_sig
    d_gate = d_gated * read_ref[...].astype(FULL) * gate_sig * (1.0 + gate * (1.0 - gate_sig))
    d_chan_ref[CONV : CONV + 1] += jnp.sum(d_read * act, axis=0, keepdims=True)
    d_act = skip_ref[0:1] * d_read

    d_log = jnp.zeros_like(v["gram"])
    d_log_t = jnp.zeros_like(v["gram"])
    d_gram = jnp.zeros_like(v["gram"])
    tiles = []
    for p in range(PAIRS):
        at = slice(128 * p, 128 * p + 128)
        d_pair = halves(d_read[:, at].astype(LOW))
        d_mixing = dot_any(d_pair, moved[:, at].astype(LOW), (1, 1))
        mixings = []
        for j in range(2):
            h = 2 * p + j
            decay = v["decays"](h)
            mixing = decay * v["gram"]
            d_one = d_mixing[CHUNK * j : CHUNK * (j + 1)]
            d_gram = d_gram + d_one * decay
            d_gap = d_one * mixing
            mixings.append(mixing.astype(LOW))
            d_log = d_log + jnp.where(lane == STEP_AT + h, jnp.sum(d_gap, axis=1, keepdims=True), 0.0)
            d_log_t = d_log_t + jnp.where(row == STEP_AT + h, jnp.sum(d_gap, axis=0, keepdims=True), 0.0)
        tiles.append(dot_any(jnp.concatenate(mixings, axis=0), d_pair, (0, 0)))
    d_moved = jnp.concatenate(tiles, axis=1)
    d_log = d_log - d_log_t.T

    d_product = d_read * pair_spread(v["reach"])
    state_low = state_ref[...].astype(LOW)
    product = dot_any(v["c_at"].astype(LOW), state_low, (1, 0))
    d_log = d_log + head_sum(d_product * product)
    d_c = low_dot(d_product, state_low, (1, 1)) + low_dot(d_gram, pltpu.roll(v["b_in"], STATE, 1), (1, 0))
    d_state_in = low_dot(v["c_at"], d_product, (0, 0))[STATE : 2 * STATE]

    d_state = d_state_ref[...]
    d_state_low = d_state.astype(LOW)
    ends_wide = pair_spread(v["ends"])
    d_put = dot_any(v["b_in"].astype(LOW), d_state_low, (1, 0)) * ends_wide
    d_b = low_dot(moved * ends_wide, d_state_low, (1, 1)) + low_dot(d_gram, v["c_in"], (0, 0))
    d_moved = d_moved + d_put
    d_ends = head_sum(d_put * moved)
    carry_wide = pair_spread(v["carry"])
    d_carry = head_sum(
        jnp.broadcast_to(
            jnp.sum(d_state[:STATE] * states_ref[0], axis=0, keepdims=True) * carry_wide, (16, WIDE)
        )
    )[0:1]
    d_last = jnp.sum(d_ends, axis=0, keepdims=True) + d_carry
    d_log = d_log - d_ends + jnp.where(row == CHUNK - 1, d_last, 0.0)
    d_state_ref[:STATE] = d_state_in + carry_wide * d_state[:STATE]

    d_act = d_act + d_moved * v["step_wide"]
    d_rate_step = lax.dot_general(
        (row >= lane).astype(FULL),
        d_log,
        (((0,), (0,)), ((), ())),
        precision=lax.Precision.HIGHEST,
        preferred_element_type=FULL,
    )
    d_step = head_sum(d_moved * act) - rate_ref[0:1] * d_rate_step
    d_rate_ref[0:1] += jnp.sum(-v["step"] * d_rate_step, axis=0, keepdims=True)
    is_step = (lane >= STEP_AT) & (lane < STEP_AT + LOCAL_HEADS)
    d_bc = d_b + d_c + jnp.where(is_step, d_step * jax.nn.sigmoid(v["bc"]), 0.0)

    d_conv = d_act * v["conv_sig"] * (1.0 + v["conv"] * (1.0 - v["conv_sig"]))
    d_pad_ref[0:CHUNK] = d_conv
    d_raw = jnp.zeros_like(d_conv)
    for k in range(CONV):
        ahead = CONV - 1 - k
        d_chan_ref[k : k + 1] += jnp.sum(d_conv * v["taps"][k], axis=0, keepdims=True)
        same = v["doc_of"](v["pos"]) == v["doc_of"](v["pos"] + ahead)
        d_raw = d_raw + conv_ref[k : k + 1] * jnp.where(same, d_pad_ref[ahead : ahead + CHUNK], 0.0)
    d_pad_ref[CHUNK : CHUNK + 8] = d_conv[0:8]

    moved_gate = pltpu.roll(jnp.concatenate([d_gate, jnp.zeros_like(row).astype(FULL)], axis=1), 64, 1)
    d_xzb_ref[:, : LOCAL_CH - 64] = d_raw[:, : LOCAL_CH - 64].astype(LOW)
    d_xzb_ref[:, LOCAL_CH - 64 : LOCAL_CH + 64] = (
        d_raw[:, LOCAL_CH - 64 :] + moved_gate[:, :128]
    ).astype(LOW)
    d_xzb_ref[:, LOCAL_CH + 64 : 2 * LOCAL_CH] = moved_gate[:, 128:WIDE].astype(LOW)
    d_xzb_ref[:, 2 * LOCAL_CH :] = d_bc.astype(LOW)


def mamba_specs(chunk_of):
    tail = lambda g: (jnp.maximum(chunk_of(g) * (CHUNK // 8) - 1, 0), 0)
    fixed = lambda shape: pl.BlockSpec(shape, lambda g: (0,) * len(shape))
    return [
        pl.BlockSpec(memory_space=pltpu.SMEM),
        pl.BlockSpec((CHUNK, XZB), lambda g: (chunk_of(g), 0)),
        pl.BlockSpec((8, XZB), tail),
        fixed((8, WIDE)),
        fixed((8, 128)),
        fixed((8, WIDE)),
    ]


def mamba_forward(lengths, xzb, conv_rows, rate_row, skip_row):
    total = xzb.shape[0]
    chunks = total // CHUNK
    by_chunk = lambda width: pl.BlockSpec((CHUNK, width), lambda g: (g, 0))
    return pl.pallas_call(
        mamba_forward_kernel,
        grid=(chunks,),
        in_specs=mamba_specs(lambda g: g),
        out_specs=[by_chunk(WIDE), by_chunk(WIDE), pl.BlockSpec((1, STATE, WIDE), lambda g: (g, 0, 0))],
        out_shape=[
            jax.ShapeDtypeStruct((total, WIDE), LOW),
            jax.ShapeDtypeStruct((total, WIDE), LOW),
            jax.ShapeDtypeStruct((chunks, STATE, WIDE), FULL),
        ],
        scratch_shapes=[pltpu.VMEM((8 + CHUNK, WIDE), FULL), pltpu.VMEM((CHUNK, WIDE), FULL)],
        compiler_params=pltpu.CompilerParams(vmem_limit_bytes=32 << 20),
        cost_estimate=pl.CostEstimate(flops=2 * 10**10, bytes_accessed=16 << 20, transcendentals=10**7),
    )(lengths, xzb, xzb, conv_rows, rate_row, skip_row)


def mamba_backward(lengths, xzb, conv_rows, rate_row, skip_row, states, read, d_gated):
    total = xzb.shape[0]
    chunks = total // CHUNK
    chunk_of = lambda g: chunks - 1 - g
    by_chunk = lambda width: pl.BlockSpec((CHUNK, width), lambda g: (chunk_of(g), 0))
    return pl.pallas_call(
        mamba_backward_kernel,
        grid=(chunks,),
        in_specs=mamba_specs(chunk_of)
        + [pl.BlockSpec((1, STATE, WIDE), lambda g: (chunk_of(g), 0, 0)), by_chunk(WIDE), by_chunk(WIDE)],
        out_specs=[
            by_chunk(XZB),
            pl.BlockSpec((8, WIDE), lambda g: (0, 0)),
            pl.BlockSpec((8, 128), lambda g: (0, 0)),
        ],
        out_shape=[
            jax.ShapeDtypeStruct((total, XZB), LOW),
            jax.ShapeDtypeStruct((8, WIDE), FULL),
            jax.ShapeDtypeStruct((8, 128), FULL),
        ],
        scratch_shapes=[
            pltpu.VMEM((8 + CHUNK, WIDE), FULL),
            pltpu.VMEM((CHUNK, WIDE), FULL),
            pltpu.VMEM((CHUNK, WIDE), FULL),
            pltpu.VMEM((8 + CHUNK, WIDE), FULL),
        ],
        compiler_params=pltpu.CompilerParams(vmem_limit_bytes=32 << 20),
        cost_estimate=pl.CostEstimate(flops=6 * 10**10, bytes_accessed=24 << 20, transcendentals=10**7),
    )(lengths, xzb, xzb, conv_rows, rate_row, skip_row, states, read, d_gated)


def head_under(h, at, value):
    row, lane = iota((QW, 128), 0), iota((QW, 128), 1)
    inside = (lane >= at) & (lane < at + HEAD) & (row == h * HEAD + lane - at)
    return jnp.where(inside, value, 0.0).astype(LOW)


def row_block(t):
    return jnp.where(t < SEQ, t, lax.axis_index("seq"))


def allowed_keys(lengths_ref, block, rows, extent):
    first_end = lengths_ref[0, 0]
    second_end = first_end + lengths_ref[0, 1]
    row = block * rows + iota((rows, 1), 0)
    start = jnp.where(row >= second_end, second_end, jnp.where(row >= first_end, first_end, 0))
    least = jnp.maximum(start, row - (WINDOW - 1))
    key = iota((rows, extent), 1)
    return (key >= least) & (key <= row)


def for_extent(block, rows, run):
    for e in range(SEQ):
        pl.when(block == e)(lambda e=e: run((e + 1) * rows))


def attention_forward_kernel(lengths_ref, q_ref, kv_ref, out_ref, log_ref):
    t, h = pl.program_id(0), pl.program_id(1)
    rows = q_ref.shape[0]
    block = row_block(t)

    def run(extent):
        q = dot_any(q_ref[...], head_under(h, 0, HEAD ** (-0.5)), (1, 0)).astype(LOW)
        kv = kv_ref[:extent]
        scores = dot_any(q, kv, (1, 1))
        scores = jnp.where(allowed_keys(lengths_ref, block, rows, extent), scores, MASKED)
        top = jnp.max(scores, axis=1, keepdims=True)
        expos = jnp.exp(scores - top)
        denom = jnp.sum(expos, axis=1, keepdims=True)
        mixed = dot_any((expos * (1.0 / denom)).astype(LOW), kv, (1, 0)).astype(LOW)
        out = dot_any(mixed, head_under(h, HEAD, 1.0), (1, 1)).astype(LOW)
        log = jnp.where(iota((rows, 128), 1) == h, top + jnp.log(denom), 0.0)

        @pl.when(h == 0)
        def _():
            out_ref[...] = out
            log_ref[...] = log

        @pl.when(h > 0)
        def _():
            out_ref[...] += out
            log_ref[...] += log

    for_extent(block, rows, run)


def attention_backward_kernel(
    lengths_ref, q_ref, kv_ref, out_ref, log_ref, d_out_ref, d_q_ref, d_kv_ref, sum_ref
):
    t, h = pl.program_id(0), pl.program_id(1)
    rows = q_ref.shape[0]
    block = row_block(t)

    @pl.when((h == 0) & ((t == 0) | (t == SEQ)))
    def _():
        sum_ref[...] = jnp.zeros_like(sum_ref)

    def run(extent):
        under_q = head_under(h, 0, HEAD ** (-0.5))
        q = dot_any(q_ref[...], under_q, (1, 0)).astype(LOW)
        d_out = dot_any(d_out_ref[...], head_under(h, HEAD, 1.0), (1, 0)).astype(LOW)
        log = jnp.sum(jnp.where(iota((rows, 128), 1) == h, log_ref[...], 0.0), axis=1, keepdims=True)
        own = iota((rows, QW), 1) // HEAD == h
        product = d_out_ref[...].astype(FULL) * out_ref[...].astype(FULL)
        d_total = jnp.sum(jnp.where(own, product, 0.0), axis=1, keepdims=True)
        kv = kv_ref[:extent]
        scores = dot_any(q, kv, (1, 1))
        allowed = allowed_keys(lengths_ref, block, rows, extent)
        probs = jnp.exp(jnp.where(allowed, scores - log, MASKED))
        d_probs = dot_any(d_out, kv, (1, 1))
        d_scores = (probs * (d_probs - d_total)).astype(LOW)
        sum_ref[:extent] += dot_any(probs.astype(LOW), d_out, (0, 0)) + dot_any(d_scores, q, (0, 0))
        d_q = dot_any(dot_any(d_scores, kv, (1, 0)).astype(LOW), under_q, (1, 1)).astype(LOW)

        @pl.when(h == 0)
        def _():
            d_q_ref[...] = d_q

        @pl.when(h > 0)
        def _():
            d_q_ref[...] += d_q

    for_extent(block, rows, run)

    @pl.when((h == GROUP_HEADS - 1) & (t >= SEQ - 1))
    def _():
        d_kv_ref[...] = sum_ref[...].astype(LOW)


def attention_specs(rows, group):
    by_step = lambda width: pl.BlockSpec((rows, width), lambda t, h: (t, 0))
    kv_block = pl.BlockSpec((group, 128), lambda t, h: (0, t // SEQ))
    return by_step, kv_block


def attention_forward(lengths, queries, kv, rows):
    by_step, kv_block = attention_specs(rows, kv.shape[0])
    return pl.pallas_call(
        attention_forward_kernel,
        grid=(SEQ + 1, GROUP_HEADS),
        in_specs=[pl.BlockSpec(memory_space=pltpu.SMEM), by_step(QW), kv_block],
        out_specs=[by_step(QW), by_step(128)],
        out_shape=[
            jax.ShapeDtypeStruct(queries.shape, LOW),
            jax.ShapeDtypeStruct((queries.shape[0], 128), FULL),
        ],
        compiler_params=pltpu.CompilerParams(vmem_limit_bytes=32 << 20),
        cost_estimate=pl.CostEstimate(flops=4 * 10**10, bytes_accessed=4 << 20, transcendentals=8 * 10**6),
    )(lengths, queries, kv)


def attention_backward(lengths, queries, kv, out, logs, d_out, rows, parts, collective_id):
    group = kv.shape[0]
    by_step, kv_block = attention_specs(rows, group)
    total = lax.axis_size("dp")
    beside = parts if total == 8 else []
    count, line = len(beside), total // 2
    pieces = pieces_of(beside, 1)

    def kernel(*refs):
        own_in, parts_in = refs[:6], refs[6 : 6 + count]
        own_out, sums_out = refs[6 + count : 8 + count], refs[8 + count : 8 + 2 * count]
        sum_ref, transfer = refs[8 + 2 * count], refs[9 + 2 * count :]
        step = pl.program_id(0) * GROUP_HEADS + pl.program_id(1)
        steps = (SEQ + 1) * GROUP_HEADS
        phases = scatter_phases(pieces, line, parts_in + sums_out + transfer) if count else []
        spots = [min(13 * k, steps - 1) for k in range(len(phases))]
        for phase, spot in zip(phases, spots):
            if spot < steps - 1:
                pl.when(step == spot)(phase)
        attention_backward_kernel(*own_in, *own_out, sum_ref)
        for phase, spot in zip(phases, spots):
            if spot == steps - 1:
                pl.when(step == spot)(phase)

    found = pl.pallas_call(
        kernel,
        grid=(SEQ + 1, GROUP_HEADS),
        in_specs=[pl.BlockSpec(memory_space=pltpu.SMEM), by_step(QW), kv_block]
        + [by_step(QW), by_step(128), by_step(QW)]
        + [pl.BlockSpec(memory_space=pl.ANY)] * count,
        out_specs=[by_step(QW), kv_block] + [pl.BlockSpec(memory_space=pltpu.VMEM)] * count,
        out_shape=[jax.ShapeDtypeStruct(queries.shape, LOW), jax.ShapeDtypeStruct(kv.shape, LOW)]
        + [jax.ShapeDtypeStruct(p.shape[1:], FULL) for p in beside],
        scratch_shapes=[pltpu.VMEM((group, 128), FULL)]
        + (scatter_scratch(beside, pieces, line) if count else []),
        compiler_params=pltpu.CompilerParams(
            vmem_limit_bytes=56 << 20,
            **(dict(collective_id=collective_id, has_side_effects=True) if count else {}),
        ),
        cost_estimate=pl.CostEstimate(flops=10**11, bytes_accessed=8 << 20, transcendentals=8 * 10**6),
    )(lengths, queries, kv, out, logs, d_out, *beside)
    return found[0], found[1], list(found[2:]) if count else scatter_dp(parts, collective_id)


def pick(options, seq_index):
    return lax.select_n(seq_index, *options)


def own_cut(values, seq_index, axis, unit):
    cuts = []
    for first, count in zip(FIRST_HEAD, HEAD_COUNT):
        cut = lax.slice_in_dim(values, first * unit, (first + count) * unit, axis=axis)
        pads = [(0, 0)] * values.ndim
        pads[axis] = (0, (LOCAL_HEADS - count) * unit)
        cuts.append(jnp.pad(cut, pads))
    return pick(cuts, seq_index)


def own_spread(values, seq_index, unit):
    spreads = []
    for first, count in zip(FIRST_HEAD, HEAD_COUNT):
        pads = [(0, 0)] * (values.ndim - 1) + [(first * unit, (SSM_HEADS - first - count) * unit)]
        spreads.append(jnp.pad(values[..., : count * unit], pads))
    return pick(spreads, seq_index)


def channel_cut(wide, seq_index, axis):
    return own_cut(wide, seq_index, axis, SSM_HEAD)


def bcdt_cut(w_bcdt, seq_index):
    first = pick([jnp.int32(h) for h in FIRST_HEAD], seq_index)
    count = pick([jnp.int32(c) for c in HEAD_COUNT], seq_index)
    source = jnp.arange(w_bcdt.shape[1], dtype=jnp.int32)[:, None]
    target = jnp.arange(BCDT_PAD, dtype=jnp.int32)[None]
    shared = (target < 2 * STATE) & (source == target)
    steps = (target >= 2 * STATE) & (target < 2 * STATE + count) & (source == target + first)
    return mm(w_bcdt, (shared | steps).astype(LOW)).astype(LOW)


def wide_of(arrivals):
    me = lax.axis_index("seq")
    return jnp.concatenate([pick(arrivals, me ^ j) for j in range(SEQ)], axis=1)


def on_device(
    tokens_in,
    doc_lengths,
    norm_gains,
    w_qkv,
    w_o,
    w_xz,
    w_bcdt,
    conv_w,
    ssm_rate,
    ssm_skip,
    w_out,
    w_gate_up,
    w_down,
    cotangent,
):
    rows = tokens_in.shape[0]
    group = rows * SEQ
    s = lax.axis_index("seq")
    dp_index = lax.axis_index("dp")
    dp_total = lax.axis_size("dp")
    block_rows = w_qkv.shape[0]
    kv_width = KV_HEADS * HEAD
    lengths = doc_lengths[0]
    live = (jnp.arange(rows, dtype=jnp.int32) + s * rows < lengths[0] + lengths[1]).astype(FULL)[:, None]

    gains_block = norm_gains.shape[1]
    conv_block = conv_w.shape[1]
    width = -(-max(conv_block, gains_block) // 128) * 128
    small = jnp.concatenate(
        [
            jnp.pad(conv_w, ((0, 4), (0, width - conv_block))),
            jnp.pad(norm_gains, ((0, 4), (0, width - gains_block))),
        ]
    )
    out_block = w_out.shape[0]
    out_packet = jnp.concatenate([w_o, w_out], axis=0)
    qkv_shards = seq_arrivals(w_qkv)
    x_part, z_part = trade_halves(
        w_xz[:, :LOCAL_CH], jnp.pad(w_xz[:, LOCAL_CH:], ((0, 0), (0, 2 * LOCAL_CH - w_xz.shape[1])))
    )
    token_blocks = seq_arrivals(tokens_in)
    small, out_cols = gather_dp([small, out_packet], 0)
    small, out_cols, qkv_shards, x_part, z_part, token_blocks = lax.optimization_barrier(
        (small, out_cols, qkv_shards, x_part, z_part, token_blocks)
    )
    full_conv = small[:, :4, :conv_block].transpose(1, 0, 2).reshape(4, INNER).astype(FULL)
    gains = small[:, 8:12, :gains_block].transpose(1, 0, 2).reshape(4, D).astype(FULL)
    tokens_group = place(list(zip(seq_order(), token_blocks))).reshape(group, D)
    normed = norm_rows(tokens_group, gains[0])
    qkv_wide = wide_of(qkv_shards)
    q_at = lambda h: lax.dynamic_slice_in_dim(qkv_wide, h * QW, QW, 1)
    kv_at = lambda h: [
        lax.dynamic_slice_in_dim(qkv_wide, D + h * HEAD, HEAD, 1),
        lax.dynamic_slice_in_dim(qkv_wide, D + kv_width + h * HEAD, HEAD, 1),
    ]
    qkv_packet = jnp.concatenate(kv_at(s) + kv_at(KV_HEADS - 1) + [q_at(s), q_at(KV_HEADS - 1)], axis=1)
    xz_packet = jnp.concatenate([x_part, z_part, bcdt_cut(w_bcdt, s)], axis=1)
    full_qkv, full_xz = gather_dp([qkv_packet, xz_packet], 1)
    gate_up_packet = jnp.pad(w_gate_up, ((0, 0), (0, 0), (0, UNITS_PAD - UNITS))).reshape(block_rows, -1)
    down_packet = jnp.pad(w_down, ((0, 0), (0, UNITS_PAD - UNITS)))
    d_total = cotangent.astype(FULL) * live
    d_ffn = d_total.astype(LOW)
    d_ffn_far, d_ffn_near = swap(d_ffn, "seq", 2), swap(d_ffn, "seq", 1)
    full_qkv, full_xz, out_cols, gate_up_packet, down_packet, d_ffn_far, d_ffn_near = lax.optimization_barrier(
        (full_qkv, full_xz, out_cols, gate_up_packet, down_packet, d_ffn_far, d_ffn_near)
    )
    d_ffn_group = jnp.concatenate([d_ffn, d_ffn_near, d_ffn_far, swap(d_ffn_far, "seq", 1)])
    full_qkv = full_qkv.reshape(D, -1)
    full_xz = full_xz.reshape(D, -1)
    full_gate_up = gather_dp_apart(gate_up_packet)
    full_down = gather_dp_apart(down_packet)


    own = lambda a: lax.dynamic_slice_in_dim(a, s * rows, rows, 0)
    normed_own = own(normed)
    kvq = mm(normed, full_qkv[:, : 256 + QW]).astype(LOW)
    q_last = mm(normed_own, full_qkv[:, 256 + QW :]).astype(LOW)
    queries = jnp.concatenate([kvq[:, 256:], q_last])
    kv = kvq[:, :256]
    attended, logs = attention_forward(doc_lengths, queries, kv, rows)
    o_cols = out_cols[:, :block_rows].reshape(D, -1)
    mamba_cols = out_cols[:, block_rows:].reshape(INNER, -1)

    def rows_for(peer):
        cut = channel_cut(mamba_cols, peer, 0)
        heads = lax.dynamic_slice_in_dim(o_cols, peer * QW, QW, 0)
        spare = lambda n: jnp.zeros((n, cut.shape[1]), LOW)
        return jnp.concatenate(
            [cut, spare(O_AT - LOCAL_CH), heads, spare(O5_AT - O_AT - QW), o_cols[(KV_HEADS - 1) * QW :]]
        )

    out_pieces = [rows_for(s)] + [swap(rows_for(s ^ bit), "seq", bit) for bit in (1, 2, 3)]
    out_rows = lax.optimization_barrier(wide_of(after(out_pieces, attended)))
    w_out_rows = out_rows[:WIDE]
    w_o_rows = out_rows[O_AT : O_AT + QW]
    w_o5_rows = out_rows[O5_AT:]
    attn_part = mm(attended[:group], w_o_rows).astype(LOW)
    normed_now, attn_part = lax.optimization_barrier((normed, attn_part))
    attn_keep, attn_got = scatter_begin(attn_part)

    xzb = mm(normed_now, full_xz)
    attn_held, attn_far = scatter_far(attn_keep, after(attn_got, xzb))
    xzb, attn_held = lax.optimization_barrier((xzb, attn_held))
    conv_rows = jnp.pad(channel_cut(full_conv, s, 1), ((0, 4), (0, WIDE - LOCAL_CH)))
    rate_row = jnp.pad(own_cut(ssm_rate, s, 0, 1), (STEP_AT, 128 - STEP_AT - LOCAL_HEADS))
    rate_row = jnp.broadcast_to(rate_row, (8, 128))
    skip_row = jnp.pad(jnp.repeat(own_cut(ssm_skip, s, 0, 1), SSM_HEAD), (0, WIDE - LOCAL_CH))
    skip_row = jnp.broadcast_to(skip_row, (8, WIDE))
    mamba_in = (doc_lengths, xzb, conv_rows, rate_row, skip_row)
    gated, read, states = mamba_forward(*mamba_in)
    gated, attn_far = meet(gated, attn_far)
    ssm_held, ssm_far = scatter_far(*scatter_begin(mm(gated, w_out_rows)))
    attn_o = scatter_end(attn_held, attn_far) + mm(attended[group:], w_o5_rows)
    ssm_o = scatter_end(ssm_held, ssm_far)

    inputs_x = tokens_in.astype(FULL)
    (residual, normed_two), pull_join = jax.vjp(join_tail, inputs_x, attn_o, ssm_o, gains)
    normed_two, d_act = seq_arrivals(normed_two.astype(LOW), mm(d_ffn_group, full_down))
    normed_two = jnp.concatenate(normed_two)
    gate_up = mm(normed_two, full_gate_up)
    ffn_gate, ffn_up = gate_up[:, :UNITS_PAD], gate_up[:, UNITS_PAD:]
    ffn_act = (jax.nn.silu(ffn_gate) * ffn_up).astype(LOW)

    sig = jax.nn.sigmoid(ffn_gate)
    d_gate = d_act * ffn_up * (sig * (1.0 + ffn_gate * (1.0 - sig)))
    d_up = d_act * ffn_gate * sig
    d_gate_up = jnp.concatenate([d_gate.astype(LOW), d_up.astype(LOW)], axis=1)
    two_keep, two_got = relative_begin(mm_nt(d_gate_up, full_gate_up))
    two_got, grad_down_part = meet(two_got, mm_tn(d_ffn_group, ffn_act).astype(LOW))
    two_held, two_far = relative_far(two_keep, two_got)
    two_far, grad_gate_up_part = meet(two_far, mm_tn(normed_two, d_gate_up).astype(LOW))
    d_normed_two = scatter_end(two_held, two_far)
    grad_gate_up_sum = scatter_dp_apart(grad_gate_up_part)
    grad_down_sum = scatter_dp_apart(grad_down_part)
    grad_gate_up = grad_gate_up_sum.reshape(block_rows, 2, UNITS_PAD)[:, :, :UNITS]
    grad_down = grad_down_sum[:, :UNITS]

    d_x_tail, d_attn_o, d_ssm_o, d_gains = pull_join((d_total, d_normed_two))
    ssm_arrivals, ffn_part = seq_arrivals(d_ssm_o.astype(LOW), mm_nt(ffn_act, full_down).astype(LOW))
    d_attn_own = after(d_attn_o.astype(LOW), ssm_arrivals[2])
    attn_near, attn_away = swap(d_attn_own, "seq", 1), swap(d_attn_own, "seq", 2)
    d_ssm = place(list(zip(seq_order(), ssm_arrivals))).reshape(group, D)
    d_gated = mm_nt(d_ssm, w_out_rows).astype(LOW)

    def send_columns(grad):
        width = D // SEQ
        blocks = [grad[:, width * j : width * (j + 1)] for j in range(SEQ)]
        return [with_layout_constraint(pick(blocks, s ^ k), Layout((0, 1))) for k in range(SEQ)]

    def trade(blocks):
        return blocks[:1] + [swap(blocks[bit], "seq", bit) for bit in (1, 2, 3)]

    mamba_blocks, d_gated = meet(send_columns(mm_tn(gated, d_ssm).astype(LOW)), d_gated)
    mamba_pieces = trade(mamba_blocks)
    (mamba_pieces[1], attn_near), d_gated = meet((mamba_pieces[1], attn_near), d_gated)
    d_xzb, d_chan, d_rate = mamba_backward(*mamba_in, states, read, d_gated)
    (mamba_pieces[2:], attn_away), d_xzb = meet((mamba_pieces[2:], attn_away), d_xzb)
    ffn_keep, ffn_got = relative_begin(ffn_part)
    attn_arrivals = [d_attn_own, attn_near, attn_away, swap(attn_away, "seq", 1)]
    arrived = place(list(zip(seq_order(), mamba_pieces)))
    grad_out_part = jnp.concatenate(
        [arrived[j, : HEAD_COUNT[j] * SSM_HEAD] for j in range(SEQ)]
    ).reshape(dp_total, out_block, -1)

    d_attn = place(list(zip(seq_order(), attn_arrivals))).reshape(group, D)
    d_attended = jnp.concatenate([mm_nt(d_attn, w_o_rows), mm_nt(d_attn_own, w_o5_rows)]).astype(LOW)
    head_blocks = send_columns(
        jnp.concatenate([mm_tn(attended[:group], d_attn), mm_tn(attended[group:], d_attn_own)]).astype(LOW)
    )
    head_blocks, d_attended = meet(head_blocks, d_attended)
    head_pieces = trade(head_blocks)
    ffn_got, d_attended = meet(ffn_got, d_attended)
    ffn_held, ffn_far = relative_far(ffn_keep, ffn_got)
    ffn_held, d_attended = meet(ffn_held, d_attended)
    d_conv = d_chan[:CONV, :LOCAL_CH]
    d_skip = jnp.sum(d_chan[CONV, :LOCAL_CH].reshape(LOCAL_HEADS, SSM_HEAD), axis=1)
    d_rate = d_rate[0, STEP_AT : STEP_AT + LOCAL_HEADS]
    grad_xz_part = mm_tn(normed, d_xzb).astype(LOW).reshape(dp_total, block_rows, -1)

    d_queries, d_kv, (grad_xz_sum, grad_out) = attention_backward(
        doc_lengths, queries, kv, attended, logs, d_attended, rows, [grad_xz_part, grad_out_part], 3
    )
    (head_pieces, ffn_far), d_queries = meet((head_pieces, ffn_far), d_queries)
    mixed_out = ((residual + scatter_end(ffn_held, ffn_far)) * live).astype(LOW)
    arrived = place(list(zip(seq_order(), head_pieces)))
    grad_o_part = jnp.concatenate(
        [arrived[j, :QW] for j in range(SEQ)] + [jnp.sum(arrived[:, QW:].astype(FULL), axis=0).astype(LOW)]
    ).reshape(dp_total, block_rows, -1)
    d_kvq = jnp.concatenate([d_kv, d_queries[:group]], axis=1)
    d_q_last = d_queries[group:]
    grad_qkv_part = jnp.concatenate(
        [mm_tn(normed, d_kvq).astype(LOW), mm_tn(normed_own, d_q_last).astype(LOW)], axis=1
    ).reshape(dp_total, block_rows, -1)
    d_normed_part = mm_nt(d_xzb, full_xz) + mm_nt(d_kvq, full_qkv[:, : 256 + QW])
    d_normed_own = mm_nt(d_q_last, full_qkv[:, 256 + QW :])

    tokens_wide = tokens_group.astype(FULL)
    unit = tokens_wide * lax.rsqrt(jnp.mean(tokens_wide * tokens_wide, axis=-1, keepdims=True) + NORM_EPS)
    d_gain_first = jnp.sum(d_normed_part * unit, axis=0) + jnp.sum(d_normed_own * own(unit), axis=0)
    d_gains = d_gains.at[0].add(d_gain_first)
    by_dp = lambda a: a.reshape(a.shape[0], dp_total, -1).transpose(1, 0, 2)
    d_heads = jnp.concatenate([own_spread(d_rate, s, 1), own_spread(d_skip, s, 1)])[None]
    small_part = jnp.concatenate(
        [
            jnp.pad(by_dp(own_spread(d_conv, s, SSM_HEAD)), ((0, 0), (0, 0), (0, width - conv_block))),
            jnp.pad(by_dp(d_gains), ((0, 0), (0, 0), (0, width - gains_block))),
            jnp.broadcast_to(
                jnp.pad(d_heads, ((0, 7), (0, width - d_heads.shape[1])))[None], (dp_total, 8, width)
            ),
        ],
        axis=1,
    )
    normed_keep, normed_got = scatter_begin(d_normed_part)
    normed_got, grad_qkv_part = meet(normed_got, grad_qkv_part)
    normed_held, normed_far = scatter_far(normed_keep, normed_got)
    grad_o_part, normed_held = meet(grad_o_part, normed_held)
    grad_qkv_sum, grad_o, small_sum = scatter_dp([grad_qkv_part, grad_o_part, small_part], 2)
    normed_far, small_sum = meet(normed_far, small_sum)
    small_sum = small_sum + swap(small_sum, "seq", 1)
    small_sum = small_sum + swap(small_sum, "seq", 2)
    grad_xz_sum = grad_xz_sum.astype(LOW)
    first, last = trade_back(grad_xz_sum[:, :LOCAL_CH], grad_xz_sum[:, LOCAL_CH : 2 * LOCAL_CH])
    grad_xz = jnp.concatenate([first, last], axis=1)[:, : w_xz.shape[1]].astype(FULL)
    both_all = gather_seq(jnp.concatenate([grad_qkv_sum.astype(LOW), grad_xz_sum[:, 2 * LOCAL_CH :]], axis=1))
    bcdt_all = both_all[:, :, grad_qkv_sum.shape[1] :].astype(FULL)
    grad_bcdt = jnp.concatenate(
        [jnp.sum(bcdt_all[:, :, : 2 * STATE], axis=0)]
        + [bcdt_all[j, :, 2 * STATE : 2 * STATE + HEAD_COUNT[j]] for j in range(SEQ)],
        axis=1,
    )
    qkv_all = both_all[:, :, : grad_qkv_sum.shape[1]].astype(FULL)
    col = lambda j, at, width: qkv_all[j, :, at : at + width]
    shared = lambda at, width: jnp.sum(qkv_all[:, :, at : at + width], axis=0)
    grad_qkv_wide = jnp.concatenate(
        [col(j, 256, QW) for j in range(SEQ)]
        + [shared(256 + QW, QW)]
        + [col(j, 0, HEAD) for j in range(SEQ)]
        + [shared(128, HEAD)]
        + [col(j, HEAD, HEAD) for j in range(SEQ)]
        + [shared(128 + HEAD, HEAD)],
        axis=1,
    )
    qkv_width = w_qkv.shape[1]
    grad_qkv = lax.dynamic_slice_in_dim(grad_qkv_wide, s * qkv_width, qkv_width, 1)

    d_normed = scatter_end(normed_held, normed_far) + d_normed_own
    d_unit = d_normed * gains[0]
    scale = lax.rsqrt(jnp.mean(inputs_x * inputs_x, axis=-1, keepdims=True) + NORM_EPS)
    d_x_head = scale * (
        d_unit - inputs_x * scale * scale * jnp.mean(d_unit * inputs_x, axis=-1, keepdims=True)
    )
    input_grad = (d_x_tail + d_x_head).astype(LOW)
    grad_conv = small_sum[:CONV, :conv_block]
    grad_gains = small_sum[CONV : CONV + 4, :gains_block]
    grad_rate = small_sum[8, :SSM_HEADS]
    grad_skip = small_sum[8, SSM_HEADS : 2 * SSM_HEADS]
    return (
        mixed_out,
        input_grad,
        grad_gains,
        grad_qkv,
        grad_o,
        grad_xz,
        grad_bcdt,
        grad_conv,
        grad_rate,
        grad_skip,
        grad_out,
        grad_gate_up,
        grad_down,
    )


def solution(mesh):
    placed = (
        P(("dp", "seq"), None),
        P("dp", None),
        P(None, "dp"),
        P("dp", "seq"),
        P("dp", "seq"),
        P("dp", "seq"),
        P("dp", None),
        P(None, "dp"),
        P(),
        P(),
        P("dp", "seq"),
        P("dp", None, "seq"),
        P("dp", "seq"),
        P(("dp", "seq"), None),
    )
    return jax.shard_map(
        on_device,
        mesh=mesh,
        in_specs=placed,
        out_specs=(
            P(("dp", "seq"), None),
            P(("dp", "seq"), None),
            P(None, "dp"),
            P("dp", "seq"),
            P("dp", "seq"),
            P("dp", "seq"),
            P("dp", None),
            P(None, "dp"),
            P(),
            P(),
            P("dp", "seq"),
            P("dp", None, "seq"),
            P("dp", "seq"),
        ),
        check_vma=False,
    )
```

```python
import jax
import jax.numpy as jnp
from jax import lax
from jax.experimental import pallas as pl
from jax.experimental.layout import Layout, with_layout_constraint
from jax.experimental.pallas import tpu as pltpu
from jax.sharding import PartitionSpec as P

D = 1600
HEADS = 25
KV_HEADS = 5
HEAD = 64
INNER = 3200
SSM_HEAD = 64
STATE = 16
CONV = 4
FF = 5504
WINDOW = 1024
SSM_HEADS = 50

NORM_EPS = 1e-05
MASKED = -1e30
LOW = jnp.bfloat16
FULL = jnp.float32

SEQ = 4
GROUP_HEADS = HEADS // KV_HEADS
QW = GROUP_HEADS * HEAD
LOCAL_HEADS = 13
LOCAL_CH = LOCAL_HEADS * SSM_HEAD
CHUNK = 128
UNITS = FF // SEQ
UNITS_PAD = 1408
BCDT_PAD = 128
OUT_AT, O_AT, O5_AT, OUT_WIDTH = 0, 896, 1280, 1600
FIRST_HEAD = tuple((SSM_HEADS * s // 2 + 1) // 2 for s in range(SEQ))
HEAD_COUNT = tuple(b - a for a, b in zip(FIRST_HEAD, FIRST_HEAD[1:] + (SSM_HEADS,)))


def swap(value, axis, bit):
    return lax.ppermute(value, axis, [(i, i ^ bit) for i in range(lax.axis_size(axis))])


def place_kernel(count, index_ref, *refs):
    blocks, stacked, held, in_sems, out_sems = refs[:count], *refs[count:]
    loads = [
        pltpu.make_async_copy(block, held.at[i], in_sems.at[i]) for i, block in enumerate(blocks)
    ]
    stores = [
        pltpu.make_async_copy(held.at[i], stacked.at[index_ref[i]], out_sems.at[i])
        for i in range(count)
    ]
    for load in loads:
        load.start()
    for load, store in zip(loads, stores):
        load.wait()
        store.start()
    for store in stores:
        store.wait()


def place(blocks):
    count = len(blocks)
    block = blocks[0][1]
    anywhere = pl.BlockSpec(memory_space=pl.ANY)
    return pl.pallas_call(
        lambda *refs: place_kernel(count, *refs),
        out_shape=jax.ShapeDtypeStruct((count,) + block.shape, block.dtype),
        grid_spec=pltpu.PrefetchScalarGridSpec(
            num_scalar_prefetch=1,
            grid=(1,),
            in_specs=[anywhere] * count,
            out_specs=anywhere,
            scratch_shapes=[
                pltpu.VMEM((count,) + block.shape, block.dtype),
                pltpu.SemaphoreType.DMA((count,)),
                pltpu.SemaphoreType.DMA((count,)),
            ],
        ),
        compiler_params=pltpu.CompilerParams(vmem_limit_bytes=32 << 20),
        cost_estimate=pl.CostEstimate(
            flops=0, bytes_accessed=2 * count * block.size * block.dtype.itemsize, transcendentals=0
        ),
    )(jnp.stack([jnp.asarray(i, jnp.int32) for i, _ in blocks]), *[b for _, b in blocks])


def seq_order():
    me = lax.axis_index("seq")
    return [me, me ^ 1, me ^ 2, me ^ 3]


def seq_arrivals(block, beside=None):
    far, near = swap(block, "seq", 2), swap(block, "seq", 1)
    if beside is not None:
        far, beside = meet(far, beside)
    blocks = [block, near, far, swap(far, "seq", 1)]
    return blocks if beside is None else (blocks, beside)


def gather_seq(block):
    return place(list(zip(seq_order(), seq_arrivals(block))))


def scatter_begin(part):
    core = lax.axis_index("seq") % 2
    part = with_layout_constraint(part.astype(LOW), Layout((0, 1)))
    by_core = part.reshape((2, 2, part.shape[0] // SEQ) + part.shape[1:])
    give = lax.dynamic_index_in_dim(by_core, 1 - core, 1, False)
    keep = lax.dynamic_index_in_dim(by_core, core, 1, False)
    return keep, swap(give, "seq", 1)


def scatter_far(keep, got):
    far = lax.axis_index("seq") // 2
    at = lambda a, i: lax.dynamic_index_in_dim(a, i, 0, False).astype(FULL)
    give_far = (at(keep, 1 - far) + at(got, 1 - far)).astype(LOW)
    return at(keep, far) + at(got, far), swap(give_far, "seq", 2)


def scatter_end(held, got_far):
    return held + got_far.astype(FULL)


def relative_begin(part):
    part = with_layout_constraint(part.astype(LOW), Layout((0, 1)))
    rows = part.shape[0] // SEQ
    block = lambda k: part[rows * k : rows * (k + 1)]
    got = swap(jnp.concatenate([block(1), block(3)]), "seq", 1)
    return (block(0), block(2)), got


def relative_far(keep, got):
    rows = got.shape[0] // 2
    add = lambda k: keep[k].astype(FULL) + got[rows * k : rows * (k + 1)].astype(FULL)
    return add(0), swap(add(1).astype(LOW), "seq", 2)


def meet(one, two):
    return lax.optimization_barrier((one, two))


def after(values, done):
    return lax.optimization_barrier((values, done))[0]


def line_place():
    me = lax.axis_index("dp")
    return lax.axis_size("dp") // 2, me // 2, lax.rem(me, 2)


def greet(line, z, x):
    barrier = pltpu.get_barrier_semaphore()

    def signal(target):
        pl.semaphore_signal(
            barrier, inc=1, device_id={"dp": target}, device_id_type=pl.DeviceIdType.MESH
        )

    signal(2 * z + 1 - x)
    pl.when(z > 0)(lambda: signal(2 * (z - 1) + x))
    pl.when(z < line - 1)(lambda: signal(2 * (z + 1) + x))
    pl.semaphore_wait(
        barrier, 1 + (z > 0).astype(jnp.int32) + (z < line - 1).astype(jnp.int32)
    )


def pieces_of(arrays, axis):
    pieces = []
    for i, array in enumerate(arrays):
        rows = array.shape[axis]
        count = 1 if rows < 64 else 3 if rows < 256 else 4
        size = rows // count // 16 * 16 if count > 1 else rows
        for k in range(count):
            pieces.append((i, pl.ds(k * size, size if k < count - 1 else rows - k * size)))
    return pieces


def gather_phases(pieces, line, refs):
    packets = pieces[-1][0] + 1
    sources, outs = refs[:packets], refs[packets : 2 * packets]
    own_sem, up_sem, down_sem, line_sem, give_sem, got_sem = refs[2 * packets :]
    _, z, x = line_place()
    held = lambda i, zb: outs[pieces[i][0]].at[2 * zb + x, pieces[i][1]]
    mine = lambda i: sources[pieces[i][0]].at[pieces[i][1]]

    def copy(src, i, zb, send_sem, recv_sem, target):
        return pltpu.make_async_remote_copy(
            src_ref=src,
            dst_ref=held(i, zb),
            send_sem=send_sem.at[i, zb],
            recv_sem=recv_sem.at[i, zb],
            device_id={"dp": target},
            device_id_type=pl.DeviceIdType.MESH,
        )

    up_to = lambda src, i, zb: copy(src, i, zb, up_sem, line_sem, 2 * (z + 1) + x)
    down_to = lambda src, i, zb: copy(src, i, zb, down_sem, line_sem, 2 * (z - 1) + x)
    give = lambda src, i, zb: copy(src, i, zb, give_sem, got_sem, 2 * z + 1 - x)
    own = lambda i: pltpu.make_async_copy(mine(i), held(i, z), own_sem.at[i])

    def take_turn(turn):
        if turn == 0:
            greet(line, z, x)
        for i in range(len(pieces)):
            far = turn - i
            if far == 0:
                pl.when(z < line - 1)(lambda: up_to(mine(i), i, z).start())
                pl.when(z > 0)(lambda: down_to(mine(i), i, z).start())
                give(mine(i), i, z).start()
                own(i).start()
            elif 0 < far < line:

                @pl.when(z - far >= 0)
                def _():
                    zb = z - far
                    up_to(held(i, zb), i, zb).wait_recv()
                    pl.when(z < line - 1)(lambda: up_to(held(i, zb), i, zb).start())
                    give(held(i, zb), i, zb).start()

                @pl.when(z + far < line)
                def _():
                    zb = z + far
                    down_to(held(i, zb), i, zb).wait_recv()
                    pl.when(z > 0)(lambda: down_to(held(i, zb), i, zb).start())
                    give(held(i, zb), i, zb).start()

    def finish():
        for i in range(len(pieces)):
            own(i).wait()
            for zb in range(line):
                give(held(i, zb), i, zb).wait()
                pl.when((zb <= z) & (z < line - 1))(lambda: up_to(held(i, zb), i, zb).wait_send())
                pl.when((zb >= z) & (z > 0))(lambda: down_to(held(i, zb), i, zb).wait_send())

    turns = len(pieces) + line - 1
    return [lambda turn=turn: take_turn(turn) for turn in range(turns)] + [finish]


def gather_kernel(pieces, line, *refs):
    for phase in gather_phases(pieces, line, refs):
        phase()


def gather_scratch(pieces, line):
    count = len(pieces)
    sems = lambda *shape: pltpu.SemaphoreType.DMA(shape)
    return [sems(count)] + [sems(count, line) for _ in range(5)]


def gather_shapes(packets):
    return [jax.ShapeDtypeStruct((lax.axis_size("dp"),) + p.shape, p.dtype) for p in packets]


def gather_dp(packets, collective_id):
    total = lax.axis_size("dp")
    if total != 8:
        return [lax.all_gather(packet, "dp", axis=0) for packet in packets]
    pieces, line = pieces_of(packets, 0), total // 2
    return pl.pallas_call(
        lambda *refs: gather_kernel(pieces, line, *refs),
        out_shape=gather_shapes(packets),
        in_specs=[pl.BlockSpec(memory_space=pltpu.VMEM)] * len(packets),
        out_specs=[pl.BlockSpec(memory_space=pl.ANY)] * len(packets),
        scratch_shapes=gather_scratch(pieces, line),
        compiler_params=pltpu.CompilerParams(
            collective_id=collective_id, has_side_effects=True, vmem_limit_bytes=32 << 20
        ),
        cost_estimate=pl.CostEstimate(
            flops=0,
            bytes_accessed=2 * total * sum(p.size * p.dtype.itemsize for p in packets),
            transcendentals=0,
        ),
    )(*packets)


def add_columns(total, parts):
    width = total.shape[-1]
    step = 128 if width % 256 else 256

    def columns(c):
        at = pl.ds(pl.multiple_of(c * step, step), step)
        total[:, at] = sum(part[:, at].astype(FULL) for part in parts).astype(total.dtype)

    pl.loop(0, width // step)(columns)
    if width % step:
        at = slice(width // step * step, width)
        total[:, at] = sum(part[:, at].astype(FULL) for part in parts).astype(total.dtype)


def scatter_phases(pieces, line, refs):
    count = pieces[-1][0] + 1
    parts, outs = refs[:count], refs[count : 2 * count]
    own_refs, near_refs, line_refs = (
        refs[2 * count : 3 * count],
        refs[3 * count : 4 * count],
        refs[4 * count : 5 * count],
    )
    load_sem, give_sem, got_sem, send_sem, line_sem = refs[5 * count :]
    _, z, x = line_place()
    order = [t for pair in zip(range(line - 1, -1, -1), range(line)) for t in pair][:line]
    at = lambda arrays, i, t: arrays[pieces[i][0]].at[t, pieces[i][1]]
    remote = lambda src, dst, send, recv, target: pltpu.make_async_remote_copy(
        src_ref=src,
        dst_ref=dst,
        send_sem=send,
        recv_sem=recv,
        device_id={"dp": target},
        device_id_type=pl.DeviceIdType.MESH,
    )
    give = lambda i, t: remote(
        at(parts, i, 2 * t + 1 - x),
        at(near_refs, i, t),
        give_sem.at[i, t],
        got_sem.at[i, t],
        2 * z + 1 - x,
    )
    load = lambda i, t: pltpu.make_async_copy(
        at(parts, i, 2 * t + x), at(own_refs, i, t), load_sem.at[i, t]
    )
    along = lambda i, t, slot, target: remote(
        at(own_refs, i, t), at(line_refs, i, slot), send_sem.at[i, t], line_sem.at[i, slot], target
    )
    def views(i):
        return [lambda t, arrays=arrays: at(arrays, i, t) for arrays in (own_refs, near_refs, line_refs)]

    def start():
        greet(line, z, x)
        for i in range(len(pieces)):
            for t in order:
                load(i, t).start()
                give(i, t).start()

    def pass_on(i, t, zz):
        own, near, held = views(i)
        load(i, t).wait()
        give(i, t).wait_recv()
        terms = [own(t), near(t)]
        if 0 < zz < t or t < zz < line - 1:
            along(i, t, t, 0).wait_recv()
            terms.append(held(t))
        add_columns(own(t), terms)
        step = 1 if t > zz else -1
        along(i, t, line if t == zz - 1 else t, 2 * (zz + step) + x).start()

    def take_round(r):
        for zz in range(line):

            @pl.when(z == zz)
            def _():
                up, down = r - zz, r - (line - 1 - zz)
                for t in range(line - 1, zz, -1):
                    if 0 <= up < len(pieces):
                        pass_on(up, t, zz)
                for t in range(zz):
                    if 0 <= down < len(pieces):
                        pass_on(down, t, zz)

    def finish():
        for i in range(len(pieces)):
            own, near, held = views(i)
            for t in range(line):

                @pl.when(t == z)
                def _():
                    load(i, t).wait()
                    give(i, t).wait_recv()
                    terms = [own(t), near(t)]
                    if t > 0:
                        along(i, t, t, 0).wait_recv()
                        terms.append(held(t))
                    if t < line - 1:
                        along(i, t, line, 0).wait_recv()
                        terms.append(held(line))
                    add_columns(outs[pieces[i][0]].at[pieces[i][1]], terms)

                pl.when(t != z)(lambda: along(i, t, t, 0).wait_send())
                give(i, t).wait_send()

    rounds = len(pieces) + line - 2
    return [start] + [lambda r=r: take_round(r) for r in range(rounds)] + [finish]


def scatter_kernel(pieces, line, *refs):
    for phase in scatter_phases(pieces, line, refs):
        phase()


def scatter_scratch(parts, pieces, line):
    count = len(pieces)
    sems = lambda *shape: pltpu.SemaphoreType.DMA(shape)
    buffers = [pltpu.VMEM((n,) + p.shape[1:], p.dtype) for n in (line, line, line + 1) for p in parts]
    return buffers + [sems(count, line) for _ in range(4)] + [sems(count, line + 1)]


def scatter_dp(parts, collective_id):
    total = lax.axis_size("dp")
    if total != 8:
        sums = [lax.psum_scatter(p, "dp", scatter_dimension=0) for p in parts]
        return [lax.optimization_barrier(p).astype(FULL) for p in sums]
    pieces, line = pieces_of(parts, 1), total // 2
    return pl.pallas_call(
        lambda *refs: scatter_kernel(pieces, line, *refs),
        out_shape=[jax.ShapeDtypeStruct(p.shape[1:], FULL) for p in parts],
        in_specs=[pl.BlockSpec(memory_space=pl.ANY)] * len(parts),
        out_specs=[pl.BlockSpec(memory_space=pltpu.VMEM)] * len(parts),
        scratch_shapes=scatter_scratch(parts, pieces, line),
        compiler_params=pltpu.CompilerParams(
            collective_id=collective_id, has_side_effects=True, vmem_limit_bytes=56 << 20
        ),
        cost_estimate=pl.CostEstimate(
            flops=0, bytes_accessed=sum(p.size * 2 for p in parts), transcendentals=0
        ),
    )(*parts)


def gather_dp_apart(packet):
    return lax.all_gather(packet, "dp", axis=0, tiled=True)


def scatter_dp_apart(parts):
    summed = lax.psum_scatter(parts.astype(LOW), "dp", scatter_dimension=0, tiled=True)
    return lax.optimization_barrier(summed).astype(FULL)


def trade_halves(first, last):
    me = lax.axis_index("seq")
    one = lax.ppermute(jnp.where(me == 0, last, first), "seq", [(0, 1), (1, 2), (2, 0)])
    two = lax.ppermute(jnp.where(me == 3, first, last), "seq", [(1, 3), (2, 1), (3, 2)])
    return pick([first, one, one, two], me), pick([one, two, two, last], me)


def trade_back(x_part, z_part):
    me = lax.axis_index("seq")
    one = lax.ppermute(jnp.where(me == 0, z_part, x_part), "seq", [(1, 0), (2, 1), (0, 2)])
    two = lax.ppermute(jnp.where(me == 3, x_part, z_part), "seq", [(3, 1), (1, 2), (2, 3)])
    return pick([x_part, one, one, two], me), pick([one, two, two, z_part], me)


def mm(left, right):
    return jnp.dot(left, right, preferred_element_type=FULL)


def mm_nt(left, right):
    return lax.dot_general(left, right, (((1,), (1,)), ((), ())), preferred_element_type=FULL)


def mm_tn(left, right):
    return lax.dot_general(left, right, (((0,), (0,)), ((), ())), preferred_element_type=FULL)


def rms_norm(values, gain):
    return values * lax.rsqrt(jnp.mean(values * values, axis=-1, keepdims=True) + NORM_EPS) * gain


def norm_rows_kernel(values_ref, gain_ref, out_ref):
    out_ref[...] = rms_norm(values_ref[...].astype(FULL), gain_ref[0:1]).astype(LOW)


def norm_rows(values, gain):
    rows, width = values.shape
    block = rows // SEQ
    by_block = pl.BlockSpec((block, width), lambda i: (i, 0))
    return pl.pallas_call(
        norm_rows_kernel,
        grid=(SEQ,),
        in_specs=[by_block, pl.BlockSpec((8, width), lambda i: (0, 0))],
        out_specs=by_block,
        out_shape=jax.ShapeDtypeStruct(values.shape, LOW),
        cost_estimate=pl.CostEstimate(flops=4 * values.size, bytes_accessed=4 * values.size, transcendentals=rows),
    )(values, jnp.broadcast_to(gain, (8, width)))


def join_tail(inputs_x, attn_o, ssm_o, gains):
    residual = inputs_x + 0.5 * (rms_norm(attn_o, gains[1]) + rms_norm(ssm_o, gains[2]))
    return (residual, rms_norm(residual, gains[3]))


STEP_AT = 2 * STATE
WIDE = 896
PAIRS = WIDE // 128
XZB = 1792


def dot_any(left, right, contract):
    return lax.dot_general(
        left, right, ((contract[:1], contract[1:]), ((), ())), preferred_element_type=FULL
    )


def low_dot(left, right, contract):
    return dot_any(left.astype(LOW), right.astype(LOW), contract)


def iota(shape, axis):
    return lax.broadcasted_iota(jnp.int32, shape, axis)


def pair_spread(values):
    rows = values.shape[0]
    low_half = iota((rows, 128), 1) < SSM_HEAD
    tiles = []
    for p in range(PAIRS):
        one = values[:, STEP_AT + 2 * p : STEP_AT + 2 * p + 1]
        two = values[:, STEP_AT + 2 * p + 1 : STEP_AT + 2 * p + 2]
        tiles.append(
            jnp.where(
                low_half,
                jnp.broadcast_to(one, (rows, 128)),
                jnp.broadcast_to(two, (rows, 128)),
            )
        )
    return jnp.concatenate(tiles, axis=1)


def halves(tile):
    low_half = iota(tile.shape, 1) < SSM_HEAD
    zero = jnp.zeros_like(tile)
    return jnp.concatenate([jnp.where(low_half, tile, zero), jnp.where(low_half, zero, tile)], axis=0)


def mamba_chunk(c, lengths_ref, xzb_ref, tail_ref, conv_ref, rate_ref, pad_ref):
    first_end = lengths_ref[0, 0]
    second_end = first_end + lengths_ref[0, 1]
    doc_of = lambda pos: (pos >= first_end).astype(jnp.int32) + (pos >= second_end).astype(jnp.int32)
    base = c * CHUNK
    square = (CHUNK, CHUNK)
    row, lane = iota(square, 0), iota(square, 1)
    doc_row = doc_of(base + row)
    doc_lane = doc_of(base + lane)
    before = jnp.where(c > 0, doc_of(base - 1), -1)
    end = doc_of(base + CHUNK - 1)
    causal = (row >= lane) & (doc_row == doc_lane)
    channel = iota((CHUNK, WIDE), 1) < LOCAL_CH

    raw = jnp.where(channel, xzb_ref[:, :WIDE], 0.0).astype(LOW).astype(FULL)
    gate = pltpu.roll(xzb_ref[:, LOCAL_CH - 64 :], XZB - LOCAL_CH, 1)[:, :WIDE]
    gate = jnp.where(channel, gate, 0.0)
    pad_ref[0:8] = tail_ref[:, :WIDE].astype(LOW).astype(FULL)
    pad_ref[8 : 8 + CHUNK] = raw
    taps = []
    pos = base + iota((CHUNK, 1), 0)
    conv = jnp.zeros((CHUNK, WIDE), FULL)
    for k in range(CONV):
        back = CONV - 1 - k
        same = (doc_of(pos) == doc_of(pos - back)) & (pos >= back)
        shifted = jnp.where(same, pad_ref[8 - back : 8 - back + CHUNK], 0.0)
        taps.append(shifted)
        conv = conv + conv_ref[k : k + 1] * shifted
    conv_sig = jax.nn.sigmoid(conv)
    act = conv * conv_sig

    bc = xzb_ref[:, 2 * LOCAL_CH :]
    b_in = jnp.where(lane < STATE, bc, 0.0)
    c_at = jnp.where((lane >= STATE) & (lane < 2 * STATE), bc, 0.0)
    c_in = pltpu.roll(c_at, CHUNK - STATE, 1)
    step = jnp.maximum(bc, 0.0) + jnp.log(1.0 + jnp.exp(-jnp.abs(bc)))
    lower = (row >= lane).astype(FULL)
    log = lax.dot_general(
        lower,
        -step * rate_ref[0:1],
        (((1,), (0,)), ((), ())),
        precision=lax.Precision.HIGHEST,
        preferred_element_type=FULL,
    )
    last = log[CHUNK - 1 : CHUNK]
    ends = jnp.where(doc_row == end, jnp.exp(last - log), 0.0)
    reach = jnp.where(doc_row == before, jnp.exp(log), 0.0)
    carry = jnp.where(end == before, jnp.exp(last), 0.0)
    gram = low_dot(c_in, b_in, (1, 1))
    log_t = log.T

    def decays(h):
        gap = log[:, STEP_AT + h : STEP_AT + h + 1] - log_t[STEP_AT + h : STEP_AT + h + 1]
        return jnp.exp(jnp.where(causal, gap, MASKED))

    step_wide = pair_spread(step)
    return dict(
        row=row, lane=lane, pos=pos, doc_of=doc_of, gate=gate, taps=taps, conv=conv, conv_sig=conv_sig,
        act=act, bc=bc, b_in=b_in, c_in=c_in, c_at=c_at, step=step, ends=ends, reach=reach,
        carry=carry, gram=gram, decays=decays, step_wide=step_wide, moved=act * step_wide,
    )


def mamba_forward_kernel(
    lengths_ref, xzb_ref, tail_ref, conv_ref, rate_ref, skip_ref, gated_ref, read_ref, states_ref, pad_ref, state_ref
):
    c = pl.program_id(0)

    @pl.when(c == 0)
    def _():
        state_ref[...] = jnp.zeros_like(state_ref)

    v = mamba_chunk(c, lengths_ref, xzb_ref, tail_ref, conv_ref, rate_ref, pad_ref)
    states_ref[0] = state_ref[STATE : 2 * STATE]
    moved = v["moved"]
    from_state = low_dot(v["c_at"], state_ref[...], (1, 0)) * pair_spread(v["reach"])
    tiles = []
    for p in range(PAIRS):
        mixing = jnp.concatenate(
            [(v["decays"](2 * p + j) * v["gram"]).astype(LOW) for j in range(2)], axis=1
        )
        tiles.append(dot_any(mixing, halves(moved[:, 128 * p : 128 * p + 128].astype(LOW)), (1, 0)))
    read = jnp.concatenate(tiles, axis=1) + from_state + skip_ref[0:1] * v["act"]
    read_ref[...] = read.astype(LOW)
    gated_ref[...] = (read * v["gate"] * jax.nn.sigmoid(v["gate"])).astype(LOW)
    added = low_dot(v["b_in"], moved * pair_spread(v["ends"]), (0, 0))[:STATE]
    state_ref[STATE : 2 * STATE] = pair_spread(v["carry"]) * state_ref[STATE : 2 * STATE] + added


def mamba_backward_kernel(
    lengths_ref, xzb_ref, tail_ref, conv_ref, rate_ref, skip_ref, states_ref, read_ref, d_gated_ref,
    d_xzb_ref, d_chan_ref, d_rate_ref, pad_ref, state_ref, d_state_ref, d_pad_ref,
):
    g = pl.program_id(0)
    c = pl.num_programs(0) - 1 - g

    @pl.when(g == 0)
    def _():
        state_ref[...] = jnp.zeros_like(state_ref)
        d_state_ref[...] = jnp.zeros_like(d_state_ref)
        d_pad_ref[...] = jnp.zeros_like(d_pad_ref)
        d_chan_ref[...] = jnp.zeros_like(d_chan_ref)
        d_rate_ref[...] = jnp.zeros_like(d_rate_ref)

    v = mamba_chunk(c, lengths_ref, xzb_ref, tail_ref, conv_ref, rate_ref, pad_ref)
    row, lane, act, moved, gate = v["row"], v["lane"], v["act"], v["moved"], v["gate"]
    state_ref[STATE : 2 * STATE] = states_ref[0]
    by_head = (iota((WIDE, 128), 0) // SSM_HEAD + STEP_AT == iota((WIDE, 128), 1)).astype(LOW)
    head_sum = lambda wide: dot_any(wide.astype(LOW), by_head, (1, 0))

    d_gated = d_gated_ref[...].astype(FULL)
    gate_sig = jax.nn.sigmoid(gate)
    d_read = d_gated * gate * gate_sig
    d_gate = d_gated * read_ref[...].astype(FULL) * gate_sig * (1.0 + gate * (1.0 - gate_sig))
    d_chan_ref[CONV : CONV + 1] += jnp.sum(d_read * act, axis=0, keepdims=True)
    d_act = skip_ref[0:1] * d_read

    d_log = jnp.zeros_like(v["gram"])
    d_log_t = jnp.zeros_like(v["gram"])
    d_gram = jnp.zeros_like(v["gram"])
    tiles = []
    for p in range(PAIRS):
        at = slice(128 * p, 128 * p + 128)
        d_pair = halves(d_read[:, at].astype(LOW))
        d_mixing = dot_any(d_pair, moved[:, at].astype(LOW), (1, 1))
        mixings = []
        for j in range(2):
            h = 2 * p + j
            decay = v["decays"](h)
            mixing = decay * v["gram"]
            d_one = d_mixing[CHUNK * j : CHUNK * (j + 1)]
            d_gram = d_gram + d_one * decay
            d_gap = d_one * mixing
            mixings.append(mixing.astype(LOW))
            d_log = d_log + jnp.where(lane == STEP_AT + h, jnp.sum(d_gap, axis=1, keepdims=True), 0.0)
            d_log_t = d_log_t + jnp.where(row == STEP_AT + h, jnp.sum(d_gap, axis=0, keepdims=True), 0.0)
        tiles.append(dot_any(jnp.concatenate(mixings, axis=0), d_pair, (0, 0)))
    d_moved = jnp.concatenate(tiles, axis=1)
    d_log = d_log - d_log_t.T

    d_product = d_read * pair_spread(v["reach"])
    state_low = state_ref[...].astype(LOW)
    product = dot_any(v["c_at"].astype(LOW), state_low, (1, 0))
    d_log = d_log + head_sum(d_product * product)
    d_c = low_dot(d_product, state_low, (1, 1)) + low_dot(d_gram, pltpu.roll(v["b_in"], STATE, 1), (1, 0))
    d_state_in = low_dot(v["c_at"], d_product, (0, 0))[STATE : 2 * STATE]

    d_state = d_state_ref[...]
    d_state_low = d_state.astype(LOW)
    ends_wide = pair_spread(v["ends"])
    d_put = dot_any(v["b_in"].astype(LOW), d_state_low, (1, 0)) * ends_wide
    d_b = low_dot(moved * ends_wide, d_state_low, (1, 1)) + low_dot(d_gram, v["c_in"], (0, 0))
    d_moved = d_moved + d_put
    d_ends = head_sum(d_put * moved)
    carry_wide = pair_spread(v["carry"])
    d_carry = head_sum(
        jnp.broadcast_to(
            jnp.sum(d_state[:STATE] * states_ref[0], axis=0, keepdims=True) * carry_wide, (16, WIDE)
        )
    )[0:1]
    d_last = jnp.sum(d_ends, axis=0, keepdims=True) + d_carry
    d_log = d_log - d_ends + jnp.where(row == CHUNK - 1, d_last, 0.0)
    d_state_ref[:STATE] = d_state_in + carry_wide * d_state[:STATE]

    d_act = d_act + d_moved * v["step_wide"]
    d_rate_step = lax.dot_general(
        (row >= lane).astype(FULL),
        d_log,
        (((0,), (0,)), ((), ())),
        precision=lax.Precision.HIGHEST,
        preferred_element_type=FULL,
    )
    d_step = head_sum(d_moved * act) - rate_ref[0:1] * d_rate_step
    d_rate_ref[0:1] += jnp.sum(-v["step"] * d_rate_step, axis=0, keepdims=True)
    is_step = (lane >= STEP_AT) & (lane < STEP_AT + LOCAL_HEADS)
    d_bc = d_b + d_c + jnp.where(is_step, d_step * jax.nn.sigmoid(v["bc"]), 0.0)

    d_conv = d_act * v["conv_sig"] * (1.0 + v["conv"] * (1.0 - v["conv_sig"]))
    d_pad_ref[0:CHUNK] = d_conv
    d_raw = jnp.zeros_like(d_conv)
    for k in range(CONV):
        ahead = CONV - 1 - k
        d_chan_ref[k : k + 1] += jnp.sum(d_conv * v["taps"][k], axis=0, keepdims=True)
        same = v["doc_of"](v["pos"]) == v["doc_of"](v["pos"] + ahead)
        d_raw = d_raw + conv_ref[k : k + 1] * jnp.where(same, d_pad_ref[ahead : ahead + CHUNK], 0.0)
    d_pad_ref[CHUNK : CHUNK + 8] = d_conv[0:8]

    moved_gate = pltpu.roll(jnp.concatenate([d_gate, jnp.zeros_like(row).astype(FULL)], axis=1), 64, 1)
    d_xzb_ref[:, : LOCAL_CH - 64] = d_raw[:, : LOCAL_CH - 64].astype(LOW)
    d_xzb_ref[:, LOCAL_CH - 64 : LOCAL_CH + 64] = (
        d_raw[:, LOCAL_CH - 64 :] + moved_gate[:, :128]
    ).astype(LOW)
    d_xzb_ref[:, LOCAL_CH + 64 : 2 * LOCAL_CH] = moved_gate[:, 128:WIDE].astype(LOW)
    d_xzb_ref[:, 2 * LOCAL_CH :] = d_bc.astype(LOW)


def mamba_specs(chunk_of):
    tail = lambda g: (jnp.maximum(chunk_of(g) * (CHUNK // 8) - 1, 0), 0)
    fixed = lambda shape: pl.BlockSpec(shape, lambda g: (0,) * len(shape))
    return [
        pl.BlockSpec(memory_space=pltpu.SMEM),
        pl.BlockSpec((CHUNK, XZB), lambda g: (chunk_of(g), 0)),
        pl.BlockSpec((8, XZB), tail),
        fixed((8, WIDE)),
        fixed((8, 128)),
        fixed((8, WIDE)),
    ]


def mamba_forward(lengths, xzb, conv_rows, rate_row, skip_row):
    total = xzb.shape[0]
    chunks = total // CHUNK
    by_chunk = lambda width: pl.BlockSpec((CHUNK, width), lambda g: (g, 0))
    return pl.pallas_call(
        mamba_forward_kernel,
        grid=(chunks,),
        in_specs=mamba_specs(lambda g: g),
        out_specs=[by_chunk(WIDE), by_chunk(WIDE), pl.BlockSpec((1, STATE, WIDE), lambda g: (g, 0, 0))],
        out_shape=[
            jax.ShapeDtypeStruct((total, WIDE), LOW),
            jax.ShapeDtypeStruct((total, WIDE), LOW),
            jax.ShapeDtypeStruct((chunks, STATE, WIDE), FULL),
        ],
        scratch_shapes=[pltpu.VMEM((8 + CHUNK, WIDE), FULL), pltpu.VMEM((CHUNK, WIDE), FULL)],
        compiler_params=pltpu.CompilerParams(vmem_limit_bytes=32 << 20),
        cost_estimate=pl.CostEstimate(flops=2 * 10**10, bytes_accessed=16 << 20, transcendentals=10**7),
    )(lengths, xzb, xzb, conv_rows, rate_row, skip_row)


def mamba_backward(lengths, xzb, conv_rows, rate_row, skip_row, states, read, d_gated):
    total = xzb.shape[0]
    chunks = total // CHUNK
    chunk_of = lambda g: chunks - 1 - g
    by_chunk = lambda width: pl.BlockSpec((CHUNK, width), lambda g: (chunk_of(g), 0))
    return pl.pallas_call(
        mamba_backward_kernel,
        grid=(chunks,),
        in_specs=mamba_specs(chunk_of)
        + [pl.BlockSpec((1, STATE, WIDE), lambda g: (chunk_of(g), 0, 0)), by_chunk(WIDE), by_chunk(WIDE)],
        out_specs=[
            by_chunk(XZB),
            pl.BlockSpec((8, WIDE), lambda g: (0, 0)),
            pl.BlockSpec((8, 128), lambda g: (0, 0)),
        ],
        out_shape=[
            jax.ShapeDtypeStruct((total, XZB), LOW),
            jax.ShapeDtypeStruct((8, WIDE), FULL),
            jax.ShapeDtypeStruct((8, 128), FULL),
        ],
        scratch_shapes=[
            pltpu.VMEM((8 + CHUNK, WIDE), FULL),
            pltpu.VMEM((CHUNK, WIDE), FULL),
            pltpu.VMEM((CHUNK, WIDE), FULL),
            pltpu.VMEM((8 + CHUNK, WIDE), FULL),
        ],
        compiler_params=pltpu.CompilerParams(vmem_limit_bytes=32 << 20),
        cost_estimate=pl.CostEstimate(flops=6 * 10**10, bytes_accessed=24 << 20, transcendentals=10**7),
    )(lengths, xzb, xzb, conv_rows, rate_row, skip_row, states, read, d_gated)


def head_under(h, at, value):
    row, lane = iota((QW, 128), 0), iota((QW, 128), 1)
    inside = (lane >= at) & (lane < at + HEAD) & (row == h * HEAD + lane - at)
    return jnp.where(inside, value, 0.0).astype(LOW)


def row_block(t):
    return jnp.where(t < SEQ, t, lax.axis_index("seq"))


def allowed_keys(lengths_ref, block, rows, extent):
    first_end = lengths_ref[0, 0]
    second_end = first_end + lengths_ref[0, 1]
    row = block * rows + iota((rows, 1), 0)
    start = jnp.where(row >= second_end, second_end, jnp.where(row >= first_end, first_end, 0))
    least = jnp.maximum(start, row - (WINDOW - 1))
    key = iota((rows, extent), 1)
    return (key >= least) & (key <= row)


def for_extent(block, rows, run):
    for e in range(SEQ):
        pl.when(block == e)(lambda e=e: run((e + 1) * rows))


def attention_forward_kernel(lengths_ref, q_ref, kv_ref, out_ref, log_ref):
    t, h = pl.program_id(0), pl.program_id(1)
    rows = q_ref.shape[0]
    block = row_block(t)

    def run(extent):
        q = dot_any(q_ref[...], head_under(h, 0, HEAD ** (-0.5)), (1, 0)).astype(LOW)
        kv = kv_ref[:extent]
        scores = dot_any(q, kv, (1, 1))
        scores = jnp.where(allowed_keys(lengths_ref, block, rows, extent), scores, MASKED)
        top = jnp.max(scores, axis=1, keepdims=True)
        expos = jnp.exp(scores - top)
        denom = jnp.sum(expos, axis=1, keepdims=True)
        mixed = dot_any((expos * (1.0 / denom)).astype(LOW), kv, (1, 0)).astype(LOW)
        out = dot_any(mixed, head_under(h, HEAD, 1.0), (1, 1)).astype(LOW)
        log = jnp.where(iota((rows, 128), 1) == h, top + jnp.log(denom), 0.0)

        @pl.when(h == 0)
        def _():
            out_ref[...] = out
            log_ref[...] = log

        @pl.when(h > 0)
        def _():
            out_ref[...] += out
            log_ref[...] += log

    for_extent(block, rows, run)


def attention_backward_kernel(
    lengths_ref, q_ref, kv_ref, out_ref, log_ref, d_out_ref, d_q_ref, d_kv_ref, sum_ref
):
    t, h = pl.program_id(0), pl.program_id(1)
    rows = q_ref.shape[0]
    block = row_block(t)

    @pl.when((h == 0) & ((t == 0) | (t == SEQ)))
    def _():
        sum_ref[...] = jnp.zeros_like(sum_ref)

    def run(extent):
        under_q = head_under(h, 0, HEAD ** (-0.5))
        q = dot_any(q_ref[...], under_q, (1, 0)).astype(LOW)
        d_out = dot_any(d_out_ref[...], head_under(h, HEAD, 1.0), (1, 0)).astype(LOW)
        log = jnp.sum(jnp.where(iota((rows, 128), 1) == h, log_ref[...], 0.0), axis=1, keepdims=True)
        own = iota((rows, QW), 1) // HEAD == h
        product = d_out_ref[...].astype(FULL) * out_ref[...].astype(FULL)
        d_total = jnp.sum(jnp.where(own, product, 0.0), axis=1, keepdims=True)
        kv = kv_ref[:extent]
        scores = dot_any(q, kv, (1, 1))
        allowed = allowed_keys(lengths_ref, block, rows, extent)
        probs = jnp.exp(jnp.where(allowed, scores - log, MASKED))
        d_probs = dot_any(d_out, kv, (1, 1))
        d_scores = (probs * (d_probs - d_total)).astype(LOW)
        sum_ref[:extent] += dot_any(probs.astype(LOW), d_out, (0, 0)) + dot_any(d_scores, q, (0, 0))
        d_q = dot_any(dot_any(d_scores, kv, (1, 0)).astype(LOW), under_q, (1, 1)).astype(LOW)

        @pl.when(h == 0)
        def _():
            d_q_ref[...] = d_q

        @pl.when(h > 0)
        def _():
            d_q_ref[...] += d_q

    for_extent(block, rows, run)

    @pl.when((h == GROUP_HEADS - 1) & (t >= SEQ - 1))
    def _():
        d_kv_ref[...] = sum_ref[...].astype(LOW)


def attention_specs(rows, group):
    by_step = lambda width: pl.BlockSpec((rows, width), lambda t, h: (t, 0))
    kv_block = pl.BlockSpec((group, 128), lambda t, h: (0, t // SEQ))
    return by_step, kv_block


def attention_forward(lengths, queries, kv, rows):
    by_step, kv_block = attention_specs(rows, kv.shape[0])
    return pl.pallas_call(
        attention_forward_kernel,
        grid=(SEQ + 1, GROUP_HEADS),
        in_specs=[pl.BlockSpec(memory_space=pltpu.SMEM), by_step(QW), kv_block],
        out_specs=[by_step(QW), by_step(128)],
        out_shape=[
            jax.ShapeDtypeStruct(queries.shape, LOW),
            jax.ShapeDtypeStruct((queries.shape[0], 128), FULL),
        ],
        compiler_params=pltpu.CompilerParams(vmem_limit_bytes=32 << 20),
        cost_estimate=pl.CostEstimate(flops=4 * 10**10, bytes_accessed=4 << 20, transcendentals=8 * 10**6),
    )(lengths, queries, kv)


def attention_backward(lengths, queries, kv, out, logs, d_out, rows, parts, collective_id):
    group = kv.shape[0]
    by_step, kv_block = attention_specs(rows, group)
    total = lax.axis_size("dp")
    beside = parts if total == 8 else []
    count, line = len(beside), total // 2
    pieces = pieces_of(beside, 1)

    def kernel(*refs):
        own_in, parts_in = refs[:6], refs[6 : 6 + count]
        own_out, sums_out = refs[6 + count : 8 + count], refs[8 + count : 8 + 2 * count]
        sum_ref, transfer = refs[8 + 2 * count], refs[9 + 2 * count :]
        step = pl.program_id(0) * GROUP_HEADS + pl.program_id(1)
        steps = (SEQ + 1) * GROUP_HEADS
        phases = scatter_phases(pieces, line, parts_in + sums_out + transfer) if count else []
        spots = [min(13 * k, steps - 1) for k in range(len(phases))]
        for phase, spot in zip(phases, spots):
            if spot < steps - 1:
                pl.when(step == spot)(phase)
        attention_backward_kernel(*own_in, *own_out, sum_ref)
        for phase, spot in zip(phases, spots):
            if spot == steps - 1:
                pl.when(step == spot)(phase)

    found = pl.pallas_call(
        kernel,
        grid=(SEQ + 1, GROUP_HEADS),
        in_specs=[pl.BlockSpec(memory_space=pltpu.SMEM), by_step(QW), kv_block]
        + [by_step(QW), by_step(128), by_step(QW)]
        + [pl.BlockSpec(memory_space=pl.ANY)] * count,
        out_specs=[by_step(QW), kv_block] + [pl.BlockSpec(memory_space=pltpu.VMEM)] * count,
        out_shape=[jax.ShapeDtypeStruct(queries.shape, LOW), jax.ShapeDtypeStruct(kv.shape, LOW)]
        + [jax.ShapeDtypeStruct(p.shape[1:], FULL) for p in beside],
        scratch_shapes=[pltpu.VMEM((group, 128), FULL)]
        + (scatter_scratch(beside, pieces, line) if count else []),
        compiler_params=pltpu.CompilerParams(
            vmem_limit_bytes=56 << 20,
            **(dict(collective_id=collective_id, has_side_effects=True) if count else {}),
        ),
        cost_estimate=pl.CostEstimate(flops=10**11, bytes_accessed=8 << 20, transcendentals=8 * 10**6),
    )(lengths, queries, kv, out, logs, d_out, *beside)
    return found[0], found[1], list(found[2:]) if count else scatter_dp(parts, collective_id)


def pick(options, seq_index):
    return lax.select_n(seq_index, *options)


def own_cut(values, seq_index, axis, unit):
    cuts = []
    for first, count in zip(FIRST_HEAD, HEAD_COUNT):
        cut = lax.slice_in_dim(values, first * unit, (first + count) * unit, axis=axis)
        pads = [(0, 0)] * values.ndim
        pads[axis] = (0, (LOCAL_HEADS - count) * unit)
        cuts.append(jnp.pad(cut, pads))
    return pick(cuts, seq_index)


def own_spread(values, seq_index, unit):
    spreads = []
    for first, count in zip(FIRST_HEAD, HEAD_COUNT):
        pads = [(0, 0)] * (values.ndim - 1) + [(first * unit, (SSM_HEADS - first - count) * unit)]
        spreads.append(jnp.pad(values[..., : count * unit], pads))
    return pick(spreads, seq_index)


def channel_cut(wide, seq_index, axis):
    return own_cut(wide, seq_index, axis, SSM_HEAD)


def bcdt_cut(w_bcdt, seq_index):
    first = pick([jnp.int32(h) for h in FIRST_HEAD], seq_index)
    count = pick([jnp.int32(c) for c in HEAD_COUNT], seq_index)
    source = jnp.arange(w_bcdt.shape[1], dtype=jnp.int32)[:, None]
    target = jnp.arange(BCDT_PAD, dtype=jnp.int32)[None]
    shared = (target < 2 * STATE) & (source == target)
    steps = (target >= 2 * STATE) & (target < 2 * STATE + count) & (source == target + first)
    return mm(w_bcdt, (shared | steps).astype(LOW)).astype(LOW)


def rows_by_peer_kernel(mamba_ref, o_ref, *refs):
    outs, held, load_sem, store_sem = refs[:SEQ], *refs[SEQ:]
    me = lax.axis_index("seq")
    shared = (KV_HEADS - 1) * QW

    def loads(p):
        own = HEAD_COUNT[p] * SSM_HEAD
        parts = [
            (mamba_ref, FIRST_HEAD[p] * SSM_HEAD, OUT_AT, own),
            (o_ref, p * QW, O_AT, QW),
            (o_ref, shared, O5_AT, QW),
        ]
        return [
            pltpu.make_async_copy(
                source.at[pl.ds(at, count)], held.at[p, pl.ds(to, count)], load_sem.at[p, k]
            )
            for k, (source, at, to, count) in enumerate(parts)
        ]

    for p in range(SEQ):
        for load in loads(p):
            load.start()
        for start, end in ((HEAD_COUNT[p] * SSM_HEAD, O_AT), (O_AT + QW, O5_AT)):
            held[p, start:end] = jnp.zeros((end - start, held.shape[2]), held.dtype)

    def stores(act):
        for p in range(SEQ):
            if act == "start":
                for load in loads(p):
                    load.wait()
            for k in range(SEQ):
                copy = pltpu.make_async_copy(held.at[p], outs[k], store_sem.at[p])
                pl.when(jnp.bitwise_xor(me, p) == k)(copy.start if act == "start" else copy.wait)

    stores("start")
    stores("wait")


def rows_by_peer(mamba_cols, o_cols):
    block = (OUT_WIDTH, o_cols.shape[1])
    anywhere = pl.BlockSpec(memory_space=pl.ANY)
    return pl.pallas_call(
        rows_by_peer_kernel,
        in_specs=[anywhere] * 2,
        out_specs=[anywhere] * SEQ,
        out_shape=[jax.ShapeDtypeStruct(block, LOW)] * SEQ,
        scratch_shapes=[
            pltpu.VMEM((SEQ,) + block, LOW),
            pltpu.SemaphoreType.DMA((SEQ, 3)),
            pltpu.SemaphoreType.DMA((SEQ,)),
        ],
        compiler_params=pltpu.CompilerParams(vmem_limit_bytes=32 << 20),
        cost_estimate=pl.CostEstimate(flops=0, bytes_accessed=12 << 20, transcendentals=0),
    )(mamba_cols, o_cols)


def wide_kernel(*refs):
    pieces, out = refs[:SEQ], refs[SEQ]
    me, width = lax.axis_index("seq"), pieces[0].shape[1]
    for j in range(SEQ):
        for k in range(SEQ):

            @pl.when(jnp.bitwise_xor(me, j) == k)
            def _():
                out[:, width * j : width * (j + 1)] = pieces[k][...]


def wide_of(arrivals):
    rows, width = arrivals[0].shape
    block = rows if rows < 400 else 400
    return pl.pallas_call(
        wide_kernel,
        grid=(rows // block,),
        in_specs=[pl.BlockSpec((block, width), lambda i: (i, 0))] * SEQ,
        out_specs=pl.BlockSpec((block, SEQ * width), lambda i: (i, 0)),
        out_shape=jax.ShapeDtypeStruct((rows, SEQ * width), arrivals[0].dtype),
        cost_estimate=pl.CostEstimate(flops=0, bytes_accessed=16 * rows * width, transcendentals=0),
    )(*arrivals)


def on_device(
    tokens_in,
    doc_lengths,
    norm_gains,
    w_qkv,
    w_o,
    w_xz,
    w_bcdt,
    conv_w,
    ssm_rate,
    ssm_skip,
    w_out,
    w_gate_up,
    w_down,
    cotangent,
):
    rows = tokens_in.shape[0]
    group = rows * SEQ
    s = lax.axis_index("seq")
    dp_index = lax.axis_index("dp")
    dp_total = lax.axis_size("dp")
    block_rows = w_qkv.shape[0]
    kv_width = KV_HEADS * HEAD
    lengths = doc_lengths[0]
    live = (jnp.arange(rows, dtype=jnp.int32) + s * rows < lengths[0] + lengths[1]).astype(FULL)[:, None]

    gains_block = norm_gains.shape[1]
    conv_block = conv_w.shape[1]
    width = -(-max(conv_block, gains_block) // 128) * 128
    small = jnp.concatenate(
        [
            jnp.pad(conv_w, ((0, 4), (0, width - conv_block))),
            jnp.pad(norm_gains, ((0, 4), (0, width - gains_block))),
        ]
    )
    out_block = w_out.shape[0]
    qkv_far, qkv_near = swap(w_qkv, "seq", 2), swap(w_qkv, "seq", 1)
    x_part, z_part = trade_halves(
        w_xz[:, :LOCAL_CH], jnp.pad(w_xz[:, LOCAL_CH:], ((0, 0), (0, 2 * LOCAL_CH - w_xz.shape[1])))
    )
    tokens_far, tokens_near = swap(tokens_in, "seq", 2), swap(tokens_in, "seq", 1)
    small, o_cols, mamba_cols = gather_dp([small, w_o, w_out], 0)
    small, o_cols, mamba_cols, qkv_far, qkv_near, x_part, z_part, tokens_far, tokens_near = lax.optimization_barrier(
        (small, o_cols, mamba_cols, qkv_far, qkv_near, x_part, z_part, tokens_far, tokens_near)
    )
    qkv_shards = [w_qkv, qkv_near, qkv_far, swap(qkv_far, "seq", 1)]
    token_blocks = [tokens_in, tokens_near, tokens_far, swap(tokens_far, "seq", 1)]
    full_conv = small[:, :4, :conv_block].transpose(1, 0, 2).reshape(4, INNER).astype(FULL)
    gains = small[:, 8:12, :gains_block].transpose(1, 0, 2).reshape(4, D).astype(FULL)
    tokens_group = place(list(zip(seq_order(), token_blocks))).reshape(group, D)
    normed = norm_rows(tokens_group, gains[0])
    qkv_wide = wide_of(qkv_shards)
    q_at = lambda h: lax.dynamic_slice_in_dim(qkv_wide, h * QW, QW, 1)
    kv_at = lambda h: [
        lax.dynamic_slice_in_dim(qkv_wide, D + h * HEAD, HEAD, 1),
        lax.dynamic_slice_in_dim(qkv_wide, D + kv_width + h * HEAD, HEAD, 1),
    ]
    qkv_packet = jnp.concatenate(kv_at(s) + kv_at(KV_HEADS - 1) + [q_at(s), q_at(KV_HEADS - 1)], axis=1)
    xz_packet = jnp.concatenate([x_part, z_part, bcdt_cut(w_bcdt, s)], axis=1)
    full_qkv, full_xz = gather_dp([qkv_packet, xz_packet], 1)
    gate_up_packet = jnp.pad(w_gate_up, ((0, 0), (0, 0), (0, UNITS_PAD - UNITS))).reshape(block_rows, -1)
    down_packet = jnp.pad(w_down, ((0, 0), (0, UNITS_PAD - UNITS)))
    d_total = cotangent.astype(FULL) * live
    d_ffn = d_total.astype(LOW)
    d_ffn_far, d_ffn_near = swap(d_ffn, "seq", 2), swap(d_ffn, "seq", 1)
    full_qkv, full_xz, o_cols, mamba_cols, gate_up_packet, down_packet, d_ffn_far, d_ffn_near = (
        lax.optimization_barrier(
            (full_qkv, full_xz, o_cols, mamba_cols, gate_up_packet, down_packet, d_ffn_far, d_ffn_near)
        )
    )
    d_ffn_group = jnp.concatenate([d_ffn, d_ffn_near, d_ffn_far, swap(d_ffn_far, "seq", 1)])
    full_qkv = full_qkv.reshape(D, -1)
    full_xz = full_xz.reshape(D, -1)
    full_gate_up = gather_dp_apart(gate_up_packet)
    full_down = gather_dp_apart(down_packet)


    own = lambda a: lax.dynamic_slice_in_dim(a, s * rows, rows, 0)
    normed_own = own(normed)
    kvq = mm(normed, full_qkv[:, : 256 + QW]).astype(LOW)
    q_last = mm(normed_own, full_qkv[:, 256 + QW :]).astype(LOW)
    queries = jnp.concatenate([kvq[:, 256:], q_last])
    kv = kvq[:, :256]
    out_blocks = list(rows_by_peer(mamba_cols.reshape(INNER, -1), o_cols.reshape(D, -1)))
    out_blocks, queries = meet(out_blocks, queries)
    attended, logs = attention_forward(doc_lengths, queries, kv, rows)
    out_pieces = out_blocks[:1] + [swap(out_blocks[bit], "seq", bit) for bit in (1, 2, 3)]
    out_rows = wide_of(after(out_pieces, attended))
    w_out_rows = out_rows[:WIDE]
    w_o_rows = out_rows[O_AT : O_AT + QW]
    w_o5_rows = out_rows[O5_AT:]
    attn_part = mm(attended[:group], w_o_rows).astype(LOW)
    normed_now, attn_part = lax.optimization_barrier((normed, attn_part))
    attn_keep, attn_got = scatter_begin(attn_part)

    xzb = mm(normed_now, full_xz)
    attn_held, attn_far = scatter_far(attn_keep, after(attn_got, xzb))
    xzb, attn_held = lax.optimization_barrier((xzb, attn_held))
    conv_rows = jnp.pad(channel_cut(full_conv, s, 1), ((0, 4), (0, WIDE - LOCAL_CH)))
    rate_row = jnp.pad(own_cut(ssm_rate, s, 0, 1), (STEP_AT, 128 - STEP_AT - LOCAL_HEADS))
    rate_row = jnp.broadcast_to(rate_row, (8, 128))
    skip_row = jnp.pad(jnp.repeat(own_cut(ssm_skip, s, 0, 1), SSM_HEAD), (0, WIDE - LOCAL_CH))
    skip_row = jnp.broadcast_to(skip_row, (8, WIDE))
    mamba_in = (doc_lengths, xzb, conv_rows, rate_row, skip_row)
    gated, read, states = mamba_forward(*mamba_in)
    gated, attn_far = meet(gated, attn_far)
    ssm_held, ssm_far = scatter_far(*scatter_begin(mm(gated, w_out_rows)))
    attn_o = scatter_end(attn_held, attn_far) + mm(attended[group:], w_o5_rows)
    ssm_o = scatter_end(ssm_held, ssm_far)

    inputs_x = tokens_in.astype(FULL)
    (residual, normed_two), pull_join = jax.vjp(join_tail, inputs_x, attn_o, ssm_o, gains)
    normed_two, d_act = seq_arrivals(normed_two.astype(LOW), mm(d_ffn_group, full_down))
    normed_two = jnp.concatenate(normed_two)
    gate_up = mm(normed_two, full_gate_up)
    ffn_gate, ffn_up = gate_up[:, :UNITS_PAD], gate_up[:, UNITS_PAD:]
    ffn_act = (jax.nn.silu(ffn_gate) * ffn_up).astype(LOW)

    sig = jax.nn.sigmoid(ffn_gate)
    d_gate = d_act * ffn_up * (sig * (1.0 + ffn_gate * (1.0 - sig)))
    d_up = d_act * ffn_gate * sig
    d_gate_up = jnp.concatenate([d_gate.astype(LOW), d_up.astype(LOW)], axis=1)
    two_keep, two_got = relative_begin(mm_nt(d_gate_up, full_gate_up))
    two_got, grad_down_part = meet(two_got, mm_tn(d_ffn_group, ffn_act).astype(LOW))
    two_held, two_far = relative_far(two_keep, two_got)
    two_far, grad_gate_up_part = meet(two_far, mm_tn(normed_two, d_gate_up).astype(LOW))
    d_normed_two = scatter_end(two_held, two_far)
    grad_gate_up_sum = scatter_dp_apart(grad_gate_up_part)
    grad_down_sum = scatter_dp_apart(grad_down_part)
    grad_gate_up = grad_gate_up_sum.reshape(block_rows, 2, UNITS_PAD)[:, :, :UNITS]
    grad_down = grad_down_sum[:, :UNITS]

    d_x_tail, d_attn_o, d_ssm_o, d_gains = pull_join((d_total, d_normed_two))
    ssm_arrivals, ffn_part = seq_arrivals(d_ssm_o.astype(LOW), mm_nt(ffn_act, full_down).astype(LOW))
    d_attn_own = after(d_attn_o.astype(LOW), ssm_arrivals[2])
    attn_near, attn_away = swap(d_attn_own, "seq", 1), swap(d_attn_own, "seq", 2)
    d_ssm = place(list(zip(seq_order(), ssm_arrivals))).reshape(group, D)
    d_gated = mm_nt(d_ssm, w_out_rows).astype(LOW)

    def send_columns(grad):
        width = D // SEQ
        blocks = [grad[:, width * j : width * (j + 1)] for j in range(SEQ)]
        return [with_layout_constraint(pick(blocks, s ^ k), Layout((0, 1))) for k in range(SEQ)]

    def trade(blocks):
        return blocks[:1] + [swap(blocks[bit], "seq", bit) for bit in (1, 2, 3)]

    mamba_blocks, d_gated = meet(send_columns(mm_tn(gated, d_ssm).astype(LOW)), d_gated)
    mamba_pieces = trade(mamba_blocks)
    (mamba_pieces[1], attn_near), d_gated = meet((mamba_pieces[1], attn_near), d_gated)
    d_xzb, d_chan, d_rate = mamba_backward(*mamba_in, states, read, d_gated)
    (mamba_pieces[2:], attn_away), d_xzb = meet((mamba_pieces[2:], attn_away), d_xzb)
    ffn_keep, ffn_got = relative_begin(ffn_part)
    attn_arrivals = [d_attn_own, attn_near, attn_away, swap(attn_away, "seq", 1)]
    arrived = place(list(zip(seq_order(), mamba_pieces)))
    grad_out_part = jnp.concatenate(
        [arrived[j, : HEAD_COUNT[j] * SSM_HEAD] for j in range(SEQ)]
    ).reshape(dp_total, out_block, -1)

    d_attn = place(list(zip(seq_order(), attn_arrivals))).reshape(group, D)
    d_attended = jnp.concatenate([mm_nt(d_attn, w_o_rows), mm_nt(d_attn_own, w_o5_rows)]).astype(LOW)
    head_blocks = send_columns(
        jnp.concatenate([mm_tn(attended[:group], d_attn), mm_tn(attended[group:], d_attn_own)]).astype(LOW)
    )
    head_blocks, d_attended = meet(head_blocks, d_attended)
    head_pieces = trade(head_blocks)
    ffn_got, d_attended = meet(ffn_got, d_attended)
    ffn_held, ffn_far = relative_far(ffn_keep, ffn_got)
    ffn_held, d_attended = meet(ffn_held, d_attended)
    d_conv = d_chan[:CONV, :LOCAL_CH]
    d_skip = jnp.sum(d_chan[CONV, :LOCAL_CH].reshape(LOCAL_HEADS, SSM_HEAD), axis=1)
    d_rate = d_rate[0, STEP_AT : STEP_AT + LOCAL_HEADS]
    grad_xz_part = mm_tn(normed, d_xzb).astype(LOW).reshape(dp_total, block_rows, -1)

    d_queries, d_kv, (grad_xz_sum, grad_out) = attention_backward(
        doc_lengths, queries, kv, attended, logs, d_attended, rows, [grad_xz_part, grad_out_part], 3
    )
    (head_pieces, ffn_far), d_queries = meet((head_pieces, ffn_far), d_queries)
    mixed_out = ((residual + scatter_end(ffn_held, ffn_far)) * live).astype(LOW)
    arrived = place(list(zip(seq_order(), head_pieces)))
    grad_o_part = jnp.concatenate(
        [arrived[j, :QW] for j in range(SEQ)] + [jnp.sum(arrived[:, QW:].astype(FULL), axis=0).astype(LOW)]
    ).reshape(dp_total, block_rows, -1)
    d_kvq = jnp.concatenate([d_kv, d_queries[:group]], axis=1)
    d_q_last = d_queries[group:]
    grad_qkv_part = jnp.concatenate(
        [mm_tn(normed, d_kvq).astype(LOW), mm_tn(normed_own, d_q_last).astype(LOW)], axis=1
    ).reshape(dp_total, block_rows, -1)
    d_normed_part = mm_nt(d_xzb, full_xz) + mm_nt(d_kvq, full_qkv[:, : 256 + QW])
    d_normed_own = mm_nt(d_q_last, full_qkv[:, 256 + QW :])

    tokens_wide = tokens_group.astype(FULL)
    unit = tokens_wide * lax.rsqrt(jnp.mean(tokens_wide * tokens_wide, axis=-1, keepdims=True) + NORM_EPS)
    d_gain_first = jnp.sum(d_normed_part * unit, axis=0) + jnp.sum(d_normed_own * own(unit), axis=0)
    d_gains = d_gains.at[0].add(d_gain_first)
    by_dp = lambda a: a.reshape(a.shape[0], dp_total, -1).transpose(1, 0, 2)
    d_heads = jnp.concatenate([own_spread(d_rate, s, 1), own_spread(d_skip, s, 1)])[None]
    small_part = jnp.concatenate(
        [
            jnp.pad(by_dp(own_spread(d_conv, s, SSM_HEAD)), ((0, 0), (0, 0), (0, width - conv_block))),
            jnp.pad(by_dp(d_gains), ((0, 0), (0, 0), (0, width - gains_block))),
            jnp.broadcast_to(
                jnp.pad(d_heads, ((0, 7), (0, width - d_heads.shape[1])))[None], (dp_total, 8, width)
            ),
        ],
        axis=1,
    )
    normed_keep, normed_got = scatter_begin(d_normed_part)
    normed_got, grad_qkv_part = meet(normed_got, grad_qkv_part)
    normed_held, normed_far = scatter_far(normed_keep, normed_got)
    grad_o_part, normed_held = meet(grad_o_part, normed_held)
    grad_qkv_sum, grad_o, small_sum = scatter_dp([grad_qkv_part, grad_o_part, small_part], 2)
    normed_far, small_sum = meet(normed_far, small_sum)
    small_sum = small_sum + swap(small_sum, "seq", 1)
    small_sum = small_sum + swap(small_sum, "seq", 2)
    grad_xz_sum = grad_xz_sum.astype(LOW)
    first, last = trade_back(grad_xz_sum[:, :LOCAL_CH], grad_xz_sum[:, LOCAL_CH : 2 * LOCAL_CH])
    grad_xz = jnp.concatenate([first, last], axis=1)[:, : w_xz.shape[1]].astype(FULL)
    both_all = gather_seq(jnp.concatenate([grad_qkv_sum.astype(LOW), grad_xz_sum[:, 2 * LOCAL_CH :]], axis=1))
    bcdt_all = both_all[:, :, grad_qkv_sum.shape[1] :].astype(FULL)
    grad_bcdt = jnp.concatenate(
        [jnp.sum(bcdt_all[:, :, : 2 * STATE], axis=0)]
        + [bcdt_all[j, :, 2 * STATE : 2 * STATE + HEAD_COUNT[j]] for j in range(SEQ)],
        axis=1,
    )
    qkv_all = both_all[:, :, : grad_qkv_sum.shape[1]].astype(FULL)
    col = lambda j, at, width: qkv_all[j, :, at : at + width]
    shared = lambda at, width: jnp.sum(qkv_all[:, :, at : at + width], axis=0)
    grad_qkv_wide = jnp.concatenate(
        [col(j, 256, QW) for j in range(SEQ)]
        + [shared(256 + QW, QW)]
        + [col(j, 0, HEAD) for j in range(SEQ)]
        + [shared(128, HEAD)]
        + [col(j, HEAD, HEAD) for j in range(SEQ)]
        + [shared(128 + HEAD, HEAD)],
        axis=1,
    )
    qkv_width = w_qkv.shape[1]
    grad_qkv = lax.dynamic_slice_in_dim(grad_qkv_wide, s * qkv_width, qkv_width, 1)

    d_normed = scatter_end(normed_held, normed_far) + d_normed_own
    d_unit = d_normed * gains[0]
    scale = lax.rsqrt(jnp.mean(inputs_x * inputs_x, axis=-1, keepdims=True) + NORM_EPS)
    d_x_head = scale * (
        d_unit - inputs_x * scale * scale * jnp.mean(d_unit * inputs_x, axis=-1, keepdims=True)
    )
    input_grad = (d_x_tail + d_x_head).astype(LOW)
    grad_conv = small_sum[:CONV, :conv_block]
    grad_gains = small_sum[CONV : CONV + 4, :gains_block]
    grad_rate = small_sum[8, :SSM_HEADS]
    grad_skip = small_sum[8, SSM_HEADS : 2 * SSM_HEADS]
    return (
        mixed_out,
        input_grad,
        grad_gains,
        grad_qkv,
        grad_o,
        grad_xz,
        grad_bcdt,
        grad_conv,
        grad_rate,
        grad_skip,
        grad_out,
        grad_gate_up,
        grad_down,
    )


def solution(mesh):
    placed = (
        P(("dp", "seq"), None),
        P("dp", None),
        P(None, "dp"),
        P("dp", "seq"),
        P("dp", "seq"),
        P("dp", "seq"),
        P("dp", None),
        P(None, "dp"),
        P(),
        P(),
        P("dp", "seq"),
        P("dp", None, "seq"),
        P("dp", "seq"),
        P(("dp", "seq"), None),
    )
    return jax.shard_map(
        on_device,
        mesh=mesh,
        in_specs=placed,
        out_specs=(
            P(("dp", "seq"), None),
            P(("dp", "seq"), None),
            P(None, "dp"),
            P("dp", "seq"),
            P("dp", "seq"),
            P("dp", "seq"),
            P("dp", None),
            P(None, "dp"),
            P(),
            P(),
            P("dp", "seq"),
            P("dp", None, "seq"),
            P("dp", "seq"),
        ),
        check_vma=False,
    )
```

```python
import jax
import jax.numpy as jnp
from jax import lax
from jax.experimental import pallas as pl
from jax.experimental.layout import Layout, with_layout_constraint
from jax.experimental.pallas import tpu as pltpu
from jax.sharding import PartitionSpec as P

D = 1600
HEADS = 25
KV_HEADS = 5
HEAD = 64
INNER = 3200
SSM_HEAD = 64
STATE = 16
CONV = 4
FF = 5504
WINDOW = 1024
SSM_HEADS = 50

NORM_EPS = 1e-05
MASKED = -1e30
LOW = jnp.bfloat16
FULL = jnp.float32

SEQ = 4
GROUP_HEADS = HEADS // KV_HEADS
QW = GROUP_HEADS * HEAD
LOCAL_HEADS = 13
LOCAL_CH = LOCAL_HEADS * SSM_HEAD
CHUNK = 128
UNITS = FF // SEQ
UNITS_PAD = 1408
BCDT_PAD = 128
OUT_AT, O_AT, O5_AT, OUT_WIDTH = 0, 896, 1280, 1600
FIRST_HEAD = tuple((SSM_HEADS * s // 2 + 1) // 2 for s in range(SEQ))
HEAD_COUNT = tuple(b - a for a, b in zip(FIRST_HEAD, FIRST_HEAD[1:] + (SSM_HEADS,)))


def swap(value, axis, bit):
    return lax.ppermute(value, axis, [(i, i ^ bit) for i in range(lax.axis_size(axis))])


def place_kernel(count, index_ref, *refs):
    blocks, stacked, held, in_sems, out_sems = refs[:count], *refs[count:]
    loads = [
        pltpu.make_async_copy(block, held.at[i], in_sems.at[i]) for i, block in enumerate(blocks)
    ]
    stores = [
        pltpu.make_async_copy(held.at[i], stacked.at[index_ref[i]], out_sems.at[i])
        for i in range(count)
    ]
    for load in loads:
        load.start()
    for load, store in zip(loads, stores):
        load.wait()
        store.start()
    for store in stores:
        store.wait()


def place(blocks):
    count = len(blocks)
    block = blocks[0][1]
    anywhere = pl.BlockSpec(memory_space=pl.ANY)
    return pl.pallas_call(
        lambda *refs: place_kernel(count, *refs),
        out_shape=jax.ShapeDtypeStruct((count,) + block.shape, block.dtype),
        grid_spec=pltpu.PrefetchScalarGridSpec(
            num_scalar_prefetch=1,
            grid=(1,),
            in_specs=[anywhere] * count,
            out_specs=anywhere,
            scratch_shapes=[
                pltpu.VMEM((count,) + block.shape, block.dtype),
                pltpu.SemaphoreType.DMA((count,)),
                pltpu.SemaphoreType.DMA((count,)),
            ],
        ),
        compiler_params=pltpu.CompilerParams(vmem_limit_bytes=32 << 20),
        cost_estimate=pl.CostEstimate(
            flops=0, bytes_accessed=2 * count * block.size * block.dtype.itemsize, transcendentals=0
        ),
    )(jnp.stack([jnp.asarray(i, jnp.int32) for i, _ in blocks]), *[b for _, b in blocks])


def seq_order():
    me = lax.axis_index("seq")
    return [me, me ^ 1, me ^ 2, me ^ 3]


def seq_arrivals(block, beside=None):
    far, near = swap(block, "seq", 2), swap(block, "seq", 1)
    if beside is not None:
        far, beside = meet(far, beside)
    blocks = [block, near, far, swap(far, "seq", 1)]
    return blocks if beside is None else (blocks, beside)


def gather_seq(block):
    return place(list(zip(seq_order(), seq_arrivals(block))))


def scatter_begin(part):
    core = lax.axis_index("seq") % 2
    part = with_layout_constraint(part.astype(LOW), Layout((0, 1)))
    by_core = part.reshape((2, 2, part.shape[0] // SEQ) + part.shape[1:])
    give = lax.dynamic_index_in_dim(by_core, 1 - core, 1, False)
    keep = lax.dynamic_index_in_dim(by_core, core, 1, False)
    return keep, swap(give, "seq", 1)


def scatter_far(keep, got):
    far = lax.axis_index("seq") // 2
    at = lambda a, i: lax.dynamic_index_in_dim(a, i, 0, False).astype(FULL)
    give_far = (at(keep, 1 - far) + at(got, 1 - far)).astype(LOW)
    return at(keep, far) + at(got, far), swap(give_far, "seq", 2)


def scatter_end(held, got_far):
    return held + got_far.astype(FULL)


def relative_begin(part):
    part = with_layout_constraint(part.astype(LOW), Layout((0, 1)))
    rows = part.shape[0] // SEQ
    block = lambda k: part[rows * k : rows * (k + 1)]
    got = swap(jnp.concatenate([block(1), block(3)]), "seq", 1)
    return (block(0), block(2)), got


def relative_far(keep, got):
    rows = got.shape[0] // 2
    add = lambda k: keep[k].astype(FULL) + got[rows * k : rows * (k + 1)].astype(FULL)
    return add(0), swap(add(1).astype(LOW), "seq", 2)


def meet(one, two):
    return lax.optimization_barrier((one, two))


def after(values, done):
    return lax.optimization_barrier((values, done))[0]


def line_place():
    me = lax.axis_index("dp")
    return lax.axis_size("dp") // 2, me // 2, lax.rem(me, 2)


def greet(line, z, x):
    barrier = pltpu.get_barrier_semaphore()

    def signal(target):
        pl.semaphore_signal(
            barrier, inc=1, device_id={"dp": target}, device_id_type=pl.DeviceIdType.MESH
        )

    signal(2 * z + 1 - x)
    pl.when(z > 0)(lambda: signal(2 * (z - 1) + x))
    pl.when(z < line - 1)(lambda: signal(2 * (z + 1) + x))
    pl.semaphore_wait(
        barrier, 1 + (z > 0).astype(jnp.int32) + (z < line - 1).astype(jnp.int32)
    )


def pieces_of(arrays, axis):
    pieces = []
    for i, array in enumerate(arrays):
        rows = array.shape[axis]
        count = 1 if rows < 64 else 3 if rows < 256 else 4
        size = rows // count // 16 * 16 if count > 1 else rows
        for k in range(count):
            pieces.append((i, pl.ds(k * size, size if k < count - 1 else rows - k * size)))
    return pieces


def gather_phases(pieces, line, refs):
    packets = pieces[-1][0] + 1
    sources, outs = refs[:packets], refs[packets : 2 * packets]
    own_sem, up_sem, down_sem, line_sem, give_sem, got_sem = refs[2 * packets :]
    _, z, x = line_place()
    held = lambda i, zb: outs[pieces[i][0]].at[2 * zb + x, pieces[i][1]]
    mine = lambda i: sources[pieces[i][0]].at[pieces[i][1]]

    def copy(src, i, zb, send_sem, recv_sem, target):
        return pltpu.make_async_remote_copy(
            src_ref=src,
            dst_ref=held(i, zb),
            send_sem=send_sem.at[i, zb],
            recv_sem=recv_sem.at[i, zb],
            device_id={"dp": target},
            device_id_type=pl.DeviceIdType.MESH,
        )

    up_to = lambda src, i, zb: copy(src, i, zb, up_sem, line_sem, 2 * (z + 1) + x)
    down_to = lambda src, i, zb: copy(src, i, zb, down_sem, line_sem, 2 * (z - 1) + x)
    give = lambda src, i, zb: copy(src, i, zb, give_sem, got_sem, 2 * z + 1 - x)
    own = lambda i: pltpu.make_async_copy(mine(i), held(i, z), own_sem.at[i])

    def take_turn(turn):
        if turn == 0:
            greet(line, z, x)
        for i in range(len(pieces)):
            far = turn - i
            if far == 0:
                pl.when(z < line - 1)(lambda: up_to(mine(i), i, z).start())
                pl.when(z > 0)(lambda: down_to(mine(i), i, z).start())
                give(mine(i), i, z).start()
                own(i).start()
            elif 0 < far < line:

                @pl.when(z - far >= 0)
                def _():
                    zb = z - far
                    up_to(held(i, zb), i, zb).wait_recv()
                    pl.when(z < line - 1)(lambda: up_to(held(i, zb), i, zb).start())
                    give(held(i, zb), i, zb).start()

                @pl.when(z + far < line)
                def _():
                    zb = z + far
                    down_to(held(i, zb), i, zb).wait_recv()
                    pl.when(z > 0)(lambda: down_to(held(i, zb), i, zb).start())
                    give(held(i, zb), i, zb).start()

    def finish():
        for i in range(len(pieces)):
            own(i).wait()
            for zb in range(line):
                give(held(i, zb), i, zb).wait()
                pl.when((zb <= z) & (z < line - 1))(lambda: up_to(held(i, zb), i, zb).wait_send())
                pl.when((zb >= z) & (z > 0))(lambda: down_to(held(i, zb), i, zb).wait_send())

    turns = len(pieces) + line - 1
    return [lambda turn=turn: take_turn(turn) for turn in range(turns)] + [finish]


def gather_kernel(pieces, line, *refs):
    for phase in gather_phases(pieces, line, refs):
        phase()


def gather_scratch(pieces, line):
    count = len(pieces)
    sems = lambda *shape: pltpu.SemaphoreType.DMA(shape)
    return [sems(count)] + [sems(count, line) for _ in range(5)]


def gather_shapes(packets):
    return [jax.ShapeDtypeStruct((lax.axis_size("dp"),) + p.shape, p.dtype) for p in packets]


def gather_dp(packets, collective_id):
    total = lax.axis_size("dp")
    if total != 8:
        return [lax.all_gather(packet, "dp", axis=0) for packet in packets]
    pieces, line = pieces_of(packets, 0), total // 2
    return pl.pallas_call(
        lambda *refs: gather_kernel(pieces, line, *refs),
        out_shape=gather_shapes(packets),
        in_specs=[pl.BlockSpec(memory_space=pltpu.VMEM)] * len(packets),
        out_specs=[pl.BlockSpec(memory_space=pl.ANY)] * len(packets),
        scratch_shapes=gather_scratch(pieces, line),
        compiler_params=pltpu.CompilerParams(
            collective_id=collective_id, has_side_effects=True, vmem_limit_bytes=32 << 20
        ),
        cost_estimate=pl.CostEstimate(
            flops=0,
            bytes_accessed=2 * total * sum(p.size * p.dtype.itemsize for p in packets),
            transcendentals=0,
        ),
    )(*packets)


def add_columns(total, parts):
    width = total.shape[-1]
    step = 128 if width % 256 else 256

    def columns(c):
        at = pl.ds(pl.multiple_of(c * step, step), step)
        total[:, at] = sum(part[:, at].astype(FULL) for part in parts).astype(total.dtype)

    pl.loop(0, width // step)(columns)
    if width % step:
        at = slice(width // step * step, width)
        total[:, at] = sum(part[:, at].astype(FULL) for part in parts).astype(total.dtype)


def scatter_phases(pieces, line, refs):
    count = pieces[-1][0] + 1
    parts, outs = refs[:count], refs[count : 2 * count]
    own_refs, near_refs, line_refs = (
        refs[2 * count : 3 * count],
        refs[3 * count : 4 * count],
        refs[4 * count : 5 * count],
    )
    load_sem, give_sem, got_sem, send_sem, line_sem = refs[5 * count :]
    _, z, x = line_place()
    order = [t for pair in zip(range(line - 1, -1, -1), range(line)) for t in pair][:line]
    at = lambda arrays, i, t: arrays[pieces[i][0]].at[t, pieces[i][1]]
    remote = lambda src, dst, send, recv, target: pltpu.make_async_remote_copy(
        src_ref=src,
        dst_ref=dst,
        send_sem=send,
        recv_sem=recv,
        device_id={"dp": target},
        device_id_type=pl.DeviceIdType.MESH,
    )
    give = lambda i, t: remote(
        at(parts, i, 2 * t + 1 - x),
        at(near_refs, i, t),
        give_sem.at[i, t],
        got_sem.at[i, t],
        2 * z + 1 - x,
    )
    load = lambda i, t: pltpu.make_async_copy(
        at(parts, i, 2 * t + x), at(own_refs, i, t), load_sem.at[i, t]
    )
    along = lambda i, t, slot, target: remote(
        at(own_refs, i, t), at(line_refs, i, slot), send_sem.at[i, t], line_sem.at[i, slot], target
    )
    def views(i):
        return [lambda t, arrays=arrays: at(arrays, i, t) for arrays in (own_refs, near_refs, line_refs)]

    def start():
        greet(line, z, x)
        for i in range(len(pieces)):
            for t in order:
                load(i, t).start()
                give(i, t).start()

    def pass_on(i, t, zz):
        own, near, held = views(i)
        load(i, t).wait()
        give(i, t).wait_recv()
        terms = [own(t), near(t)]
        if 0 < zz < t or t < zz < line - 1:
            along(i, t, t, 0).wait_recv()
            terms.append(held(t))
        add_columns(own(t), terms)
        step = 1 if t > zz else -1
        along(i, t, line if t == zz - 1 else t, 2 * (zz + step) + x).start()

    def take_round(r):
        for zz in range(line):

            @pl.when(z == zz)
            def _():
                up, down = r - zz, r - (line - 1 - zz)
                for t in range(line - 1, zz, -1):
                    if 0 <= up < len(pieces):
                        pass_on(up, t, zz)
                for t in range(zz):
                    if 0 <= down < len(pieces):
                        pass_on(down, t, zz)

    def finish():
        for i in range(len(pieces)):
            own, near, held = views(i)
            for t in range(line):

                @pl.when(t == z)
                def _():
                    load(i, t).wait()
                    give(i, t).wait_recv()
                    terms = [own(t), near(t)]
                    if t > 0:
                        along(i, t, t, 0).wait_recv()
                        terms.append(held(t))
                    if t < line - 1:
                        along(i, t, line, 0).wait_recv()
                        terms.append(held(line))
                    add_columns(outs[pieces[i][0]].at[pieces[i][1]], terms)

                pl.when(t != z)(lambda: along(i, t, t, 0).wait_send())
                give(i, t).wait_send()

    rounds = len(pieces) + line - 2
    return [start] + [lambda r=r: take_round(r) for r in range(rounds)] + [finish]


def scatter_kernel(pieces, line, *refs):
    for phase in scatter_phases(pieces, line, refs):
        phase()


def scatter_scratch(parts, pieces, line):
    count = len(pieces)
    sems = lambda *shape: pltpu.SemaphoreType.DMA(shape)
    buffers = [pltpu.VMEM((n,) + p.shape[1:], p.dtype) for n in (line, line, line + 1) for p in parts]
    return buffers + [sems(count, line) for _ in range(4)] + [sems(count, line + 1)]


def scatter_dp(parts, collective_id):
    total = lax.axis_size("dp")
    if total != 8:
        sums = [lax.psum_scatter(p, "dp", scatter_dimension=0) for p in parts]
        return [lax.optimization_barrier(p).astype(FULL) for p in sums]
    pieces, line = pieces_of(parts, 1), total // 2
    return pl.pallas_call(
        lambda *refs: scatter_kernel(pieces, line, *refs),
        out_shape=[jax.ShapeDtypeStruct(p.shape[1:], FULL) for p in parts],
        in_specs=[pl.BlockSpec(memory_space=pl.ANY)] * len(parts),
        out_specs=[pl.BlockSpec(memory_space=pltpu.VMEM)] * len(parts),
        scratch_shapes=scatter_scratch(parts, pieces, line),
        compiler_params=pltpu.CompilerParams(
            collective_id=collective_id, has_side_effects=True, vmem_limit_bytes=56 << 20
        ),
        cost_estimate=pl.CostEstimate(
            flops=6 * 10**10, bytes_accessed=sum(p.size * 2 for p in parts), transcendentals=0
        ),
    )(*parts)


def gather_dp_apart(packet):
    return lax.all_gather(packet, "dp", axis=0, tiled=True)


def scatter_dp_apart(parts):
    summed = lax.psum_scatter(parts.astype(LOW), "dp", scatter_dimension=0, tiled=True)
    return lax.optimization_barrier(summed).astype(FULL)


def trade_halves(first, last):
    me = lax.axis_index("seq")
    one = lax.ppermute(jnp.where(me == 0, last, first), "seq", [(0, 1), (1, 2), (2, 0)])
    two = lax.ppermute(jnp.where(me == 3, first, last), "seq", [(1, 3), (2, 1), (3, 2)])
    return pick([first, one, one, two], me), pick([one, two, two, last], me)


def trade_back(x_part, z_part):
    me = lax.axis_index("seq")
    one = lax.ppermute(jnp.where(me == 0, z_part, x_part), "seq", [(1, 0), (2, 1), (0, 2)])
    two = lax.ppermute(jnp.where(me == 3, x_part, z_part), "seq", [(3, 1), (1, 2), (2, 3)])
    return pick([x_part, one, one, two], me), pick([one, two, two, z_part], me)


def mm(left, right):
    return jnp.dot(left, right, preferred_element_type=FULL)


def mm_nt(left, right):
    return lax.dot_general(left, right, (((1,), (1,)), ((), ())), preferred_element_type=FULL)


def mm_tn(left, right):
    return lax.dot_general(left, right, (((0,), (0,)), ((), ())), preferred_element_type=FULL)


def rms_norm(values, gain):
    return values * lax.rsqrt(jnp.mean(values * values, axis=-1, keepdims=True) + NORM_EPS) * gain


def norm_rows_kernel(values_ref, gain_ref, out_ref):
    out_ref[...] = rms_norm(values_ref[...].astype(FULL), gain_ref[0:1]).astype(LOW)


def norm_rows(values, gain):
    rows, width = values.shape
    block = rows // SEQ
    by_block = pl.BlockSpec((block, width), lambda i: (i, 0))
    return pl.pallas_call(
        norm_rows_kernel,
        grid=(SEQ,),
        in_specs=[by_block, pl.BlockSpec((8, width), lambda i: (0, 0))],
        out_specs=by_block,
        out_shape=jax.ShapeDtypeStruct(values.shape, LOW),
        cost_estimate=pl.CostEstimate(flops=4 * values.size, bytes_accessed=4 * values.size, transcendentals=rows),
    )(values, jnp.broadcast_to(gain, (8, width)))


def join_tail(inputs_x, attn_o, ssm_o, gains):
    residual = inputs_x + 0.5 * (rms_norm(attn_o, gains[1]) + rms_norm(ssm_o, gains[2]))
    return (residual, rms_norm(residual, gains[3]))


STEP_AT = 2 * STATE
WIDE = 896
PAIRS = WIDE // 128
XZB = 1792


def dot_any(left, right, contract):
    return lax.dot_general(
        left, right, ((contract[:1], contract[1:]), ((), ())), preferred_element_type=FULL
    )


def low_dot(left, right, contract):
    return dot_any(left.astype(LOW), right.astype(LOW), contract)


def iota(shape, axis):
    return lax.broadcasted_iota(jnp.int32, shape, axis)


def pair_spread(values):
    rows = values.shape[0]
    low_half = iota((rows, 128), 1) < SSM_HEAD
    tiles = []
    for p in range(PAIRS):
        one = values[:, STEP_AT + 2 * p : STEP_AT + 2 * p + 1]
        two = values[:, STEP_AT + 2 * p + 1 : STEP_AT + 2 * p + 2]
        tiles.append(
            jnp.where(
                low_half,
                jnp.broadcast_to(one, (rows, 128)),
                jnp.broadcast_to(two, (rows, 128)),
            )
        )
    return jnp.concatenate(tiles, axis=1)


def halves(tile):
    low_half = iota(tile.shape, 1) < SSM_HEAD
    zero = jnp.zeros_like(tile)
    return jnp.concatenate([jnp.where(low_half, tile, zero), jnp.where(low_half, zero, tile)], axis=0)


def mamba_chunk(c, lengths_ref, xzb_ref, tail_ref, conv_ref, rate_ref, pad_ref):
    first_end = lengths_ref[0, 0]
    second_end = first_end + lengths_ref[0, 1]
    doc_of = lambda pos: (pos >= first_end).astype(jnp.int32) + (pos >= second_end).astype(jnp.int32)
    base = c * CHUNK
    square = (CHUNK, CHUNK)
    row, lane = iota(square, 0), iota(square, 1)
    doc_row = doc_of(base + row)
    doc_lane = doc_of(base + lane)
    before = jnp.where(c > 0, doc_of(base - 1), -1)
    end = doc_of(base + CHUNK - 1)
    causal = (row >= lane) & (doc_row == doc_lane)
    channel = iota((CHUNK, WIDE), 1) < LOCAL_CH

    raw = jnp.where(channel, xzb_ref[:, :WIDE], 0.0).astype(LOW).astype(FULL)
    gate = pltpu.roll(xzb_ref[:, LOCAL_CH - 64 :], XZB - LOCAL_CH, 1)[:, :WIDE]
    gate = jnp.where(channel, gate, 0.0)
    pad_ref[0:8] = tail_ref[:, :WIDE].astype(LOW).astype(FULL)
    pad_ref[8 : 8 + CHUNK] = raw
    taps = []
    pos = base + iota((CHUNK, 1), 0)
    conv = jnp.zeros((CHUNK, WIDE), FULL)
    for k in range(CONV):
        back = CONV - 1 - k
        same = (doc_of(pos) == doc_of(pos - back)) & (pos >= back)
        shifted = jnp.where(same, pad_ref[8 - back : 8 - back + CHUNK], 0.0)
        taps.append(shifted)
        conv = conv + conv_ref[k : k + 1] * shifted
    conv_sig = jax.nn.sigmoid(conv)
    act = conv * conv_sig

    bc = xzb_ref[:, 2 * LOCAL_CH :]
    b_in = jnp.where(lane < STATE, bc, 0.0)
    c_at = jnp.where((lane >= STATE) & (lane < 2 * STATE), bc, 0.0)
    c_in = pltpu.roll(c_at, CHUNK - STATE, 1)
    step = jnp.maximum(bc, 0.0) + jnp.log(1.0 + jnp.exp(-jnp.abs(bc)))
    lower = (row >= lane).astype(FULL)
    log = lax.dot_general(
        lower,
        -step * rate_ref[0:1],
        (((1,), (0,)), ((), ())),
        precision=lax.Precision.HIGHEST,
        preferred_element_type=FULL,
    )
    last = log[CHUNK - 1 : CHUNK]
    ends = jnp.where(doc_row == end, jnp.exp(last - log), 0.0)
    reach = jnp.where(doc_row == before, jnp.exp(log), 0.0)
    carry = jnp.where(end == before, jnp.exp(last), 0.0)
    gram = low_dot(c_in, b_in, (1, 1))
    log_t = log.T

    def decays(h):
        gap = log[:, STEP_AT + h : STEP_AT + h + 1] - log_t[STEP_AT + h : STEP_AT + h + 1]
        return jnp.exp(jnp.where(causal, gap, MASKED))

    step_wide = pair_spread(step)
    return dict(
        row=row, lane=lane, pos=pos, doc_of=doc_of, gate=gate, taps=taps, conv=conv, conv_sig=conv_sig,
        act=act, bc=bc, b_in=b_in, c_in=c_in, c_at=c_at, step=step, ends=ends, reach=reach,
        carry=carry, gram=gram, decays=decays, step_wide=step_wide, moved=act * step_wide,
    )


def mamba_forward_kernel(
    lengths_ref, xzb_ref, tail_ref, conv_ref, rate_ref, skip_ref, gated_ref, read_ref, states_ref, pad_ref, state_ref
):
    c = pl.program_id(0)

    @pl.when(c == 0)
    def _():
        state_ref[...] = jnp.zeros_like(state_ref)

    v = mamba_chunk(c, lengths_ref, xzb_ref, tail_ref, conv_ref, rate_ref, pad_ref)
    states_ref[0] = state_ref[STATE : 2 * STATE]
    moved = v["moved"]
    from_state = low_dot(v["c_at"], state_ref[...], (1, 0)) * pair_spread(v["reach"])
    tiles = []
    for p in range(PAIRS):
        mixing = jnp.concatenate(
            [(v["decays"](2 * p + j) * v["gram"]).astype(LOW) for j in range(2)], axis=1
        )
        tiles.append(dot_any(mixing, halves(moved[:, 128 * p : 128 * p + 128].astype(LOW)), (1, 0)))
    read = jnp.concatenate(tiles, axis=1) + from_state + skip_ref[0:1] * v["act"]
    read_ref[...] = read.astype(LOW)
    gated_ref[...] = (read * v["gate"] * jax.nn.sigmoid(v["gate"])).astype(LOW)
    added = low_dot(v["b_in"], moved * pair_spread(v["ends"]), (0, 0))[:STATE]
    state_ref[STATE : 2 * STATE] = pair_spread(v["carry"]) * state_ref[STATE : 2 * STATE] + added


def mamba_backward_kernel(
    lengths_ref, xzb_ref, tail_ref, conv_ref, rate_ref, skip_ref, states_ref, read_ref, d_gated_ref,
    d_xzb_ref, d_chan_ref, d_rate_ref, pad_ref, state_ref, d_state_ref, d_pad_ref,
):
    g = pl.program_id(0)
    c = pl.num_programs(0) - 1 - g

    @pl.when(g == 0)
    def _():
        state_ref[...] = jnp.zeros_like(state_ref)
        d_state_ref[...] = jnp.zeros_like(d_state_ref)
        d_pad_ref[...] = jnp.zeros_like(d_pad_ref)
        d_chan_ref[...] = jnp.zeros_like(d_chan_ref)
        d_rate_ref[...] = jnp.zeros_like(d_rate_ref)

    v = mamba_chunk(c, lengths_ref, xzb_ref, tail_ref, conv_ref, rate_ref, pad_ref)
    row, lane, act, moved, gate = v["row"], v["lane"], v["act"], v["moved"], v["gate"]
    state_ref[STATE : 2 * STATE] = states_ref[0]
    by_head = (iota((WIDE, 128), 0) // SSM_HEAD + STEP_AT == iota((WIDE, 128), 1)).astype(LOW)
    head_sum = lambda wide: dot_any(wide.astype(LOW), by_head, (1, 0))

    d_gated = d_gated_ref[...].astype(FULL)
    gate_sig = jax.nn.sigmoid(gate)
    d_read = d_gated * gate * gate_sig
    d_gate = d_gated * read_ref[...].astype(FULL) * gate_sig * (1.0 + gate * (1.0 - gate_sig))
    d_chan_ref[CONV : CONV + 1] += jnp.sum(d_read * act, axis=0, keepdims=True)
    d_act = skip_ref[0:1] * d_read

    d_log = jnp.zeros_like(v["gram"])
    d_log_t = jnp.zeros_like(v["gram"])
    d_gram = jnp.zeros_like(v["gram"])
    tiles = []
    for p in range(PAIRS):
        at = slice(128 * p, 128 * p + 128)
        d_pair = halves(d_read[:, at].astype(LOW))
        d_mixing = dot_any(d_pair, moved[:, at].astype(LOW), (1, 1))
        mixings = []
        for j in range(2):
            h = 2 * p + j
            decay = v["decays"](h)
            mixing = decay * v["gram"]
            d_one = d_mixing[CHUNK * j : CHUNK * (j + 1)]
            d_gram = d_gram + d_one * decay
            d_gap = d_one * mixing
            mixings.append(mixing.astype(LOW))
            d_log = d_log + jnp.where(lane == STEP_AT + h, jnp.sum(d_gap, axis=1, keepdims=True), 0.0)
            d_log_t = d_log_t + jnp.where(row == STEP_AT + h, jnp.sum(d_gap, axis=0, keepdims=True), 0.0)
        tiles.append(dot_any(jnp.concatenate(mixings, axis=0), d_pair, (0, 0)))
    d_moved = jnp.concatenate(tiles, axis=1)
    d_log = d_log - d_log_t.T

    d_product = d_read * pair_spread(v["reach"])
    state_low = state_ref[...].astype(LOW)
    product = dot_any(v["c_at"].astype(LOW), state_low, (1, 0))
    d_log = d_log + head_sum(d_product * product)
    d_c = low_dot(d_product, state_low, (1, 1)) + low_dot(d_gram, pltpu.roll(v["b_in"], STATE, 1), (1, 0))
    d_state_in = low_dot(v["c_at"], d_product, (0, 0))[STATE : 2 * STATE]

    d_state = d_state_ref[...]
    d_state_low = d_state.astype(LOW)
    ends_wide = pair_spread(v["ends"])
    d_put = dot_any(v["b_in"].astype(LOW), d_state_low, (1, 0)) * ends_wide
    d_b = low_dot(moved * ends_wide, d_state_low, (1, 1)) + low_dot(d_gram, v["c_in"], (0, 0))
    d_moved = d_moved + d_put
    d_ends = head_sum(d_put * moved)
    carry_wide = pair_spread(v["carry"])
    d_carry = head_sum(
        jnp.broadcast_to(
            jnp.sum(d_state[:STATE] * states_ref[0], axis=0, keepdims=True) * carry_wide, (16, WIDE)
        )
    )[0:1]
    d_last = jnp.sum(d_ends, axis=0, keepdims=True) + d_carry
    d_log = d_log - d_ends + jnp.where(row == CHUNK - 1, d_last, 0.0)
    d_state_ref[:STATE] = d_state_in + carry_wide * d_state[:STATE]

    d_act = d_act + d_moved * v["step_wide"]
    d_rate_step = lax.dot_general(
        (row >= lane).astype(FULL),
        d_log,
        (((0,), (0,)), ((), ())),
        precision=lax.Precision.HIGHEST,
        preferred_element_type=FULL,
    )
    d_step = head_sum(d_moved * act) - rate_ref[0:1] * d_rate_step
    d_rate_ref[0:1] += jnp.sum(-v["step"] * d_rate_step, axis=0, keepdims=True)
    is_step = (lane >= STEP_AT) & (lane < STEP_AT + LOCAL_HEADS)
    d_bc = d_b + d_c + jnp.where(is_step, d_step * jax.nn.sigmoid(v["bc"]), 0.0)

    d_conv = d_act * v["conv_sig"] * (1.0 + v["conv"] * (1.0 - v["conv_sig"]))
    d_pad_ref[0:CHUNK] = d_conv
    d_raw = jnp.zeros_like(d_conv)
    for k in range(CONV):
        ahead = CONV - 1 - k
        d_chan_ref[k : k + 1] += jnp.sum(d_conv * v["taps"][k], axis=0, keepdims=True)
        same = v["doc_of"](v["pos"]) == v["doc_of"](v["pos"] + ahead)
        d_raw = d_raw + conv_ref[k : k + 1] * jnp.where(same, d_pad_ref[ahead : ahead + CHUNK], 0.0)
    d_pad_ref[CHUNK : CHUNK + 8] = d_conv[0:8]

    moved_gate = pltpu.roll(jnp.concatenate([d_gate, jnp.zeros_like(row).astype(FULL)], axis=1), 64, 1)
    d_xzb_ref[:, : LOCAL_CH - 64] = d_raw[:, : LOCAL_CH - 64].astype(LOW)
    d_xzb_ref[:, LOCAL_CH - 64 : LOCAL_CH + 64] = (
        d_raw[:, LOCAL_CH - 64 :] + moved_gate[:, :128]
    ).astype(LOW)
    d_xzb_ref[:, LOCAL_CH + 64 : 2 * LOCAL_CH] = moved_gate[:, 128:WIDE].astype(LOW)
    d_xzb_ref[:, 2 * LOCAL_CH :] = d_bc.astype(LOW)


def mamba_specs(chunk_of):
    tail = lambda g: (jnp.maximum(chunk_of(g) * (CHUNK // 8) - 1, 0), 0)
    fixed = lambda shape: pl.BlockSpec(shape, lambda g: (0,) * len(shape))
    return [
        pl.BlockSpec(memory_space=pltpu.SMEM),
        pl.BlockSpec((CHUNK, XZB), lambda g: (chunk_of(g), 0)),
        pl.BlockSpec((8, XZB), tail),
        fixed((8, WIDE)),
        fixed((8, 128)),
        fixed((8, WIDE)),
    ]


def mamba_forward(lengths, xzb, conv_rows, rate_row, skip_row):
    total = xzb.shape[0]
    chunks = total // CHUNK
    by_chunk = lambda width: pl.BlockSpec((CHUNK, width), lambda g: (g, 0))
    return pl.pallas_call(
        mamba_forward_kernel,
        grid=(chunks,),
        in_specs=mamba_specs(lambda g: g),
        out_specs=[by_chunk(WIDE), by_chunk(WIDE), pl.BlockSpec((1, STATE, WIDE), lambda g: (g, 0, 0))],
        out_shape=[
            jax.ShapeDtypeStruct((total, WIDE), LOW),
            jax.ShapeDtypeStruct((total, WIDE), LOW),
            jax.ShapeDtypeStruct((chunks, STATE, WIDE), FULL),
        ],
        scratch_shapes=[pltpu.VMEM((8 + CHUNK, WIDE), FULL), pltpu.VMEM((CHUNK, WIDE), FULL)],
        compiler_params=pltpu.CompilerParams(vmem_limit_bytes=32 << 20),
        cost_estimate=pl.CostEstimate(flops=2 * 10**10, bytes_accessed=16 << 20, transcendentals=10**7),
    )(lengths, xzb, xzb, conv_rows, rate_row, skip_row)


def mamba_backward(lengths, xzb, conv_rows, rate_row, skip_row, states, read, d_gated):
    total = xzb.shape[0]
    chunks = total // CHUNK
    chunk_of = lambda g: chunks - 1 - g
    by_chunk = lambda width: pl.BlockSpec((CHUNK, width), lambda g: (chunk_of(g), 0))
    return pl.pallas_call(
        mamba_backward_kernel,
        grid=(chunks,),
        in_specs=mamba_specs(chunk_of)
        + [pl.BlockSpec((1, STATE, WIDE), lambda g: (chunk_of(g), 0, 0)), by_chunk(WIDE), by_chunk(WIDE)],
        out_specs=[
            by_chunk(XZB),
            pl.BlockSpec((8, WIDE), lambda g: (0, 0)),
            pl.BlockSpec((8, 128), lambda g: (0, 0)),
        ],
        out_shape=[
            jax.ShapeDtypeStruct((total, XZB), LOW),
            jax.ShapeDtypeStruct((8, WIDE), FULL),
            jax.ShapeDtypeStruct((8, 128), FULL),
        ],
        scratch_shapes=[
            pltpu.VMEM((8 + CHUNK, WIDE), FULL),
            pltpu.VMEM((CHUNK, WIDE), FULL),
            pltpu.VMEM((CHUNK, WIDE), FULL),
            pltpu.VMEM((8 + CHUNK, WIDE), FULL),
        ],
        compiler_params=pltpu.CompilerParams(vmem_limit_bytes=32 << 20),
        cost_estimate=pl.CostEstimate(flops=6 * 10**10, bytes_accessed=24 << 20, transcendentals=10**7),
    )(lengths, xzb, xzb, conv_rows, rate_row, skip_row, states, read, d_gated)


def head_under(h, at, value):
    row, lane = iota((QW, 128), 0), iota((QW, 128), 1)
    inside = (lane >= at) & (lane < at + HEAD) & (row == h * HEAD + lane - at)
    return jnp.where(inside, value, 0.0).astype(LOW)


def row_block(t):
    return jnp.where(t < SEQ, t, lax.axis_index("seq"))


def allowed_keys(lengths_ref, block, rows, extent):
    first_end = lengths_ref[0, 0]
    second_end = first_end + lengths_ref[0, 1]
    row = block * rows + iota((rows, 1), 0)
    start = jnp.where(row >= second_end, second_end, jnp.where(row >= first_end, first_end, 0))
    least = jnp.maximum(start, row - (WINDOW - 1))
    key = iota((rows, extent), 1)
    return (key >= least) & (key <= row)


def for_extent(block, rows, run):
    for e in range(SEQ):
        pl.when(block == e)(lambda e=e: run((e + 1) * rows))


def attention_forward_kernel(lengths_ref, q_ref, kv_ref, out_ref, log_ref):
    t, h = pl.program_id(0), pl.program_id(1)
    rows = q_ref.shape[0]
    block = row_block(t)

    def run(extent):
        q = dot_any(q_ref[...], head_under(h, 0, HEAD ** (-0.5)), (1, 0)).astype(LOW)
        kv = kv_ref[:extent]
        scores = dot_any(q, kv, (1, 1))
        scores = jnp.where(allowed_keys(lengths_ref, block, rows, extent), scores, MASKED)
        top = jnp.max(scores, axis=1, keepdims=True)
        expos = jnp.exp(scores - top)
        denom = jnp.sum(expos, axis=1, keepdims=True)
        mixed = dot_any((expos * (1.0 / denom)).astype(LOW), kv, (1, 0)).astype(LOW)
        out = dot_any(mixed, head_under(h, HEAD, 1.0), (1, 1)).astype(LOW)
        log = jnp.where(iota((rows, 128), 1) == h, top + jnp.log(denom), 0.0)

        @pl.when(h == 0)
        def _():
            out_ref[...] = out
            log_ref[...] = log

        @pl.when(h > 0)
        def _():
            out_ref[...] += out
            log_ref[...] += log

    for_extent(block, rows, run)


def attention_backward_kernel(
    lengths_ref, q_ref, kv_ref, out_ref, log_ref, d_out_ref, d_q_ref, d_kv_ref, sum_ref
):
    t, h = pl.program_id(0), pl.program_id(1)
    rows = q_ref.shape[0]
    block = row_block(t)

    @pl.when((h == 0) & ((t == 0) | (t == SEQ)))
    def _():
        sum_ref[...] = jnp.zeros_like(sum_ref)

    def run(extent):
        under_q = head_under(h, 0, HEAD ** (-0.5))
        q = dot_any(q_ref[...], under_q, (1, 0)).astype(LOW)
        d_out = dot_any(d_out_ref[...], head_under(h, HEAD, 1.0), (1, 0)).astype(LOW)
        log = jnp.sum(jnp.where(iota((rows, 128), 1) == h, log_ref[...], 0.0), axis=1, keepdims=True)
        own = iota((rows, QW), 1) // HEAD == h
        product = d_out_ref[...].astype(FULL) * out_ref[...].astype(FULL)
        d_total = jnp.sum(jnp.where(own, product, 0.0), axis=1, keepdims=True)
        kv = kv_ref[:extent]
        scores = dot_any(q, kv, (1, 1))
        allowed = allowed_keys(lengths_ref, block, rows, extent)
        probs = jnp.exp(jnp.where(allowed, scores - log, MASKED))
        d_probs = dot_any(d_out, kv, (1, 1))
        d_scores = (probs * (d_probs - d_total)).astype(LOW)
        sum_ref[:extent] += dot_any(probs.astype(LOW), d_out, (0, 0)) + dot_any(d_scores, q, (0, 0))
        d_q = dot_any(dot_any(d_scores, kv, (1, 0)).astype(LOW), under_q, (1, 1)).astype(LOW)

        @pl.when(h == 0)
        def _():
            d_q_ref[...] = d_q

        @pl.when(h > 0)
        def _():
            d_q_ref[...] += d_q

    for_extent(block, rows, run)

    @pl.when((h == GROUP_HEADS - 1) & (t >= SEQ - 1))
    def _():
        d_kv_ref[...] = sum_ref[...].astype(LOW)


def attention_specs(rows, group):
    by_step = lambda width: pl.BlockSpec((rows, width), lambda t, h: (t, 0))
    kv_block = pl.BlockSpec((group, 128), lambda t, h: (0, t // SEQ))
    return by_step, kv_block


def attention_forward(lengths, queries, kv, rows):
    by_step, kv_block = attention_specs(rows, kv.shape[0])
    return pl.pallas_call(
        attention_forward_kernel,
        grid=(SEQ + 1, GROUP_HEADS),
        in_specs=[pl.BlockSpec(memory_space=pltpu.SMEM), by_step(QW), kv_block],
        out_specs=[by_step(QW), by_step(128)],
        out_shape=[
            jax.ShapeDtypeStruct(queries.shape, LOW),
            jax.ShapeDtypeStruct((queries.shape[0], 128), FULL),
        ],
        compiler_params=pltpu.CompilerParams(vmem_limit_bytes=32 << 20),
        cost_estimate=pl.CostEstimate(flops=4 * 10**10, bytes_accessed=4 << 20, transcendentals=8 * 10**6),
    )(lengths, queries, kv)


def attention_backward(lengths, queries, kv, out, logs, d_out, rows, parts, collective_id):
    group = kv.shape[0]
    by_step, kv_block = attention_specs(rows, group)
    total = lax.axis_size("dp")
    beside = parts if total == 8 else []
    count, line = len(beside), total // 2
    pieces = pieces_of(beside, 1)

    def kernel(*refs):
        own_in, parts_in = refs[:6], refs[6 : 6 + count]
        own_out, sums_out = refs[6 + count : 8 + count], refs[8 + count : 8 + 2 * count]
        sum_ref, transfer = refs[8 + 2 * count], refs[9 + 2 * count :]
        step = pl.program_id(0) * GROUP_HEADS + pl.program_id(1)
        steps = (SEQ + 1) * GROUP_HEADS
        phases = scatter_phases(pieces, line, parts_in + sums_out + transfer) if count else []
        spots = [min(13 * k, steps - 1) for k in range(len(phases))]
        for phase, spot in zip(phases, spots):
            if spot < steps - 1:
                pl.when(step == spot)(phase)
        attention_backward_kernel(*own_in, *own_out, sum_ref)
        for phase, spot in zip(phases, spots):
            if spot == steps - 1:
                pl.when(step == spot)(phase)

    found = pl.pallas_call(
        kernel,
        grid=(SEQ + 1, GROUP_HEADS),
        in_specs=[pl.BlockSpec(memory_space=pltpu.SMEM), by_step(QW), kv_block]
        + [by_step(QW), by_step(128), by_step(QW)]
        + [pl.BlockSpec(memory_space=pl.ANY)] * count,
        out_specs=[by_step(QW), kv_block] + [pl.BlockSpec(memory_space=pltpu.VMEM)] * count,
        out_shape=[jax.ShapeDtypeStruct(queries.shape, LOW), jax.ShapeDtypeStruct(kv.shape, LOW)]
        + [jax.ShapeDtypeStruct(p.shape[1:], FULL) for p in beside],
        scratch_shapes=[pltpu.VMEM((group, 128), FULL)]
        + (scatter_scratch(beside, pieces, line) if count else []),
        compiler_params=pltpu.CompilerParams(
            vmem_limit_bytes=56 << 20,
            **(dict(collective_id=collective_id, has_side_effects=True) if count else {}),
        ),
        cost_estimate=pl.CostEstimate(flops=10**11, bytes_accessed=8 << 20, transcendentals=8 * 10**6),
    )(lengths, queries, kv, out, logs, d_out, *beside)
    return found[0], found[1], list(found[2:]) if count else scatter_dp(parts, collective_id)


def pick(options, seq_index):
    return lax.select_n(seq_index, *options)


def own_cut(values, seq_index, axis, unit):
    cuts = []
    for first, count in zip(FIRST_HEAD, HEAD_COUNT):
        cut = lax.slice_in_dim(values, first * unit, (first + count) * unit, axis=axis)
        pads = [(0, 0)] * values.ndim
        pads[axis] = (0, (LOCAL_HEADS - count) * unit)
        cuts.append(jnp.pad(cut, pads))
    return pick(cuts, seq_index)


def own_spread(values, seq_index, unit):
    spreads = []
    for first, count in zip(FIRST_HEAD, HEAD_COUNT):
        pads = [(0, 0)] * (values.ndim - 1) + [(first * unit, (SSM_HEADS - first - count) * unit)]
        spreads.append(jnp.pad(values[..., : count * unit], pads))
    return pick(spreads, seq_index)


def channel_cut(wide, seq_index, axis):
    return own_cut(wide, seq_index, axis, SSM_HEAD)


def bcdt_cut(w_bcdt, seq_index):
    first = pick([jnp.int32(h) for h in FIRST_HEAD], seq_index)
    count = pick([jnp.int32(c) for c in HEAD_COUNT], seq_index)
    source = jnp.arange(w_bcdt.shape[1], dtype=jnp.int32)[:, None]
    target = jnp.arange(BCDT_PAD, dtype=jnp.int32)[None]
    shared = (target < 2 * STATE) & (source == target)
    steps = (target >= 2 * STATE) & (target < 2 * STATE + count) & (source == target + first)
    return mm(w_bcdt, (shared | steps).astype(LOW)).astype(LOW)


def rows_by_peer_kernel(mamba_ref, o_ref, *refs):
    outs, held, load_sem, store_sem = refs[:SEQ], *refs[SEQ:]
    me = lax.axis_index("seq")
    shared = (KV_HEADS - 1) * QW

    def loads(p):
        own = HEAD_COUNT[p] * SSM_HEAD
        parts = [
            (mamba_ref, FIRST_HEAD[p] * SSM_HEAD, OUT_AT, own),
            (o_ref, p * QW, O_AT, QW),
            (o_ref, shared, O5_AT, QW),
        ]
        return [
            pltpu.make_async_copy(
                source.at[pl.ds(at, count)], held.at[p, pl.ds(to, count)], load_sem.at[p, k]
            )
            for k, (source, at, to, count) in enumerate(parts)
        ]

    for p in range(SEQ):
        for load in loads(p):
            load.start()
        for start, end in ((HEAD_COUNT[p] * SSM_HEAD, O_AT), (O_AT + QW, O5_AT)):
            held[p, start:end] = jnp.zeros((end - start, held.shape[2]), held.dtype)

    def stores(act):
        for p in range(SEQ):
            if act == "start":
                for load in loads(p):
                    load.wait()
            for k in range(SEQ):
                copy = pltpu.make_async_copy(held.at[p], outs[k], store_sem.at[p])
                pl.when(jnp.bitwise_xor(me, p) == k)(copy.start if act == "start" else copy.wait)

    stores("start")
    stores("wait")


def rows_by_peer(mamba_cols, o_cols):
    block = (OUT_WIDTH, o_cols.shape[1])
    anywhere = pl.BlockSpec(memory_space=pl.ANY)
    return pl.pallas_call(
        rows_by_peer_kernel,
        in_specs=[anywhere] * 2,
        out_specs=[anywhere] * SEQ,
        out_shape=[jax.ShapeDtypeStruct(block, LOW)] * SEQ,
        scratch_shapes=[
            pltpu.VMEM((SEQ,) + block, LOW),
            pltpu.SemaphoreType.DMA((SEQ, 3)),
            pltpu.SemaphoreType.DMA((SEQ,)),
        ],
        compiler_params=pltpu.CompilerParams(vmem_limit_bytes=32 << 20),
        cost_estimate=pl.CostEstimate(flops=0, bytes_accessed=12 << 20, transcendentals=0),
    )(mamba_cols, o_cols)


def wide_kernel(*refs):
    pieces, out = refs[:SEQ], refs[SEQ]
    me, width = lax.axis_index("seq"), pieces[0].shape[1]
    for j in range(SEQ):
        for k in range(SEQ):

            @pl.when(jnp.bitwise_xor(me, j) == k)
            def _():
                out[:, width * j : width * (j + 1)] = pieces[k][...]


def wide_of(arrivals):
    rows, width = arrivals[0].shape
    block = rows if rows < 400 else 400
    return pl.pallas_call(
        wide_kernel,
        grid=(rows // block,),
        in_specs=[pl.BlockSpec((block, width), lambda i: (i, 0))] * SEQ,
        out_specs=pl.BlockSpec((block, SEQ * width), lambda i: (i, 0)),
        out_shape=jax.ShapeDtypeStruct((rows, SEQ * width), arrivals[0].dtype),
        cost_estimate=pl.CostEstimate(flops=0, bytes_accessed=16 * rows * width, transcendentals=0),
    )(*arrivals)


def on_device(
    tokens_in,
    doc_lengths,
    norm_gains,
    w_qkv,
    w_o,
    w_xz,
    w_bcdt,
    conv_w,
    ssm_rate,
    ssm_skip,
    w_out,
    w_gate_up,
    w_down,
    cotangent,
):
    rows = tokens_in.shape[0]
    group = rows * SEQ
    s = lax.axis_index("seq")
    dp_index = lax.axis_index("dp")
    dp_total = lax.axis_size("dp")
    block_rows = w_qkv.shape[0]
    kv_width = KV_HEADS * HEAD
    lengths = doc_lengths[0]
    live = (jnp.arange(rows, dtype=jnp.int32) + s * rows < lengths[0] + lengths[1]).astype(FULL)[:, None]

    gains_block = norm_gains.shape[1]
    conv_block = conv_w.shape[1]
    width = -(-max(conv_block, gains_block) // 128) * 128
    small = jnp.concatenate(
        [
            jnp.pad(conv_w, ((0, 4), (0, width - conv_block))),
            jnp.pad(norm_gains, ((0, 4), (0, width - gains_block))),
        ]
    )
    out_block = w_out.shape[0]
    qkv_far, qkv_near = swap(w_qkv, "seq", 2), swap(w_qkv, "seq", 1)
    x_part, z_part = trade_halves(
        w_xz[:, :LOCAL_CH], jnp.pad(w_xz[:, LOCAL_CH:], ((0, 0), (0, 2 * LOCAL_CH - w_xz.shape[1])))
    )
    tokens_far, tokens_near = swap(tokens_in, "seq", 2), swap(tokens_in, "seq", 1)
    small, o_cols, mamba_cols = gather_dp([small, w_o, w_out], 0)
    small, o_cols, mamba_cols, qkv_far, qkv_near, x_part, z_part, tokens_far, tokens_near = lax.optimization_barrier(
        (small, o_cols, mamba_cols, qkv_far, qkv_near, x_part, z_part, tokens_far, tokens_near)
    )
    qkv_shards = [w_qkv, qkv_near, qkv_far, swap(qkv_far, "seq", 1)]
    token_blocks = [tokens_in, tokens_near, tokens_far, swap(tokens_far, "seq", 1)]
    full_conv = small[:, :4, :conv_block].transpose(1, 0, 2).reshape(4, INNER).astype(FULL)
    gains = small[:, 8:12, :gains_block].transpose(1, 0, 2).reshape(4, D).astype(FULL)
    tokens_group = place(list(zip(seq_order(), token_blocks))).reshape(group, D)
    normed = norm_rows(tokens_group, gains[0])
    qkv_wide = wide_of(qkv_shards)
    q_at = lambda h: lax.dynamic_slice_in_dim(qkv_wide, h * QW, QW, 1)
    kv_at = lambda h: [
        lax.dynamic_slice_in_dim(qkv_wide, D + h * HEAD, HEAD, 1),
        lax.dynamic_slice_in_dim(qkv_wide, D + kv_width + h * HEAD, HEAD, 1),
    ]
    qkv_packet = jnp.concatenate(kv_at(s) + kv_at(KV_HEADS - 1) + [q_at(s), q_at(KV_HEADS - 1)], axis=1)
    xz_packet = jnp.concatenate([x_part, z_part, bcdt_cut(w_bcdt, s)], axis=1)
    full_qkv, full_xz = gather_dp([qkv_packet, xz_packet], 1)
    gate_up_packet = jnp.pad(w_gate_up, ((0, 0), (0, 0), (0, UNITS_PAD - UNITS))).reshape(block_rows, -1)
    down_packet = jnp.pad(w_down, ((0, 0), (0, UNITS_PAD - UNITS)))
    d_total = cotangent.astype(FULL) * live
    d_ffn = d_total.astype(LOW)
    d_ffn_far, d_ffn_near = swap(d_ffn, "seq", 2), swap(d_ffn, "seq", 1)
    full_qkv, full_xz, o_cols, mamba_cols, gate_up_packet, down_packet, d_ffn_far, d_ffn_near = (
        lax.optimization_barrier(
            (full_qkv, full_xz, o_cols, mamba_cols, gate_up_packet, down_packet, d_ffn_far, d_ffn_near)
        )
    )
    d_ffn_group = jnp.concatenate([d_ffn, d_ffn_near, d_ffn_far, swap(d_ffn_far, "seq", 1)])
    full_qkv = full_qkv.reshape(D, -1)
    full_xz = full_xz.reshape(D, -1)
    full_gate_up = gather_dp_apart(gate_up_packet)
    full_down = gather_dp_apart(down_packet)


    own = lambda a: lax.dynamic_slice_in_dim(a, s * rows, rows, 0)
    normed_own = own(normed)
    kvq = mm(normed, full_qkv[:, : 256 + QW]).astype(LOW)
    q_last = mm(normed_own, full_qkv[:, 256 + QW :]).astype(LOW)
    queries = jnp.concatenate([kvq[:, 256:], q_last])
    kv = kvq[:, :256]
    out_blocks = list(rows_by_peer(mamba_cols.reshape(INNER, -1), o_cols.reshape(D, -1)))
    out_blocks, queries = meet(out_blocks, queries)
    attended, logs = attention_forward(doc_lengths, queries, kv, rows)
    out_pieces = out_blocks[:1] + [swap(out_blocks[bit], "seq", bit) for bit in (1, 2, 3)]
    out_rows = wide_of(after(out_pieces, attended))
    w_out_rows = out_rows[:WIDE]
    w_o_rows = out_rows[O_AT : O_AT + QW]
    w_o5_rows = out_rows[O5_AT:]
    attn_part = mm(attended[:group], w_o_rows).astype(LOW)
    normed_now, attn_part = lax.optimization_barrier((normed, attn_part))
    attn_keep, attn_got = scatter_begin(attn_part)

    xzb = mm(normed_now, full_xz)
    attn_held, attn_far = scatter_far(attn_keep, after(attn_got, xzb))
    xzb, attn_held = lax.optimization_barrier((xzb, attn_held))
    conv_rows = jnp.pad(channel_cut(full_conv, s, 1), ((0, 4), (0, WIDE - LOCAL_CH)))
    rate_row = jnp.pad(own_cut(ssm_rate, s, 0, 1), (STEP_AT, 128 - STEP_AT - LOCAL_HEADS))
    rate_row = jnp.broadcast_to(rate_row, (8, 128))
    skip_row = jnp.pad(jnp.repeat(own_cut(ssm_skip, s, 0, 1), SSM_HEAD), (0, WIDE - LOCAL_CH))
    skip_row = jnp.broadcast_to(skip_row, (8, WIDE))
    mamba_in = (doc_lengths, xzb, conv_rows, rate_row, skip_row)
    gated, read, states = mamba_forward(*mamba_in)
    gated, attn_far = meet(gated, attn_far)
    ssm_held, ssm_far = scatter_far(*scatter_begin(mm(gated, w_out_rows)))
    attn_o = scatter_end(attn_held, attn_far) + mm(attended[group:], w_o5_rows)
    ssm_o = scatter_end(ssm_held, ssm_far)

    inputs_x = tokens_in.astype(FULL)
    (residual, normed_two), pull_join = jax.vjp(join_tail, inputs_x, attn_o, ssm_o, gains)
    normed_two, d_act = seq_arrivals(normed_two.astype(LOW), mm(d_ffn_group, full_down))
    normed_two = jnp.concatenate(normed_two)
    gate_up = mm(normed_two, full_gate_up)
    ffn_gate, ffn_up = gate_up[:, :UNITS_PAD], gate_up[:, UNITS_PAD:]
    ffn_act = (jax.nn.silu(ffn_gate) * ffn_up).astype(LOW)

    sig = jax.nn.sigmoid(ffn_gate)
    d_gate = d_act * ffn_up * (sig * (1.0 + ffn_gate * (1.0 - sig)))
    d_up = d_act * ffn_gate * sig
    d_gate_up = jnp.concatenate([d_gate.astype(LOW), d_up.astype(LOW)], axis=1)
    two_keep, two_got = relative_begin(mm_nt(d_gate_up, full_gate_up))
    two_got, grad_down_part = meet(two_got, mm_tn(d_ffn_group, ffn_act).astype(LOW))
    two_held, two_far = relative_far(two_keep, two_got)
    two_far, grad_gate_up_part = meet(two_far, mm_tn(normed_two, d_gate_up).astype(LOW))
    d_normed_two = scatter_end(two_held, two_far)
    grad_gate_up_sum = scatter_dp_apart(grad_gate_up_part)
    grad_down_sum = scatter_dp_apart(grad_down_part)
    grad_gate_up = grad_gate_up_sum.reshape(block_rows, 2, UNITS_PAD)[:, :, :UNITS]
    grad_down = grad_down_sum[:, :UNITS]

    d_x_tail, d_attn_o, d_ssm_o, d_gains = pull_join((d_total, d_normed_two))
    ssm_arrivals, ffn_part = seq_arrivals(d_ssm_o.astype(LOW), mm_nt(ffn_act, full_down).astype(LOW))
    d_attn_own = after(d_attn_o.astype(LOW), ssm_arrivals[2])
    attn_near, attn_away = swap(d_attn_own, "seq", 1), swap(d_attn_own, "seq", 2)
    d_ssm = place(list(zip(seq_order(), ssm_arrivals))).reshape(group, D)
    d_gated = mm_nt(d_ssm, w_out_rows).astype(LOW)

    def send_columns(grad):
        width = D // SEQ
        blocks = [grad[:, width * j : width * (j + 1)] for j in range(SEQ)]
        return [with_layout_constraint(pick(blocks, s ^ k), Layout((0, 1))) for k in range(SEQ)]

    def trade(blocks):
        return blocks[:1] + [swap(blocks[bit], "seq", bit) for bit in (1, 2, 3)]

    mamba_blocks, d_gated = meet(send_columns(mm_tn(gated, d_ssm).astype(LOW)), d_gated)
    mamba_pieces = trade(mamba_blocks)
    (mamba_pieces[1], attn_near), d_gated = meet((mamba_pieces[1], attn_near), d_gated)
    d_xzb, d_chan, d_rate = mamba_backward(*mamba_in, states, read, d_gated)
    (mamba_pieces[2:], attn_away), d_xzb = meet((mamba_pieces[2:], attn_away), d_xzb)
    ffn_keep, ffn_got = relative_begin(ffn_part)
    attn_arrivals = [d_attn_own, attn_near, attn_away, swap(attn_away, "seq", 1)]
    arrived = place(list(zip(seq_order(), mamba_pieces)))
    grad_out_part = jnp.concatenate(
        [arrived[j, : HEAD_COUNT[j] * SSM_HEAD] for j in range(SEQ)]
    ).reshape(dp_total, out_block, -1)

    d_attn = place(list(zip(seq_order(), attn_arrivals))).reshape(group, D)
    d_attended = jnp.concatenate([mm_nt(d_attn, w_o_rows), mm_nt(d_attn_own, w_o5_rows)]).astype(LOW)
    head_blocks = send_columns(
        jnp.concatenate([mm_tn(attended[:group], d_attn), mm_tn(attended[group:], d_attn_own)]).astype(LOW)
    )
    head_blocks, d_attended = meet(head_blocks, d_attended)
    head_pieces = trade(head_blocks)
    ffn_got, d_attended = meet(ffn_got, d_attended)
    ffn_held, ffn_far = relative_far(ffn_keep, ffn_got)
    ffn_held, d_attended = meet(ffn_held, d_attended)
    d_conv = d_chan[:CONV, :LOCAL_CH]
    d_skip = jnp.sum(d_chan[CONV, :LOCAL_CH].reshape(LOCAL_HEADS, SSM_HEAD), axis=1)
    d_rate = d_rate[0, STEP_AT : STEP_AT + LOCAL_HEADS]
    grad_xz_part = mm_tn(normed, d_xzb).astype(LOW).reshape(dp_total, block_rows, -1)

    d_queries, d_kv, (grad_xz_sum, grad_out) = attention_backward(
        doc_lengths, queries, kv, attended, logs, d_attended, rows, [grad_xz_part, grad_out_part], 3
    )
    (head_pieces, ffn_far), d_queries = meet((head_pieces, ffn_far), d_queries)
    mixed_out = ((residual + scatter_end(ffn_held, ffn_far)) * live).astype(LOW)
    arrived = place(list(zip(seq_order(), head_pieces)))
    grad_o_part = jnp.concatenate(
        [arrived[j, :QW] for j in range(SEQ)] + [jnp.sum(arrived[:, QW:].astype(FULL), axis=0).astype(LOW)]
    ).reshape(dp_total, block_rows, -1)
    d_kvq = jnp.concatenate([d_kv, d_queries[:group]], axis=1)
    d_q_last = d_queries[group:]
    grad_qkv_part = jnp.concatenate(
        [mm_tn(normed, d_kvq).astype(LOW), mm_tn(normed_own, d_q_last).astype(LOW)], axis=1
    ).reshape(dp_total, block_rows, -1)
    d_normed_part = mm_nt(d_xzb, full_xz) + mm_nt(d_kvq, full_qkv[:, : 256 + QW])
    d_normed_own = mm_nt(d_q_last, full_qkv[:, 256 + QW :])

    tokens_wide = tokens_group.astype(FULL)
    unit = tokens_wide * lax.rsqrt(jnp.mean(tokens_wide * tokens_wide, axis=-1, keepdims=True) + NORM_EPS)
    d_gain_first = jnp.sum(d_normed_part * unit, axis=0) + jnp.sum(d_normed_own * own(unit), axis=0)
    d_gains = d_gains.at[0].add(d_gain_first)
    by_dp = lambda a: a.reshape(a.shape[0], dp_total, -1).transpose(1, 0, 2)
    d_heads = jnp.concatenate([own_spread(d_rate, s, 1), own_spread(d_skip, s, 1)])[None]
    small_part = jnp.concatenate(
        [
            jnp.pad(by_dp(own_spread(d_conv, s, SSM_HEAD)), ((0, 0), (0, 0), (0, width - conv_block))),
            jnp.pad(by_dp(d_gains), ((0, 0), (0, 0), (0, width - gains_block))),
            jnp.broadcast_to(
                jnp.pad(d_heads, ((0, 7), (0, width - d_heads.shape[1])))[None], (dp_total, 8, width)
            ),
        ],
        axis=1,
    )
    normed_keep, normed_got = scatter_begin(d_normed_part)
    normed_got, grad_qkv_part = meet(normed_got, grad_qkv_part)
    normed_held, normed_far = scatter_far(normed_keep, normed_got)
    grad_o_part, normed_held = meet(grad_o_part, normed_held)
    grad_qkv_sum, grad_o, small_sum = scatter_dp([grad_qkv_part, grad_o_part, small_part], 2)
    normed_far, small_sum = meet(normed_far, small_sum)
    small_sum = small_sum + swap(small_sum, "seq", 1)
    small_sum = small_sum + swap(small_sum, "seq", 2)
    grad_xz_sum = grad_xz_sum.astype(LOW)
    first, last = trade_back(grad_xz_sum[:, :LOCAL_CH], grad_xz_sum[:, LOCAL_CH : 2 * LOCAL_CH])
    grad_xz = jnp.concatenate([first, last], axis=1)[:, : w_xz.shape[1]].astype(FULL)
    both_all = gather_seq(jnp.concatenate([grad_qkv_sum.astype(LOW), grad_xz_sum[:, 2 * LOCAL_CH :]], axis=1))
    bcdt_all = both_all[:, :, grad_qkv_sum.shape[1] :].astype(FULL)
    grad_bcdt = jnp.concatenate(
        [jnp.sum(bcdt_all[:, :, : 2 * STATE], axis=0)]
        + [bcdt_all[j, :, 2 * STATE : 2 * STATE + HEAD_COUNT[j]] for j in range(SEQ)],
        axis=1,
    )
    qkv_all = both_all[:, :, : grad_qkv_sum.shape[1]].astype(FULL)
    col = lambda j, at, width: qkv_all[j, :, at : at + width]
    shared = lambda at, width: jnp.sum(qkv_all[:, :, at : at + width], axis=0)
    grad_qkv_wide = jnp.concatenate(
        [col(j, 256, QW) for j in range(SEQ)]
        + [shared(256 + QW, QW)]
        + [col(j, 0, HEAD) for j in range(SEQ)]
        + [shared(128, HEAD)]
        + [col(j, HEAD, HEAD) for j in range(SEQ)]
        + [shared(128 + HEAD, HEAD)],
        axis=1,
    )
    qkv_width = w_qkv.shape[1]
    grad_qkv = lax.dynamic_slice_in_dim(grad_qkv_wide, s * qkv_width, qkv_width, 1)

    d_normed = scatter_end(normed_held, normed_far) + d_normed_own
    d_unit = d_normed * gains[0]
    scale = lax.rsqrt(jnp.mean(inputs_x * inputs_x, axis=-1, keepdims=True) + NORM_EPS)
    d_x_head = scale * (
        d_unit - inputs_x * scale * scale * jnp.mean(d_unit * inputs_x, axis=-1, keepdims=True)
    )
    input_grad = (d_x_tail + d_x_head).astype(LOW)
    grad_conv = small_sum[:CONV, :conv_block]
    grad_gains = small_sum[CONV : CONV + 4, :gains_block]
    grad_rate = small_sum[8, :SSM_HEADS]
    grad_skip = small_sum[8, SSM_HEADS : 2 * SSM_HEADS]
    return (
        mixed_out,
        input_grad,
        grad_gains,
        grad_qkv,
        grad_o,
        grad_xz,
        grad_bcdt,
        grad_conv,
        grad_rate,
        grad_skip,
        grad_out,
        grad_gate_up,
        grad_down,
    )


def solution(mesh):
    placed = (
        P(("dp", "seq"), None),
        P("dp", None),
        P(None, "dp"),
        P("dp", "seq"),
        P("dp", "seq"),
        P("dp", "seq"),
        P("dp", None),
        P(None, "dp"),
        P(),
        P(),
        P("dp", "seq"),
        P("dp", None, "seq"),
        P("dp", "seq"),
        P(("dp", "seq"), None),
    )
    return jax.shard_map(
        on_device,
        mesh=mesh,
        in_specs=placed,
        out_specs=(
            P(("dp", "seq"), None),
            P(("dp", "seq"), None),
            P(None, "dp"),
            P("dp", "seq"),
            P("dp", "seq"),
            P("dp", "seq"),
            P("dp", None),
            P(None, "dp"),
            P(),
            P(),
            P("dp", "seq"),
            P("dp", None, "seq"),
            P("dp", "seq"),
        ),
        check_vma=False,
    )
```

```python
import jax
import jax.numpy as jnp
from jax import lax
from jax.experimental import pallas as pl
from jax.experimental.layout import Layout, with_layout_constraint
from jax.experimental.pallas import tpu as pltpu
from jax.sharding import PartitionSpec as P

D = 1600
HEADS = 25
KV_HEADS = 5
HEAD = 64
INNER = 3200
SSM_HEAD = 64
STATE = 16
CONV = 4
FF = 5504
WINDOW = 1024
SSM_HEADS = 50

NORM_EPS = 1e-05
MASKED = -1e30
LOW = jnp.bfloat16
FULL = jnp.float32

SEQ = 4
GROUP_HEADS = HEADS // KV_HEADS
QW = GROUP_HEADS * HEAD
LOCAL_HEADS = 13
LOCAL_CH = LOCAL_HEADS * SSM_HEAD
CHUNK = 128
UNITS = FF // SEQ
UNITS_PAD = 1408
BCDT_PAD = 128
OUT_AT, O_AT, O5_AT, OUT_WIDTH = 0, 896, 1280, 1600
FIRST_HEAD = tuple((SSM_HEADS * s // 2 + 1) // 2 for s in range(SEQ))
HEAD_COUNT = tuple(b - a for a, b in zip(FIRST_HEAD, FIRST_HEAD[1:] + (SSM_HEADS,)))


def swap(value, axis, bit):
    return lax.ppermute(value, axis, [(i, i ^ bit) for i in range(lax.axis_size(axis))])


def place_kernel(count, index_ref, *refs):
    blocks, stacked, held, in_sems, out_sems = refs[:count], *refs[count:]
    loads = [
        pltpu.make_async_copy(block, held.at[i], in_sems.at[i]) for i, block in enumerate(blocks)
    ]
    stores = [
        pltpu.make_async_copy(held.at[i], stacked.at[index_ref[i]], out_sems.at[i])
        for i in range(count)
    ]
    for load in loads:
        load.start()
    for load, store in zip(loads, stores):
        load.wait()
        store.start()
    for store in stores:
        store.wait()


def place(blocks):
    count = len(blocks)
    block = blocks[0][1]
    anywhere = pl.BlockSpec(memory_space=pl.ANY)
    return pl.pallas_call(
        lambda *refs: place_kernel(count, *refs),
        out_shape=jax.ShapeDtypeStruct((count,) + block.shape, block.dtype),
        grid_spec=pltpu.PrefetchScalarGridSpec(
            num_scalar_prefetch=1,
            grid=(1,),
            in_specs=[anywhere] * count,
            out_specs=anywhere,
            scratch_shapes=[
                pltpu.VMEM((count,) + block.shape, block.dtype),
                pltpu.SemaphoreType.DMA((count,)),
                pltpu.SemaphoreType.DMA((count,)),
            ],
        ),
        compiler_params=pltpu.CompilerParams(vmem_limit_bytes=32 << 20),
        cost_estimate=pl.CostEstimate(
            flops=0, bytes_accessed=2 * count * block.size * block.dtype.itemsize, transcendentals=0
        ),
    )(jnp.stack([jnp.asarray(i, jnp.int32) for i, _ in blocks]), *[b for _, b in blocks])


def seq_order():
    me = lax.axis_index("seq")
    return [me, me ^ 1, me ^ 2, me ^ 3]


def seq_arrivals(block, beside=None):
    far, near = swap(block, "seq", 2), swap(block, "seq", 1)
    if beside is not None:
        far, beside = meet(far, beside)
    blocks = [block, near, far, swap(far, "seq", 1)]
    return blocks if beside is None else (blocks, beside)


def gather_seq(block):
    return place(list(zip(seq_order(), seq_arrivals(block))))


def scatter_begin(part):
    core = lax.axis_index("seq") % 2
    part = with_layout_constraint(part.astype(LOW), Layout((0, 1)))
    by_core = part.reshape((2, 2, part.shape[0] // SEQ) + part.shape[1:])
    give = lax.dynamic_index_in_dim(by_core, 1 - core, 1, False)
    keep = lax.dynamic_index_in_dim(by_core, core, 1, False)
    return keep, swap(give, "seq", 1)


def scatter_far(keep, got):
    far = lax.axis_index("seq") // 2
    at = lambda a, i: lax.dynamic_index_in_dim(a, i, 0, False).astype(FULL)
    give_far = (at(keep, 1 - far) + at(got, 1 - far)).astype(LOW)
    return at(keep, far) + at(got, far), swap(give_far, "seq", 2)


def scatter_end(held, got_far):
    return held + got_far.astype(FULL)


def relative_begin(part):
    part = with_layout_constraint(part.astype(LOW), Layout((0, 1)))
    rows = part.shape[0] // SEQ
    block = lambda k: part[rows * k : rows * (k + 1)]
    got = swap(jnp.concatenate([block(1), block(3)]), "seq", 1)
    return (block(0), block(2)), got


def relative_far(keep, got):
    rows = got.shape[0] // 2
    add = lambda k: keep[k].astype(FULL) + got[rows * k : rows * (k + 1)].astype(FULL)
    return add(0), swap(add(1).astype(LOW), "seq", 2)


def meet(one, two):
    return lax.optimization_barrier((one, two))


def after(values, done):
    return lax.optimization_barrier((values, done))[0]


def line_place():
    me = lax.axis_index("dp")
    return lax.axis_size("dp") // 2, me // 2, lax.rem(me, 2)


def greet(line, z, x):
    barrier = pltpu.get_barrier_semaphore()

    def signal(target):
        pl.semaphore_signal(
            barrier, inc=1, device_id={"dp": target}, device_id_type=pl.DeviceIdType.MESH
        )

    signal(2 * z + 1 - x)
    pl.when(z > 0)(lambda: signal(2 * (z - 1) + x))
    pl.when(z < line - 1)(lambda: signal(2 * (z + 1) + x))
    pl.semaphore_wait(
        barrier, 1 + (z > 0).astype(jnp.int32) + (z < line - 1).astype(jnp.int32)
    )


def pieces_of(arrays, axis):
    pieces = []
    for i, array in enumerate(arrays):
        rows = array.shape[axis]
        count = 1 if rows < 64 else 3 if rows < 256 else 4
        size = rows // count // 16 * 16 if count > 1 else rows
        for k in range(count):
            pieces.append((i, pl.ds(k * size, size if k < count - 1 else rows - k * size)))
    return pieces


def gather_phases(pieces, line, refs):
    packets = pieces[-1][0] + 1
    sources, outs = refs[:packets], refs[packets : 2 * packets]
    own_sem, up_sem, down_sem, line_sem, give_sem, got_sem = refs[2 * packets :]
    _, z, x = line_place()
    held = lambda i, zb: outs[pieces[i][0]].at[2 * zb + x, pieces[i][1]]
    mine = lambda i: sources[pieces[i][0]].at[pieces[i][1]]

    def copy(src, i, zb, send_sem, recv_sem, target):
        return pltpu.make_async_remote_copy(
            src_ref=src,
            dst_ref=held(i, zb),
            send_sem=send_sem.at[i, zb],
            recv_sem=recv_sem.at[i, zb],
            device_id={"dp": target},
            device_id_type=pl.DeviceIdType.MESH,
        )

    up_to = lambda src, i, zb: copy(src, i, zb, up_sem, line_sem, 2 * (z + 1) + x)
    down_to = lambda src, i, zb: copy(src, i, zb, down_sem, line_sem, 2 * (z - 1) + x)
    give = lambda src, i, zb: copy(src, i, zb, give_sem, got_sem, 2 * z + 1 - x)
    own = lambda i: pltpu.make_async_copy(mine(i), held(i, z), own_sem.at[i])

    def take_turn(turn):
        if turn == 0:
            greet(line, z, x)
        for i in range(len(pieces)):
            far = turn - i
            if far == 0:
                pl.when(z < line - 1)(lambda: up_to(mine(i), i, z).start())
                pl.when(z > 0)(lambda: down_to(mine(i), i, z).start())
                give(mine(i), i, z).start()
                own(i).start()
            elif 0 < far < line:

                @pl.when(z - far >= 0)
                def _():
                    zb = z - far
                    up_to(held(i, zb), i, zb).wait_recv()
                    pl.when(z < line - 1)(lambda: up_to(held(i, zb), i, zb).start())
                    give(held(i, zb), i, zb).start()

                @pl.when(z + far < line)
                def _():
                    zb = z + far
                    down_to(held(i, zb), i, zb).wait_recv()
                    pl.when(z > 0)(lambda: down_to(held(i, zb), i, zb).start())
                    give(held(i, zb), i, zb).start()

    def finish():
        for i in range(len(pieces)):
            own(i).wait()
            for zb in range(line):
                give(held(i, zb), i, zb).wait()
                pl.when((zb <= z) & (z < line - 1))(lambda: up_to(held(i, zb), i, zb).wait_send())
                pl.when((zb >= z) & (z > 0))(lambda: down_to(held(i, zb), i, zb).wait_send())

    turns = len(pieces) + line - 1
    return [lambda turn=turn: take_turn(turn) for turn in range(turns)] + [finish]


def gather_kernel(pieces, line, *refs):
    for phase in gather_phases(pieces, line, refs):
        phase()


def gather_scratch(pieces, line):
    count = len(pieces)
    sems = lambda *shape: pltpu.SemaphoreType.DMA(shape)
    return [sems(count)] + [sems(count, line) for _ in range(5)]


def gather_shapes(packets):
    return [jax.ShapeDtypeStruct((lax.axis_size("dp"),) + p.shape, p.dtype) for p in packets]


def gather_dp(packets, collective_id):
    total = lax.axis_size("dp")
    if total != 8:
        return [lax.all_gather(packet, "dp", axis=0) for packet in packets]
    pieces, line = pieces_of(packets, 0), total // 2
    return pl.pallas_call(
        lambda *refs: gather_kernel(pieces, line, *refs),
        out_shape=gather_shapes(packets),
        in_specs=[pl.BlockSpec(memory_space=pltpu.VMEM)] * len(packets),
        out_specs=[pl.BlockSpec(memory_space=pl.ANY)] * len(packets),
        scratch_shapes=gather_scratch(pieces, line),
        compiler_params=pltpu.CompilerParams(
            collective_id=collective_id, has_side_effects=True, vmem_limit_bytes=32 << 20
        ),
        cost_estimate=pl.CostEstimate(
            flops=0,
            bytes_accessed=2 * total * sum(p.size * p.dtype.itemsize for p in packets),
            transcendentals=0,
        ),
    )(*packets)


def add_columns(total, parts):
    width = total.shape[-1]
    step = 128 if width % 256 else 256

    def columns(c):
        at = pl.ds(pl.multiple_of(c * step, step), step)
        total[:, at] = sum(part[:, at].astype(FULL) for part in parts).astype(total.dtype)

    pl.loop(0, width // step)(columns)
    if width % step:
        at = slice(width // step * step, width)
        total[:, at] = sum(part[:, at].astype(FULL) for part in parts).astype(total.dtype)


def scatter_phases(pieces, line, refs):
    count = pieces[-1][0] + 1
    parts, outs = refs[:count], refs[count : 2 * count]
    own_refs, near_refs, line_refs = (
        refs[2 * count : 3 * count],
        refs[3 * count : 4 * count],
        refs[4 * count : 5 * count],
    )
    load_sem, give_sem, got_sem, send_sem, line_sem = refs[5 * count :]
    _, z, x = line_place()
    order = [t for pair in zip(range(line - 1, -1, -1), range(line)) for t in pair][:line]
    at = lambda arrays, i, t: arrays[pieces[i][0]].at[t, pieces[i][1]]
    remote = lambda src, dst, send, recv, target: pltpu.make_async_remote_copy(
        src_ref=src,
        dst_ref=dst,
        send_sem=send,
        recv_sem=recv,
        device_id={"dp": target},
        device_id_type=pl.DeviceIdType.MESH,
    )
    give = lambda i, t: remote(
        at(parts, i, 2 * t + 1 - x),
        at(near_refs, i, t),
        give_sem.at[i, t],
        got_sem.at[i, t],
        2 * z + 1 - x,
    )
    load = lambda i, t: pltpu.make_async_copy(
        at(parts, i, 2 * t + x), at(own_refs, i, t), load_sem.at[i, t]
    )
    along = lambda i, t, slot, target: remote(
        at(own_refs, i, t), at(line_refs, i, slot), send_sem.at[i, t], line_sem.at[i, slot], target
    )
    def views(i):
        return [lambda t, arrays=arrays: at(arrays, i, t) for arrays in (own_refs, near_refs, line_refs)]

    def start():
        greet(line, z, x)
        for i in range(len(pieces)):
            for t in order:
                load(i, t).start()
                give(i, t).start()

    def pass_on(i, t, zz):
        own, near, held = views(i)
        load(i, t).wait()
        give(i, t).wait_recv()
        terms = [own(t), near(t)]
        if 0 < zz < t or t < zz < line - 1:
            along(i, t, t, 0).wait_recv()
            terms.append(held(t))
        add_columns(own(t), terms)
        step = 1 if t > zz else -1
        along(i, t, line if t == zz - 1 else t, 2 * (zz + step) + x).start()

    def take_round(r):
        for zz in range(line):

            @pl.when(z == zz)
            def _():
                up, down = r - zz, r - (line - 1 - zz)
                for t in range(line - 1, zz, -1):
                    if 0 <= up < len(pieces):
                        pass_on(up, t, zz)
                for t in range(zz):
                    if 0 <= down < len(pieces):
                        pass_on(down, t, zz)

    def finish():
        for i in range(len(pieces)):
            own, near, held = views(i)
            for t in range(line):

                @pl.when(t == z)
                def _():
                    load(i, t).wait()
                    give(i, t).wait_recv()
                    terms = [own(t), near(t)]
                    if t > 0:
                        along(i, t, t, 0).wait_recv()
                        terms.append(held(t))
                    if t < line - 1:
                        along(i, t, line, 0).wait_recv()
                        terms.append(held(line))
                    add_columns(outs[pieces[i][0]].at[pieces[i][1]], terms)

                pl.when(t != z)(lambda: along(i, t, t, 0).wait_send())
                give(i, t).wait_send()

    rounds = len(pieces) + line - 2
    return [start] + [lambda r=r: take_round(r) for r in range(rounds)] + [finish]


def scatter_kernel(pieces, line, *refs):
    for phase in scatter_phases(pieces, line, refs):
        phase()


def scatter_scratch(parts, pieces, line):
    count = len(pieces)
    sems = lambda *shape: pltpu.SemaphoreType.DMA(shape)
    buffers = [pltpu.VMEM((n,) + p.shape[1:], p.dtype) for n in (line, line, line + 1) for p in parts]
    return buffers + [sems(count, line) for _ in range(4)] + [sems(count, line + 1)]


def scatter_dp(parts, collective_id):
    total = lax.axis_size("dp")
    if total != 8:
        sums = [lax.psum_scatter(p, "dp", scatter_dimension=0) for p in parts]
        return [lax.optimization_barrier(p).astype(FULL) for p in sums]
    pieces, line = pieces_of(parts, 1), total // 2
    return pl.pallas_call(
        lambda *refs: scatter_kernel(pieces, line, *refs),
        out_shape=[jax.ShapeDtypeStruct(p.shape[1:], FULL) for p in parts],
        in_specs=[pl.BlockSpec(memory_space=pl.ANY)] * len(parts),
        out_specs=[pl.BlockSpec(memory_space=pltpu.VMEM)] * len(parts),
        scratch_shapes=scatter_scratch(parts, pieces, line),
        compiler_params=pltpu.CompilerParams(
            collective_id=collective_id, has_side_effects=True, vmem_limit_bytes=56 << 20
        ),
        cost_estimate=pl.CostEstimate(
            flops=6 * 10**10, bytes_accessed=sum(p.size * 2 for p in parts), transcendentals=0
        ),
    )(*parts)


def gather_dp_apart(packet):
    return lax.all_gather(packet, "dp", axis=0, tiled=True)


def scatter_dp_apart(parts):
    summed = lax.psum_scatter(parts.astype(LOW), "dp", scatter_dimension=0, tiled=True)
    return lax.optimization_barrier(summed).astype(FULL)


def trade_halves(first, last):
    me = lax.axis_index("seq")
    one = lax.ppermute(jnp.where(me == 0, last, first), "seq", [(0, 1), (1, 2), (2, 0)])
    two = lax.ppermute(jnp.where(me == 3, first, last), "seq", [(1, 3), (2, 1), (3, 2)])
    return pick([first, one, one, two], me), pick([one, two, two, last], me)


def trade_back(x_part, z_part):
    me = lax.axis_index("seq")
    one = lax.ppermute(jnp.where(me == 0, z_part, x_part), "seq", [(1, 0), (2, 1), (0, 2)])
    two = lax.ppermute(jnp.where(me == 3, x_part, z_part), "seq", [(3, 1), (1, 2), (2, 3)])
    return pick([x_part, one, one, two], me), pick([one, two, two, z_part], me)


def mm(left, right):
    return jnp.dot(left, right, preferred_element_type=FULL)


def mm_nt(left, right):
    return lax.dot_general(left, right, (((1,), (1,)), ((), ())), preferred_element_type=FULL)


def mm_tn(left, right):
    return lax.dot_general(left, right, (((0,), (0,)), ((), ())), preferred_element_type=FULL)


def rms_norm(values, gain):
    return values * lax.rsqrt(jnp.mean(values * values, axis=-1, keepdims=True) + NORM_EPS) * gain


def norm_rows_kernel(values_ref, gain_ref, out_ref):
    out_ref[...] = rms_norm(values_ref[...].astype(FULL), gain_ref[0:1]).astype(LOW)


def norm_rows(values, gain):
    rows, width = values.shape
    block = rows // SEQ
    by_block = pl.BlockSpec((block, width), lambda i: (i, 0))
    return pl.pallas_call(
        norm_rows_kernel,
        grid=(SEQ,),
        in_specs=[by_block, pl.BlockSpec((8, width), lambda i: (0, 0))],
        out_specs=by_block,
        out_shape=jax.ShapeDtypeStruct(values.shape, LOW),
        cost_estimate=pl.CostEstimate(flops=4 * values.size, bytes_accessed=4 * values.size, transcendentals=rows),
    )(values, jnp.broadcast_to(gain, (8, width)))


def join_tail(inputs_x, attn_o, ssm_o, gains):
    residual = inputs_x + 0.5 * (rms_norm(attn_o, gains[1]) + rms_norm(ssm_o, gains[2]))
    return (residual, rms_norm(residual, gains[3]))


STEP_AT = 2 * STATE
WIDE = 896
PAIRS = WIDE // 128
XZB = 1792


def dot_any(left, right, contract):
    return lax.dot_general(
        left, right, ((contract[:1], contract[1:]), ((), ())), preferred_element_type=FULL
    )


def low_dot(left, right, contract):
    return dot_any(left.astype(LOW), right.astype(LOW), contract)


def iota(shape, axis):
    return lax.broadcasted_iota(jnp.int32, shape, axis)


def pair_spread(values):
    rows = values.shape[0]
    low_half = iota((rows, 128), 1) < SSM_HEAD
    tiles = []
    for p in range(PAIRS):
        one = values[:, STEP_AT + 2 * p : STEP_AT + 2 * p + 1]
        two = values[:, STEP_AT + 2 * p + 1 : STEP_AT + 2 * p + 2]
        tiles.append(
            jnp.where(
                low_half,
                jnp.broadcast_to(one, (rows, 128)),
                jnp.broadcast_to(two, (rows, 128)),
            )
        )
    return jnp.concatenate(tiles, axis=1)


def halves(tile):
    low_half = iota(tile.shape, 1) < SSM_HEAD
    zero = jnp.zeros_like(tile)
    return jnp.concatenate([jnp.where(low_half, tile, zero), jnp.where(low_half, zero, tile)], axis=0)


def mamba_chunk(c, lengths_ref, xzb_ref, tail_ref, conv_ref, rate_ref, pad_ref):
    first_end = lengths_ref[0, 0]
    second_end = first_end + lengths_ref[0, 1]
    doc_of = lambda pos: (pos >= first_end).astype(jnp.int32) + (pos >= second_end).astype(jnp.int32)
    base = c * CHUNK
    square = (CHUNK, CHUNK)
    row, lane = iota(square, 0), iota(square, 1)
    doc_row = doc_of(base + row)
    doc_lane = doc_of(base + lane)
    before = jnp.where(c > 0, doc_of(base - 1), -1)
    end = doc_of(base + CHUNK - 1)
    causal = (row >= lane) & (doc_row == doc_lane)
    channel = iota((CHUNK, WIDE), 1) < LOCAL_CH

    raw = jnp.where(channel, xzb_ref[:, :WIDE], 0.0).astype(LOW).astype(FULL)
    gate = pltpu.roll(xzb_ref[:, LOCAL_CH - 64 :], XZB - LOCAL_CH, 1)[:, :WIDE]
    gate = jnp.where(channel, gate, 0.0)
    pad_ref[0:8] = tail_ref[:, :WIDE].astype(LOW).astype(FULL)
    pad_ref[8 : 8 + CHUNK] = raw
    taps = []
    pos = base + iota((CHUNK, 1), 0)
    conv = jnp.zeros((CHUNK, WIDE), FULL)
    for k in range(CONV):
        back = CONV - 1 - k
        same = (doc_of(pos) == doc_of(pos - back)) & (pos >= back)
        shifted = jnp.where(same, pad_ref[8 - back : 8 - back + CHUNK], 0.0)
        taps.append(shifted)
        conv = conv + conv_ref[k : k + 1] * shifted
    conv_sig = jax.nn.sigmoid(conv)
    act = conv * conv_sig

    bc = xzb_ref[:, 2 * LOCAL_CH :]
    b_in = jnp.where(lane < STATE, bc, 0.0)
    c_at = jnp.where((lane >= STATE) & (lane < 2 * STATE), bc, 0.0)
    c_in = pltpu.roll(c_at, CHUNK - STATE, 1)
    step = jnp.maximum(bc, 0.0) + jnp.log(1.0 + jnp.exp(-jnp.abs(bc)))
    lower = (row >= lane).astype(FULL)
    log = lax.dot_general(
        lower,
        -step * rate_ref[0:1],
        (((1,), (0,)), ((), ())),
        precision=lax.Precision.HIGHEST,
        preferred_element_type=FULL,
    )
    last = log[CHUNK - 1 : CHUNK]
    ends = jnp.where(doc_row == end, jnp.exp(last - log), 0.0)
    reach = jnp.where(doc_row == before, jnp.exp(log), 0.0)
    carry = jnp.where(end == before, jnp.exp(last), 0.0)
    gram = low_dot(c_in, b_in, (1, 1))
    log_t = log.T

    def decays(h):
        gap = log[:, STEP_AT + h : STEP_AT + h + 1] - log_t[STEP_AT + h : STEP_AT + h + 1]
        return jnp.exp(jnp.where(causal, gap, MASKED))

    step_wide = pair_spread(step)
    return dict(
        row=row, lane=lane, pos=pos, doc_of=doc_of, gate=gate, taps=taps, conv=conv, conv_sig=conv_sig,
        act=act, bc=bc, b_in=b_in, c_in=c_in, c_at=c_at, step=step, ends=ends, reach=reach,
        carry=carry, gram=gram, decays=decays, step_wide=step_wide, moved=act * step_wide,
    )


def mamba_forward_kernel(
    lengths_ref, xzb_ref, tail_ref, conv_ref, rate_ref, skip_ref, gated_ref, read_ref, states_ref, pad_ref, state_ref
):
    c = pl.program_id(0)

    @pl.when(c == 0)
    def _():
        state_ref[...] = jnp.zeros_like(state_ref)

    v = mamba_chunk(c, lengths_ref, xzb_ref, tail_ref, conv_ref, rate_ref, pad_ref)
    states_ref[0] = state_ref[STATE : 2 * STATE]
    moved = v["moved"]
    from_state = low_dot(v["c_at"], state_ref[...], (1, 0)) * pair_spread(v["reach"])
    tiles = []
    for p in range(PAIRS):
        mixing = jnp.concatenate(
            [(v["decays"](2 * p + j) * v["gram"]).astype(LOW) for j in range(2)], axis=1
        )
        tiles.append(dot_any(mixing, halves(moved[:, 128 * p : 128 * p + 128].astype(LOW)), (1, 0)))
    read = jnp.concatenate(tiles, axis=1) + from_state + skip_ref[0:1] * v["act"]
    read_ref[...] = read.astype(LOW)
    gated_ref[...] = (read * v["gate"] * jax.nn.sigmoid(v["gate"])).astype(LOW)
    added = low_dot(v["b_in"], moved * pair_spread(v["ends"]), (0, 0))[:STATE]
    state_ref[STATE : 2 * STATE] = pair_spread(v["carry"]) * state_ref[STATE : 2 * STATE] + added


def mamba_backward_kernel(
    lengths_ref, xzb_ref, tail_ref, conv_ref, rate_ref, skip_ref, states_ref, read_ref, d_gated_ref,
    d_xzb_ref, d_chan_ref, d_rate_ref, pad_ref, state_ref, d_state_ref, d_pad_ref,
):
    g = pl.program_id(0)
    c = pl.num_programs(0) - 1 - g

    @pl.when(g == 0)
    def _():
        state_ref[...] = jnp.zeros_like(state_ref)
        d_state_ref[...] = jnp.zeros_like(d_state_ref)
        d_pad_ref[...] = jnp.zeros_like(d_pad_ref)
        d_chan_ref[...] = jnp.zeros_like(d_chan_ref)
        d_rate_ref[...] = jnp.zeros_like(d_rate_ref)

    v = mamba_chunk(c, lengths_ref, xzb_ref, tail_ref, conv_ref, rate_ref, pad_ref)
    row, lane, act, moved, gate = v["row"], v["lane"], v["act"], v["moved"], v["gate"]
    state_ref[STATE : 2 * STATE] = states_ref[0]
    by_head = (iota((WIDE, 128), 0) // SSM_HEAD + STEP_AT == iota((WIDE, 128), 1)).astype(LOW)
    head_sum = lambda wide: dot_any(wide.astype(LOW), by_head, (1, 0))

    d_gated = d_gated_ref[...].astype(FULL)
    gate_sig = jax.nn.sigmoid(gate)
    d_read = d_gated * gate * gate_sig
    d_gate = d_gated * read_ref[...].astype(FULL) * gate_sig * (1.0 + gate * (1.0 - gate_sig))
    d_chan_ref[CONV : CONV + 1] += jnp.sum(d_read * act, axis=0, keepdims=True)
    d_act = skip_ref[0:1] * d_read

    d_log = jnp.zeros_like(v["gram"])
    d_log_t = jnp.zeros_like(v["gram"])
    d_gram = jnp.zeros_like(v["gram"])
    tiles = []
    for p in range(PAIRS):
        at = slice(128 * p, 128 * p + 128)
        d_pair = halves(d_read[:, at].astype(LOW))
        d_mixing = dot_any(d_pair, moved[:, at].astype(LOW), (1, 1))
        mixings = []
        for j in range(2):
            h = 2 * p + j
            decay = v["decays"](h)
            mixing = decay * v["gram"]
            d_one = d_mixing[CHUNK * j : CHUNK * (j + 1)]
            d_gram = d_gram + d_one * decay
            d_gap = d_one * mixing
            mixings.append(mixing.astype(LOW))
            d_log = d_log + jnp.where(lane == STEP_AT + h, jnp.sum(d_gap, axis=1, keepdims=True), 0.0)
            d_log_t = d_log_t + jnp.where(row == STEP_AT + h, jnp.sum(d_gap, axis=0, keepdims=True), 0.0)
        tiles.append(dot_any(jnp.concatenate(mixings, axis=0), d_pair, (0, 0)))
    d_moved = jnp.concatenate(tiles, axis=1)
    d_log = d_log - d_log_t.T

    d_product = d_read * pair_spread(v["reach"])
    state_low = state_ref[...].astype(LOW)
    product = dot_any(v["c_at"].astype(LOW), state_low, (1, 0))
    d_log = d_log + head_sum(d_product * product)
    d_c = low_dot(d_product, state_low, (1, 1)) + low_dot(d_gram, pltpu.roll(v["b_in"], STATE, 1), (1, 0))
    d_state_in = low_dot(v["c_at"], d_product, (0, 0))[STATE : 2 * STATE]

    d_state = d_state_ref[...]
    d_state_low = d_state.astype(LOW)
    ends_wide = pair_spread(v["ends"])
    d_put = dot_any(v["b_in"].astype(LOW), d_state_low, (1, 0)) * ends_wide
    d_b = low_dot(moved * ends_wide, d_state_low, (1, 1)) + low_dot(d_gram, v["c_in"], (0, 0))
    d_moved = d_moved + d_put
    d_ends = head_sum(d_put * moved)
    carry_wide = pair_spread(v["carry"])
    d_carry = head_sum(
        jnp.broadcast_to(
            jnp.sum(d_state[:STATE] * states_ref[0], axis=0, keepdims=True) * carry_wide, (16, WIDE)
        )
    )[0:1]
    d_last = jnp.sum(d_ends, axis=0, keepdims=True) + d_carry
    d_log = d_log - d_ends + jnp.where(row == CHUNK - 1, d_last, 0.0)
    d_state_ref[:STATE] = d_state_in + carry_wide * d_state[:STATE]

    d_act = d_act + d_moved * v["step_wide"]
    d_rate_step = lax.dot_general(
        (row >= lane).astype(FULL),
        d_log,
        (((0,), (0,)), ((), ())),
        precision=lax.Precision.HIGHEST,
        preferred_element_type=FULL,
    )
    d_step = head_sum(d_moved * act) - rate_ref[0:1] * d_rate_step
    d_rate_ref[0:1] += jnp.sum(-v["step"] * d_rate_step, axis=0, keepdims=True)
    is_step = (lane >= STEP_AT) & (lane < STEP_AT + LOCAL_HEADS)
    d_bc = d_b + d_c + jnp.where(is_step, d_step * jax.nn.sigmoid(v["bc"]), 0.0)

    d_conv = d_act * v["conv_sig"] * (1.0 + v["conv"] * (1.0 - v["conv_sig"]))
    d_pad_ref[0:CHUNK] = d_conv
    d_raw = jnp.zeros_like(d_conv)
    for k in range(CONV):
        ahead = CONV - 1 - k
        d_chan_ref[k : k + 1] += jnp.sum(d_conv * v["taps"][k], axis=0, keepdims=True)
        same = v["doc_of"](v["pos"]) == v["doc_of"](v["pos"] + ahead)
        d_raw = d_raw + conv_ref[k : k + 1] * jnp.where(same, d_pad_ref[ahead : ahead + CHUNK], 0.0)
    d_pad_ref[CHUNK : CHUNK + 8] = d_conv[0:8]

    moved_gate = pltpu.roll(jnp.concatenate([d_gate, jnp.zeros_like(row).astype(FULL)], axis=1), 64, 1)
    d_xzb_ref[:, : LOCAL_CH - 64] = d_raw[:, : LOCAL_CH - 64].astype(LOW)
    d_xzb_ref[:, LOCAL_CH - 64 : LOCAL_CH + 64] = (
        d_raw[:, LOCAL_CH - 64 :] + moved_gate[:, :128]
    ).astype(LOW)
    d_xzb_ref[:, LOCAL_CH + 64 : 2 * LOCAL_CH] = moved_gate[:, 128:WIDE].astype(LOW)
    d_xzb_ref[:, 2 * LOCAL_CH :] = d_bc.astype(LOW)


def mamba_specs(chunk_of):
    tail = lambda g: (jnp.maximum(chunk_of(g) * (CHUNK // 8) - 1, 0), 0)
    fixed = lambda shape: pl.BlockSpec(shape, lambda g: (0,) * len(shape))
    return [
        pl.BlockSpec(memory_space=pltpu.SMEM),
        pl.BlockSpec((CHUNK, XZB), lambda g: (chunk_of(g), 0)),
        pl.BlockSpec((8, XZB), tail),
        fixed((8, WIDE)),
        fixed((8, 128)),
        fixed((8, WIDE)),
    ]


def mamba_forward(lengths, xzb, conv_rows, rate_row, skip_row):
    total = xzb.shape[0]
    chunks = total // CHUNK
    by_chunk = lambda width: pl.BlockSpec((CHUNK, width), lambda g: (g, 0))
    return pl.pallas_call(
        mamba_forward_kernel,
        grid=(chunks,),
        in_specs=mamba_specs(lambda g: g),
        out_specs=[by_chunk(WIDE), by_chunk(WIDE), pl.BlockSpec((1, STATE, WIDE), lambda g: (g, 0, 0))],
        out_shape=[
            jax.ShapeDtypeStruct((total, WIDE), LOW),
            jax.ShapeDtypeStruct((total, WIDE), LOW),
            jax.ShapeDtypeStruct((chunks, STATE, WIDE), FULL),
        ],
        scratch_shapes=[pltpu.VMEM((8 + CHUNK, WIDE), FULL), pltpu.VMEM((CHUNK, WIDE), FULL)],
        compiler_params=pltpu.CompilerParams(vmem_limit_bytes=32 << 20),
        cost_estimate=pl.CostEstimate(flops=2 * 10**10, bytes_accessed=16 << 20, transcendentals=10**7),
    )(lengths, xzb, xzb, conv_rows, rate_row, skip_row)


def mamba_backward(lengths, xzb, conv_rows, rate_row, skip_row, states, read, d_gated):
    total = xzb.shape[0]
    chunks = total // CHUNK
    chunk_of = lambda g: chunks - 1 - g
    by_chunk = lambda width: pl.BlockSpec((CHUNK, width), lambda g: (chunk_of(g), 0))
    return pl.pallas_call(
        mamba_backward_kernel,
        grid=(chunks,),
        in_specs=mamba_specs(chunk_of)
        + [pl.BlockSpec((1, STATE, WIDE), lambda g: (chunk_of(g), 0, 0)), by_chunk(WIDE), by_chunk(WIDE)],
        out_specs=[
            by_chunk(XZB),
            pl.BlockSpec((8, WIDE), lambda g: (0, 0)),
            pl.BlockSpec((8, 128), lambda g: (0, 0)),
        ],
        out_shape=[
            jax.ShapeDtypeStruct((total, XZB), LOW),
            jax.ShapeDtypeStruct((8, WIDE), FULL),
            jax.ShapeDtypeStruct((8, 128), FULL),
        ],
        scratch_shapes=[
            pltpu.VMEM((8 + CHUNK, WIDE), FULL),
            pltpu.VMEM((CHUNK, WIDE), FULL),
            pltpu.VMEM((CHUNK, WIDE), FULL),
            pltpu.VMEM((8 + CHUNK, WIDE), FULL),
        ],
        compiler_params=pltpu.CompilerParams(vmem_limit_bytes=32 << 20),
        cost_estimate=pl.CostEstimate(flops=6 * 10**10, bytes_accessed=24 << 20, transcendentals=10**7),
    )(lengths, xzb, xzb, conv_rows, rate_row, skip_row, states, read, d_gated)


def head_under(h, at, value):
    row, lane = iota((QW, 128), 0), iota((QW, 128), 1)
    inside = (lane >= at) & (lane < at + HEAD) & (row == h * HEAD + lane - at)
    return jnp.where(inside, value, 0.0).astype(LOW)


def row_block(t):
    return jnp.where(t < SEQ, t, lax.axis_index("seq"))


def allowed_keys(lengths_ref, block, rows, extent):
    first_end = lengths_ref[0, 0]
    second_end = first_end + lengths_ref[0, 1]
    row = block * rows + iota((rows, 1), 0)
    start = jnp.where(row >= second_end, second_end, jnp.where(row >= first_end, first_end, 0))
    least = jnp.maximum(start, row - (WINDOW - 1))
    key = iota((rows, extent), 1)
    return (key >= least) & (key <= row)


def for_extent(block, rows, run):
    for e in range(SEQ):
        pl.when(block == e)(lambda e=e: run((e + 1) * rows))


def attention_forward_kernel(lengths_ref, q_ref, kv_ref, out_ref, log_ref):
    t, h = pl.program_id(0), pl.program_id(1)
    rows = q_ref.shape[0]
    block = row_block(t)

    def run(extent):
        q = dot_any(q_ref[...], head_under(h, 0, HEAD ** (-0.5)), (1, 0)).astype(LOW)
        kv = kv_ref[:extent]
        scores = dot_any(q, kv, (1, 1))
        scores = jnp.where(allowed_keys(lengths_ref, block, rows, extent), scores, MASKED)
        top = jnp.max(scores, axis=1, keepdims=True)
        expos = jnp.exp(scores - top)
        denom = jnp.sum(expos, axis=1, keepdims=True)
        mixed = dot_any((expos * (1.0 / denom)).astype(LOW), kv, (1, 0)).astype(LOW)
        out = dot_any(mixed, head_under(h, HEAD, 1.0), (1, 1)).astype(LOW)
        log = jnp.where(iota((rows, 128), 1) == h, top + jnp.log(denom), 0.0)

        @pl.when(h == 0)
        def _():
            out_ref[...] = out
            log_ref[...] = log

        @pl.when(h > 0)
        def _():
            out_ref[...] += out
            log_ref[...] += log

    for_extent(block, rows, run)


def attention_backward_kernel(
    lengths_ref, q_ref, kv_ref, out_ref, log_ref, d_out_ref, d_q_ref, d_kv_ref, sum_ref
):
    t, h = pl.program_id(0), pl.program_id(1)
    rows = q_ref.shape[0]
    block = row_block(t)

    @pl.when((h == 0) & ((t == 0) | (t == SEQ)))
    def _():
        sum_ref[...] = jnp.zeros_like(sum_ref)

    def run(extent):
        under_q = head_under(h, 0, HEAD ** (-0.5))
        q = dot_any(q_ref[...], under_q, (1, 0)).astype(LOW)
        d_out = dot_any(d_out_ref[...], head_under(h, HEAD, 1.0), (1, 0)).astype(LOW)
        log = jnp.sum(jnp.where(iota((rows, 128), 1) == h, log_ref[...], 0.0), axis=1, keepdims=True)
        own = iota((rows, QW), 1) // HEAD == h
        product = d_out_ref[...].astype(FULL) * out_ref[...].astype(FULL)
        d_total = jnp.sum(jnp.where(own, product, 0.0), axis=1, keepdims=True)
        kv = kv_ref[:extent]
        scores = dot_any(q, kv, (1, 1))
        allowed = allowed_keys(lengths_ref, block, rows, extent)
        probs = jnp.exp(jnp.where(allowed, scores - log, MASKED))
        d_probs = dot_any(d_out, kv, (1, 1))
        d_scores = (probs * (d_probs - d_total)).astype(LOW)
        sum_ref[:extent] += dot_any(probs.astype(LOW), d_out, (0, 0)) + dot_any(d_scores, q, (0, 0))
        d_q = dot_any(dot_any(d_scores, kv, (1, 0)).astype(LOW), under_q, (1, 1)).astype(LOW)

        @pl.when(h == 0)
        def _():
            d_q_ref[...] = d_q

        @pl.when(h > 0)
        def _():
            d_q_ref[...] += d_q

    for_extent(block, rows, run)

    @pl.when((h == GROUP_HEADS - 1) & (t >= SEQ - 1))
    def _():
        d_kv_ref[...] = sum_ref[...].astype(LOW)


def attention_specs(rows, group):
    by_step = lambda width: pl.BlockSpec((rows, width), lambda t, h: (t, 0))
    kv_block = pl.BlockSpec((group, 128), lambda t, h: (0, t // SEQ))
    return by_step, kv_block


def attention_forward(lengths, queries, kv, rows):
    by_step, kv_block = attention_specs(rows, kv.shape[0])
    return pl.pallas_call(
        attention_forward_kernel,
        grid=(SEQ + 1, GROUP_HEADS),
        in_specs=[pl.BlockSpec(memory_space=pltpu.SMEM), by_step(QW), kv_block],
        out_specs=[by_step(QW), by_step(128)],
        out_shape=[
            jax.ShapeDtypeStruct(queries.shape, LOW),
            jax.ShapeDtypeStruct((queries.shape[0], 128), FULL),
        ],
        compiler_params=pltpu.CompilerParams(vmem_limit_bytes=32 << 20),
        cost_estimate=pl.CostEstimate(flops=4 * 10**10, bytes_accessed=4 << 20, transcendentals=8 * 10**6),
    )(lengths, queries, kv)


def attention_backward(lengths, queries, kv, out, logs, d_out, rows, parts, collective_id):
    group = kv.shape[0]
    by_step, kv_block = attention_specs(rows, group)
    total = lax.axis_size("dp")
    beside = parts if total == 8 else []
    count, line = len(beside), total // 2
    pieces = pieces_of(beside, 1)

    def kernel(*refs):
        own_in, parts_in = refs[:6], refs[6 : 6 + count]
        own_out, sums_out = refs[6 + count : 8 + count], refs[8 + count : 8 + 2 * count]
        sum_ref, transfer = refs[8 + 2 * count], refs[9 + 2 * count :]
        step = pl.program_id(0) * GROUP_HEADS + pl.program_id(1)
        steps = (SEQ + 1) * GROUP_HEADS
        phases = scatter_phases(pieces, line, parts_in + sums_out + transfer) if count else []
        spots = [min(13 * k, steps - 1) for k in range(len(phases))]
        for phase, spot in zip(phases, spots):
            if spot < steps - 1:
                pl.when(step == spot)(phase)
        attention_backward_kernel(*own_in, *own_out, sum_ref)
        for phase, spot in zip(phases, spots):
            if spot == steps - 1:
                pl.when(step == spot)(phase)

    found = pl.pallas_call(
        kernel,
        grid=(SEQ + 1, GROUP_HEADS),
        in_specs=[pl.BlockSpec(memory_space=pltpu.SMEM), by_step(QW), kv_block]
        + [by_step(QW), by_step(128), by_step(QW)]
        + [pl.BlockSpec(memory_space=pl.ANY)] * count,
        out_specs=[by_step(QW), kv_block] + [pl.BlockSpec(memory_space=pltpu.VMEM)] * count,
        out_shape=[jax.ShapeDtypeStruct(queries.shape, LOW), jax.ShapeDtypeStruct(kv.shape, LOW)]
        + [jax.ShapeDtypeStruct(p.shape[1:], FULL) for p in beside],
        scratch_shapes=[pltpu.VMEM((group, 128), FULL)]
        + (scatter_scratch(beside, pieces, line) if count else []),
        compiler_params=pltpu.CompilerParams(
            vmem_limit_bytes=56 << 20,
            **(dict(collective_id=collective_id, has_side_effects=True) if count else {}),
        ),
        cost_estimate=pl.CostEstimate(flops=10**11, bytes_accessed=8 << 20, transcendentals=8 * 10**6),
    )(lengths, queries, kv, out, logs, d_out, *beside)
    return found[0], found[1], list(found[2:]) if count else scatter_dp(parts, collective_id)


def pick(options, seq_index):
    return lax.select_n(seq_index, *options)


def own_cut(values, seq_index, axis, unit):
    cuts = []
    for first, count in zip(FIRST_HEAD, HEAD_COUNT):
        cut = lax.slice_in_dim(values, first * unit, (first + count) * unit, axis=axis)
        pads = [(0, 0)] * values.ndim
        pads[axis] = (0, (LOCAL_HEADS - count) * unit)
        cuts.append(jnp.pad(cut, pads))
    return pick(cuts, seq_index)


def own_spread(values, seq_index, unit):
    spreads = []
    for first, count in zip(FIRST_HEAD, HEAD_COUNT):
        pads = [(0, 0)] * (values.ndim - 1) + [(first * unit, (SSM_HEADS - first - count) * unit)]
        spreads.append(jnp.pad(values[..., : count * unit], pads))
    return pick(spreads, seq_index)


def channel_cut(wide, seq_index, axis):
    return own_cut(wide, seq_index, axis, SSM_HEAD)


def bcdt_cut(w_bcdt, seq_index):
    first = pick([jnp.int32(h) for h in FIRST_HEAD], seq_index)
    count = pick([jnp.int32(c) for c in HEAD_COUNT], seq_index)
    source = jnp.arange(w_bcdt.shape[1], dtype=jnp.int32)[:, None]
    target = jnp.arange(BCDT_PAD, dtype=jnp.int32)[None]
    shared = (target < 2 * STATE) & (source == target)
    steps = (target >= 2 * STATE) & (target < 2 * STATE + count) & (source == target + first)
    return mm(w_bcdt, (shared | steps).astype(LOW)).astype(LOW)


def rows_by_peer_kernel(mamba_ref, o_ref, *refs):
    outs, held, load_sem, store_sem = refs[:SEQ], *refs[SEQ:]
    me = lax.axis_index("seq")
    shared = (KV_HEADS - 1) * QW

    def loads(p):
        own = HEAD_COUNT[p] * SSM_HEAD
        parts = [
            (mamba_ref, FIRST_HEAD[p] * SSM_HEAD, OUT_AT, own),
            (o_ref, p * QW, O_AT, QW),
            (o_ref, shared, O5_AT, QW),
        ]
        return [
            pltpu.make_async_copy(
                source.at[pl.ds(at, count)], held.at[p, pl.ds(to, count)], load_sem.at[p, k]
            )
            for k, (source, at, to, count) in enumerate(parts)
        ]

    for p in range(SEQ):
        for load in loads(p):
            load.start()
        for start, end in ((HEAD_COUNT[p] * SSM_HEAD, O_AT), (O_AT + QW, O5_AT)):
            held[p, start:end] = jnp.zeros((end - start, held.shape[2]), held.dtype)

    def stores(act):
        for p in range(SEQ):
            if act == "start":
                for load in loads(p):
                    load.wait()
            for k in range(SEQ):
                copy = pltpu.make_async_copy(held.at[p], outs[k], store_sem.at[p])
                pl.when(jnp.bitwise_xor(me, p) == k)(copy.start if act == "start" else copy.wait)

    stores("start")
    stores("wait")


def rows_by_peer(mamba_cols, o_cols):
    block = (OUT_WIDTH, o_cols.shape[1])
    anywhere = pl.BlockSpec(memory_space=pl.ANY)
    return pl.pallas_call(
        rows_by_peer_kernel,
        in_specs=[anywhere] * 2,
        out_specs=[anywhere] * SEQ,
        out_shape=[jax.ShapeDtypeStruct(block, LOW)] * SEQ,
        scratch_shapes=[
            pltpu.VMEM((SEQ,) + block, LOW),
            pltpu.SemaphoreType.DMA((SEQ, 3)),
            pltpu.SemaphoreType.DMA((SEQ,)),
        ],
        compiler_params=pltpu.CompilerParams(vmem_limit_bytes=32 << 20),
        cost_estimate=pl.CostEstimate(flops=0, bytes_accessed=12 << 20, transcendentals=0),
    )(mamba_cols, o_cols)


def wide_kernel(*refs):
    pieces, out = refs[:SEQ], refs[SEQ]
    me, width = lax.axis_index("seq"), pieces[0].shape[1]
    for j in range(SEQ):
        for k in range(SEQ):

            @pl.when(jnp.bitwise_xor(me, j) == k)
            def _():
                out[:, width * j : width * (j + 1)] = pieces[k][...]


def wide_of(arrivals):
    rows, width = arrivals[0].shape
    block = rows if rows < 400 else 400
    return pl.pallas_call(
        wide_kernel,
        grid=(rows // block,),
        in_specs=[pl.BlockSpec((block, width), lambda i: (i, 0))] * SEQ,
        out_specs=pl.BlockSpec((block, SEQ * width), lambda i: (i, 0)),
        out_shape=jax.ShapeDtypeStruct((rows, SEQ * width), arrivals[0].dtype),
        cost_estimate=pl.CostEstimate(flops=0, bytes_accessed=16 * rows * width, transcendentals=0),
    )(*arrivals)


def on_device(
    tokens_in,
    doc_lengths,
    norm_gains,
    w_qkv,
    w_o,
    w_xz,
    w_bcdt,
    conv_w,
    ssm_rate,
    ssm_skip,
    w_out,
    w_gate_up,
    w_down,
    cotangent,
):
    rows = tokens_in.shape[0]
    group = rows * SEQ
    s = lax.axis_index("seq")
    dp_index = lax.axis_index("dp")
    dp_total = lax.axis_size("dp")
    block_rows = w_qkv.shape[0]
    kv_width = KV_HEADS * HEAD
    lengths = doc_lengths[0]
    live = (jnp.arange(rows, dtype=jnp.int32) + s * rows < lengths[0] + lengths[1]).astype(FULL)[:, None]

    gains_block = norm_gains.shape[1]
    conv_block = conv_w.shape[1]
    width = -(-max(conv_block, gains_block) // 128) * 128
    small = jnp.concatenate(
        [
            jnp.pad(conv_w, ((0, 4), (0, width - conv_block))),
            jnp.pad(norm_gains, ((0, 4), (0, width - gains_block))),
        ]
    )
    out_block = w_out.shape[0]
    qkv_far, qkv_near = swap(w_qkv, "seq", 2), swap(w_qkv, "seq", 1)
    x_part, z_part = trade_halves(
        w_xz[:, :LOCAL_CH], jnp.pad(w_xz[:, LOCAL_CH:], ((0, 0), (0, 2 * LOCAL_CH - w_xz.shape[1])))
    )
    tokens_far, tokens_near = swap(tokens_in, "seq", 2), swap(tokens_in, "seq", 1)
    small, o_cols, mamba_cols = gather_dp([small, w_o, w_out], 0)
    small, o_cols, mamba_cols, qkv_far, qkv_near, x_part, z_part, tokens_far, tokens_near = lax.optimization_barrier(
        (small, o_cols, mamba_cols, qkv_far, qkv_near, x_part, z_part, tokens_far, tokens_near)
    )
    qkv_shards = [w_qkv, qkv_near, qkv_far, swap(qkv_far, "seq", 1)]
    token_blocks = [tokens_in, tokens_near, tokens_far, swap(tokens_far, "seq", 1)]
    full_conv = small[:, :4, :conv_block].transpose(1, 0, 2).reshape(4, INNER).astype(FULL)
    gains = small[:, 8:12, :gains_block].transpose(1, 0, 2).reshape(4, D).astype(FULL)
    tokens_group = place(list(zip(seq_order(), token_blocks))).reshape(group, D)
    normed = norm_rows(tokens_group, gains[0])
    qkv_wide = wide_of(qkv_shards)
    q_at = lambda h: lax.dynamic_slice_in_dim(qkv_wide, h * QW, QW, 1)
    kv_at = lambda h: [
        lax.dynamic_slice_in_dim(qkv_wide, D + h * HEAD, HEAD, 1),
        lax.dynamic_slice_in_dim(qkv_wide, D + kv_width + h * HEAD, HEAD, 1),
    ]
    qkv_packet = jnp.concatenate(kv_at(s) + kv_at(KV_HEADS - 1) + [q_at(s), q_at(KV_HEADS - 1)], axis=1)
    xz_packet = jnp.concatenate([x_part, z_part, bcdt_cut(w_bcdt, s)], axis=1)
    full_qkv, full_xz = gather_dp([qkv_packet, xz_packet], 1)
    gate_up_packet = jnp.pad(w_gate_up, ((0, 0), (0, 0), (0, UNITS_PAD - UNITS))).reshape(block_rows, -1)
    down_packet = jnp.pad(w_down, ((0, 0), (0, UNITS_PAD - UNITS)))
    d_total = cotangent.astype(FULL) * live
    d_ffn = d_total.astype(LOW)
    d_ffn_far, d_ffn_near = swap(d_ffn, "seq", 2), swap(d_ffn, "seq", 1)
    full_qkv, full_xz, o_cols, mamba_cols, gate_up_packet, down_packet, d_ffn_far, d_ffn_near = (
        lax.optimization_barrier(
            (full_qkv, full_xz, o_cols, mamba_cols, gate_up_packet, down_packet, d_ffn_far, d_ffn_near)
        )
    )
    d_ffn_group = jnp.concatenate([d_ffn, d_ffn_near, d_ffn_far, swap(d_ffn_far, "seq", 1)])
    full_qkv = full_qkv.reshape(D, -1)
    full_xz = full_xz.reshape(D, -1)
    full_gate_up = gather_dp_apart(gate_up_packet)
    full_down = gather_dp_apart(down_packet)


    own = lambda a: lax.dynamic_slice_in_dim(a, s * rows, rows, 0)
    normed_own = own(normed)
    kvq = mm(normed, full_qkv[:, : 256 + QW]).astype(LOW)
    q_last = mm(normed_own, full_qkv[:, 256 + QW :]).astype(LOW)
    queries = jnp.concatenate([kvq[:, 256:], q_last])
    kv = kvq[:, :256]
    out_blocks = list(rows_by_peer(mamba_cols.reshape(INNER, -1), o_cols.reshape(D, -1)))
    out_blocks, queries = meet(out_blocks, queries)
    attended, logs = attention_forward(doc_lengths, queries, kv, rows)
    out_pieces = out_blocks[:1] + [swap(out_blocks[bit], "seq", bit) for bit in (1, 2, 3)]
    out_rows = wide_of(after(out_pieces, attended))
    w_out_rows = out_rows[:WIDE]
    w_o_rows = out_rows[O_AT : O_AT + QW]
    w_o5_rows = out_rows[O5_AT:]
    attn_part = mm(attended[:group], w_o_rows).astype(LOW)
    normed_now, attn_part = lax.optimization_barrier((normed, attn_part))
    attn_keep, attn_got = scatter_begin(attn_part)

    xzb = mm(normed_now, full_xz)
    attn_held, attn_far = scatter_far(attn_keep, after(attn_got, xzb))
    xzb, attn_held = lax.optimization_barrier((xzb, attn_held))
    conv_rows = jnp.pad(channel_cut(full_conv, s, 1), ((0, 4), (0, WIDE - LOCAL_CH)))
    rate_row = jnp.pad(own_cut(ssm_rate, s, 0, 1), (STEP_AT, 128 - STEP_AT - LOCAL_HEADS))
    rate_row = jnp.broadcast_to(rate_row, (8, 128))
    skip_row = jnp.pad(jnp.repeat(own_cut(ssm_skip, s, 0, 1), SSM_HEAD), (0, WIDE - LOCAL_CH))
    skip_row = jnp.broadcast_to(skip_row, (8, WIDE))
    mamba_in = (doc_lengths, xzb, conv_rows, rate_row, skip_row)
    gated, read, states = mamba_forward(*mamba_in)
    gated, attn_far = meet(gated, attn_far)
    ssm_held, ssm_far = scatter_far(*scatter_begin(mm(gated, w_out_rows)))
    attn_o = scatter_end(attn_held, attn_far) + mm(attended[group:], w_o5_rows)
    ssm_o = scatter_end(ssm_held, ssm_far)

    inputs_x = tokens_in.astype(FULL)
    (residual, normed_two), pull_join = jax.vjp(join_tail, inputs_x, attn_o, ssm_o, gains)
    normed_two, d_act = seq_arrivals(normed_two.astype(LOW), mm(d_ffn_group, full_down))
    normed_two = jnp.concatenate(normed_two)
    gate_up = mm(normed_two, full_gate_up)
    ffn_gate, ffn_up = gate_up[:, :UNITS_PAD], gate_up[:, UNITS_PAD:]
    ffn_act = (jax.nn.silu(ffn_gate) * ffn_up).astype(LOW)

    sig = jax.nn.sigmoid(ffn_gate)
    d_gate = d_act * ffn_up * (sig * (1.0 + ffn_gate * (1.0 - sig)))
    d_up = d_act * ffn_gate * sig
    d_gate_up = jnp.concatenate([d_gate.astype(LOW), d_up.astype(LOW)], axis=1)
    two_keep, two_got = relative_begin(mm_nt(d_gate_up, full_gate_up))
    two_got, grad_down_part = meet(two_got, mm_tn(d_ffn_group, ffn_act).astype(LOW))
    two_held, two_far = relative_far(two_keep, two_got)
    two_far, grad_gate_up_part = meet(two_far, mm_tn(normed_two, d_gate_up).astype(LOW))
    d_normed_two = scatter_end(two_held, two_far)
    grad_gate_up_sum = scatter_dp_apart(grad_gate_up_part)
    grad_down_sum = scatter_dp_apart(grad_down_part)
    grad_gate_up = grad_gate_up_sum.reshape(block_rows, 2, UNITS_PAD)[:, :, :UNITS]
    grad_down = grad_down_sum[:, :UNITS]

    d_x_tail, d_attn_o, d_ssm_o, d_gains = pull_join((d_total, d_normed_two))
    ssm_arrivals, ffn_part = seq_arrivals(d_ssm_o.astype(LOW), mm_nt(ffn_act, full_down).astype(LOW))
    d_attn_own = after(d_attn_o.astype(LOW), ssm_arrivals[2])
    attn_near, attn_away = swap(d_attn_own, "seq", 1), swap(d_attn_own, "seq", 2)
    d_ssm = place(list(zip(seq_order(), ssm_arrivals))).reshape(group, D)
    d_gated = mm_nt(d_ssm, w_out_rows).astype(LOW)

    def send_columns(grad):
        width = D // SEQ
        blocks = [grad[:, width * j : width * (j + 1)] for j in range(SEQ)]
        return [with_layout_constraint(pick(blocks, s ^ k), Layout((0, 1))) for k in range(SEQ)]

    def trade(blocks):
        return blocks[:1] + [swap(blocks[bit], "seq", bit) for bit in (1, 2, 3)]

    mamba_blocks, d_gated = meet(send_columns(mm_tn(gated, d_ssm).astype(LOW)), d_gated)
    mamba_pieces = trade(mamba_blocks)
    (mamba_pieces[1], attn_near), d_gated = meet((mamba_pieces[1], attn_near), d_gated)
    d_xzb, d_chan, d_rate = mamba_backward(*mamba_in, states, read, d_gated)
    (mamba_pieces[2:], attn_away), d_xzb = meet((mamba_pieces[2:], attn_away), d_xzb)
    ffn_keep, ffn_got = relative_begin(ffn_part)
    attn_arrivals = [d_attn_own, attn_near, attn_away, swap(attn_away, "seq", 1)]
    arrived = place(list(zip(seq_order(), mamba_pieces)))
    grad_out_part = jnp.concatenate(
        [arrived[j, : HEAD_COUNT[j] * SSM_HEAD] for j in range(SEQ)]
    ).reshape(dp_total, out_block, -1)

    d_attn = place(list(zip(seq_order(), attn_arrivals))).reshape(group, D)
    d_attended = jnp.concatenate([mm_nt(d_attn, w_o_rows), mm_nt(d_attn_own, w_o5_rows)]).astype(LOW)
    head_blocks = send_columns(
        jnp.concatenate([mm_tn(attended[:group], d_attn), mm_tn(attended[group:], d_attn_own)]).astype(LOW)
    )
    head_blocks, d_attended = meet(head_blocks, d_attended)
    head_pieces = trade(head_blocks)
    ffn_got, d_attended = meet(ffn_got, d_attended)
    ffn_held, ffn_far = relative_far(ffn_keep, ffn_got)
    ffn_held, d_attended = meet(ffn_held, d_attended)
    d_conv = d_chan[:CONV, :LOCAL_CH]
    d_skip = jnp.sum(d_chan[CONV, :LOCAL_CH].reshape(LOCAL_HEADS, SSM_HEAD), axis=1)
    d_rate = d_rate[0, STEP_AT : STEP_AT + LOCAL_HEADS]
    grad_xz_part = mm_tn(normed, d_xzb).astype(LOW).reshape(dp_total, block_rows, -1)

    d_queries, d_kv, (grad_xz_sum, grad_out) = attention_backward(
        doc_lengths, queries, kv, attended, logs, d_attended, rows, [grad_xz_part, grad_out_part], 3
    )
    (head_pieces, ffn_far), d_queries = meet((head_pieces, ffn_far), d_queries)
    mixed_out = ((residual + scatter_end(ffn_held, ffn_far)) * live).astype(LOW)
    arrived = place(list(zip(seq_order(), head_pieces)))
    grad_o_part = jnp.concatenate(
        [arrived[j, :QW] for j in range(SEQ)] + [jnp.sum(arrived[:, QW:].astype(FULL), axis=0).astype(LOW)]
    ).reshape(dp_total, block_rows, -1)
    d_kvq = jnp.concatenate([d_kv, d_queries[:group]], axis=1)
    d_q_last = d_queries[group:]
    grad_qkv_part = jnp.concatenate(
        [mm_tn(normed, d_kvq).astype(LOW), mm_tn(normed_own, d_q_last).astype(LOW)], axis=1
    ).reshape(dp_total, block_rows, -1)
    d_normed_part = mm_nt(d_xzb, full_xz) + mm_nt(d_kvq, full_qkv[:, : 256 + QW])
    d_normed_own = mm_nt(d_q_last, full_qkv[:, 256 + QW :])

    tokens_wide = tokens_group.astype(FULL)
    unit = tokens_wide * lax.rsqrt(jnp.mean(tokens_wide * tokens_wide, axis=-1, keepdims=True) + NORM_EPS)
    d_gain_first = jnp.sum(d_normed_part * unit, axis=0) + jnp.sum(d_normed_own * own(unit), axis=0)
    d_gains = d_gains.at[0].add(d_gain_first)
    by_dp = lambda a: a.reshape(a.shape[0], dp_total, -1).transpose(1, 0, 2)
    d_heads = jnp.concatenate([own_spread(d_rate, s, 1), own_spread(d_skip, s, 1)])[None]
    small_part = jnp.concatenate(
        [
            jnp.pad(by_dp(own_spread(d_conv, s, SSM_HEAD)), ((0, 0), (0, 0), (0, width - conv_block))),
            jnp.pad(by_dp(d_gains), ((0, 0), (0, 0), (0, width - gains_block))),
            jnp.broadcast_to(
                jnp.pad(d_heads, ((0, 7), (0, width - d_heads.shape[1])))[None], (dp_total, 8, width)
            ),
        ],
        axis=1,
    )
    normed_keep, normed_got = scatter_begin(d_normed_part)
    normed_got, grad_qkv_part = meet(normed_got, grad_qkv_part)
    normed_held, normed_far = scatter_far(normed_keep, normed_got)
    grad_o_part, normed_held = meet(grad_o_part, normed_held)
    grad_qkv_sum, grad_o, small_sum = scatter_dp([grad_qkv_part, grad_o_part, small_part], 2)
    normed_far, (grad_qkv_sum, grad_o, small_sum) = meet(normed_far, (grad_qkv_sum, grad_o, small_sum))
    small_sum = small_sum + swap(small_sum, "seq", 1)
    small_sum = small_sum + swap(small_sum, "seq", 2)
    grad_xz_sum = grad_xz_sum.astype(LOW)
    first, last = trade_back(grad_xz_sum[:, :LOCAL_CH], grad_xz_sum[:, LOCAL_CH : 2 * LOCAL_CH])
    grad_xz = jnp.concatenate([first, last], axis=1)[:, : w_xz.shape[1]].astype(FULL)
    both_all = gather_seq(jnp.concatenate([grad_qkv_sum.astype(LOW), grad_xz_sum[:, 2 * LOCAL_CH :]], axis=1))
    bcdt_all = both_all[:, :, grad_qkv_sum.shape[1] :].astype(FULL)
    grad_bcdt = jnp.concatenate(
        [jnp.sum(bcdt_all[:, :, : 2 * STATE], axis=0)]
        + [bcdt_all[j, :, 2 * STATE : 2 * STATE + HEAD_COUNT[j]] for j in range(SEQ)],
        axis=1,
    )
    qkv_all = both_all[:, :, : grad_qkv_sum.shape[1]].astype(FULL)
    col = lambda j, at, width: qkv_all[j, :, at : at + width]
    shared = lambda at, width: jnp.sum(qkv_all[:, :, at : at + width], axis=0)
    grad_qkv_wide = jnp.concatenate(
        [col(j, 256, QW) for j in range(SEQ)]
        + [shared(256 + QW, QW)]
        + [col(j, 0, HEAD) for j in range(SEQ)]
        + [shared(128, HEAD)]
        + [col(j, HEAD, HEAD) for j in range(SEQ)]
        + [shared(128 + HEAD, HEAD)],
        axis=1,
    )
    qkv_width = w_qkv.shape[1]
    grad_qkv = lax.dynamic_slice_in_dim(grad_qkv_wide, s * qkv_width, qkv_width, 1)

    d_normed = scatter_end(normed_held, normed_far) + d_normed_own
    d_unit = d_normed * gains[0]
    scale = lax.rsqrt(jnp.mean(inputs_x * inputs_x, axis=-1, keepdims=True) + NORM_EPS)
    d_x_head = scale * (
        d_unit - inputs_x * scale * scale * jnp.mean(d_unit * inputs_x, axis=-1, keepdims=True)
    )
    input_grad = (d_x_tail + d_x_head).astype(LOW)
    grad_conv = small_sum[:CONV, :conv_block]
    grad_gains = small_sum[CONV : CONV + 4, :gains_block]
    grad_rate = small_sum[8, :SSM_HEADS]
    grad_skip = small_sum[8, SSM_HEADS : 2 * SSM_HEADS]
    return (
        mixed_out,
        input_grad,
        grad_gains,
        grad_qkv,
        grad_o,
        grad_xz,
        grad_bcdt,
        grad_conv,
        grad_rate,
        grad_skip,
        grad_out,
        grad_gate_up,
        grad_down,
    )


def solution(mesh):
    placed = (
        P(("dp", "seq"), None),
        P("dp", None),
        P(None, "dp"),
        P("dp", "seq"),
        P("dp", "seq"),
        P("dp", "seq"),
        P("dp", None),
        P(None, "dp"),
        P(),
        P(),
        P("dp", "seq"),
        P("dp", None, "seq"),
        P("dp", "seq"),
        P(("dp", "seq"), None),
    )
    return jax.shard_map(
        on_device,
        mesh=mesh,
        in_specs=placed,
        out_specs=(
            P(("dp", "seq"), None),
            P(("dp", "seq"), None),
            P(None, "dp"),
            P("dp", "seq"),
            P("dp", "seq"),
            P("dp", "seq"),
            P("dp", None),
            P(None, "dp"),
            P(),
            P(),
            P("dp", "seq"),
            P("dp", None, "seq"),
            P("dp", "seq"),
        ),
        check_vma=False,
    )
```
